128 devices in a mesh: lon: 32 (over z_hi, x, y), lat: 4 (over z_lo, core).
Axes of the slice: x: 4, y: 4, z: 4 (z_hi: 2, z_lo: 2; z = z_hi * 2 + z_lo), core: 2. Of those that a mesh axis runs over, the one named last changes fastest.
Arguments:
- tokens: bfloat16 [64, 512, 1536], P('lat', 'lon'), may hold values from -48 to 48
- qkv_weight: bfloat16 [1536, 4608], replicated, may hold values from -0.15625 to 0.15625
- rel_bias: float32 [24, 15, 15], replicated, may hold values from -4 to 4
- proj_weight: bfloat16 [1536, 1536], replicated, may hold values from -0.15625 to 0.15625
- norm_gain: float32 [1536], replicated, may hold values from 0.1 to 1.9
- norm_shift: float32 [1536], replicated, may hold values from -3 to 3
- cotangent: bfloat16 [64, 512, 1536], P('lat', 'lon'), may hold values from -40 to 40
Outputs:
- out: bfloat16 [64, 512, 1536], P('lat', 'lon')
- d_tokens: bfloat16 [64, 512, 1536], P('lat', 'lon')
- d_proj_weight: float32 [1536, 1536], P(('lon', 'lat'))
- d_rel_bias: float32 [24, 15, 15], replicated
- d_norm_gain: float32 [1536], replicated
- d_norm_shift: float32 [1536], replicated
The draws below stay inside these ranges and needn't reach their ends.
All inputs are finite; a program needn't handle non-finite values.
Results may differ from the reference program's by a relative error of at most 0.015.
The reference program's roundings to bfloat16 on the way count: a program that leaves them out, or rounds other values in their place, can miss the bound.
Values may be sent and summed in bfloat16 or wider, within the bound.
A program may use at most 128 MiB of HBM per device.

```python
import math
import jax
import jax.numpy as jnp
from jax import lax

D = 1536
HEADS = 24
WIN = 8
SPAN = 15
LAT = 64
LON = 512
PARAMS = 2367768


def draw_tokens(key, part):
    key = jax.random.fold_in(key, 17)
    first_key = jax.random.fold_in(key, 0)
    channel_ramp = jnp.exp(math.log(3.0) * (jnp.arange(D, dtype=jnp.float32) / D - 0.5))
    values = jax.random.normal(first_key, (LAT, LON, D), jnp.float32)
    return jnp.clip(values * channel_ramp, -48.0, 48.0).astype(jnp.bfloat16)


def draw_cotangent(key, part):
    key = jax.random.fold_in(key, 29)
    first_key = jax.random.fold_in(key, 0)
    lon_index = jnp.arange(LON, dtype=jnp.float32)[None, :, None]
    lon_ramp = jnp.exp(math.log(3.0) * (lon_index / LON - 0.5))
    values = jax.random.normal(first_key, (LAT, LON, D), jnp.float32)
    return jnp.clip(values * lon_ramp, -40.0, 40.0).astype(jnp.bfloat16)


def normal_values(own_key, extent, scale, limit, kind=jnp.bfloat16):
    entries = scale * jax.random.normal(own_key, extent, jnp.float32)
    return jnp.clip(entries, min=-limit, max=limit).astype(kind)


def setup_inputs(seed: int = 0) -> dict:
    key_of = jax.random.split(jax.random.key(seed), 8)
    return {
        "tokens": draw_tokens(jax.random.fold_in(key_of[7], 71), 0),
        "qkv_weight": normal_values(key_of[1], (D, 3 * D), D ** -0.5, 0.15625),
        "rel_bias": normal_values(key_of[2], (HEADS, SPAN, SPAN), 1.0, 4.0, jnp.float32),
        "proj_weight": normal_values(key_of[3], (D, D), D ** -0.5, 0.15625),
        "norm_gain": jnp.clip(1.0 + 0.18 * jax.random.normal(key_of[4], (D,), jnp.float32), 0.1, 1.9),
        "norm_shift": normal_values(key_of[5], (D,), 0.5, 3.0, jnp.float32),
        "cotangent": draw_cotangent(jax.random.fold_in(key_of[7], 71), 0),
    }


norm_epsilon = 1e-05
clip_epsilon = 1e-06

def rounded(values):
    return lax.optimization_barrier(values.astype(jnp.bfloat16)).astype(jnp.float32)

def offset_onehot(window):
    places = jnp.arange(window * window, dtype=jnp.int32)
    row_of = places // window
    column_of = places % window
    rel_rows = row_of[:, None] - row_of[None, :] + window - 1
    rel_columns = column_of[:, None] - column_of[None, :] + window - 1
    slot_ids = (rel_rows * (2 * window - 1) + rel_columns).reshape(-1)
    targets = jnp.arange((2 * window - 1) * (2 * window - 1), dtype=jnp.int32)
    return (slot_ids[:, None] == targets[None, :]).astype(jnp.float32)

def to_bands(grid_cells, window):
    lat_rows, lon_cols, channels = grid_cells.shape
    blocks = grid_cells.reshape(lat_rows // window, window, lon_cols // window, window, channels)
    return blocks.transpose(0, 2, 1, 3, 4).reshape(lat_rows // window, lon_cols // window * window * window, channels)

def from_bands(band_rows, lat_rows, lon_cols, window):
    channels = band_rows.shape[-1]
    blocks = band_rows.reshape(lat_rows // window, lon_cols // window, window, window, channels)
    return blocks.transpose(0, 2, 1, 3, 4).reshape(lat_rows, lon_cols, channels)

def reference(tokens, qkv_weight, rel_bias, proj_weight, norm_gain, norm_shift, cotangent):
    half_window = WIN // 2
    window_cells = WIN * WIN
    head_size = D // HEADS
    score_scale = float(head_size) ** (-0.5)
    per_band = LON // WIN
    count_bands = LAT // WIN
    onehot = offset_onehot(WIN)
    position_bias = jnp.dot(rel_bias.reshape(HEADS, SPAN * SPAN), onehot.T, precision=lax.Precision.HIGHEST).reshape(HEADS, window_cells, window_cells)
    rolled = jnp.roll(tokens, (-half_window, -half_window), axis=(0, 1))
    rolled_cot = jnp.roll(cotangent, (-half_window, -half_window), axis=(0, 1))
    bands = to_bands(rolled, WIN)
    cot_bands = to_bands(rolled_cot, WIN)
    upper_half = jnp.arange(window_cells, dtype=jnp.int32) // WIN < half_window
    same_region = upper_half[:, None] == upper_half[None, :]

    def split_heads(flat_rows):
        return flat_rows.reshape(per_band, window_cells, HEADS, head_size)

    def band_step(carry, inputs):
        proj_acc, bias_acc, gain_acc, shift_acc = carry
        band_x, band_cot, band_index = inputs
        allowed = same_region | (band_index != count_bands - 1)
        packed_heads = rounded(jnp.dot(band_x, qkv_weight, preferred_element_type=jnp.float32))
        query = split_heads(packed_heads[:, :D])
        key_part = split_heads(packed_heads[:, D:2 * D])
        value_part = split_heads(packed_heads[:, 2 * D:])
        scores = jnp.einsum('wihe,wjhe->whij', query, key_part) * score_scale + position_bias[None]
        scores = jnp.where(allowed[None, None], scores, -jnp.inf)
        row_peak = lax.optimization_barrier(jnp.max(scores, axis=-1, keepdims=True))
        raised = jnp.exp(scores - row_peak)
        shares = raised / lax.optimization_barrier(jnp.sum(raised, axis=-1, keepdims=True))
        shares_low = rounded(shares)
        mixed_heads = rounded(jnp.einsum('whij,wjhe->wihe', shares_low, value_part).reshape(-1, D))
        projected = jnp.dot(mixed_heads, proj_weight.astype(jnp.float32))
        centre = projected - lax.optimization_barrier(jnp.mean(projected, axis=-1, keepdims=True))
        inverse = lax.rsqrt(lax.optimization_barrier(jnp.mean(centre * centre, axis=-1, keepdims=True)) + norm_epsilon)
        normed = centre * inverse
        out_band = (band_x.astype(jnp.float32) + normed * norm_gain + norm_shift).astype(jnp.bfloat16)
        upstream = band_cot.astype(jnp.float32)
        part_gain = lax.optimization_barrier(jnp.sum(upstream * normed, axis=0))
        part_shift = lax.optimization_barrier(jnp.sum(upstream, axis=0))
        d_normed = upstream * norm_gain
        d_proj = rounded(inverse * (d_normed - lax.optimization_barrier(jnp.mean(d_normed, axis=-1, keepdims=True)) - normed * lax.optimization_barrier(jnp.mean(d_normed * normed, axis=-1, keepdims=True))))
        part_proj = jnp.dot(mixed_heads.T, d_proj)
        d_mixed = rounded(jnp.dot(d_proj, proj_weight.astype(jnp.float32).T))
        d_mixed_heads = split_heads(d_mixed)
        d_shares = jnp.einsum('wihe,wjhe->whij', d_mixed_heads, value_part)
        d_scores = shares * (d_shares - lax.optimization_barrier(jnp.sum(shares * d_shares, axis=-1, keepdims=True)))
        part_bias = lax.optimization_barrier(jnp.sum(d_scores, axis=0)).reshape(HEADS, window_cells * window_cells)
        d_scores_low = rounded(d_scores)
        d_query = jnp.einsum('whij,wjhe->wihe', d_scores_low, key_part) * score_scale
        d_key = jnp.einsum('whij,wihe->wjhe', d_scores_low, query) * score_scale
        d_value = jnp.einsum('whij,wihe->wjhe', shares_low, d_mixed_heads)
        d_qkv = rounded(jnp.concatenate([d_query.reshape(-1, D), d_key.reshape(-1, D), d_value.reshape(-1, D)], axis=1))
        d_band = (upstream + jnp.dot(d_qkv, qkv_weight.astype(jnp.float32).T)).astype(jnp.bfloat16)
        carry = (proj_acc + part_proj, bias_acc + part_bias, gain_acc + part_gain, shift_acc + part_shift)
        return (carry, (out_band, d_band))
    start_carry = (jnp.zeros((D, D), jnp.float32), jnp.zeros((HEADS, window_cells * window_cells), jnp.float32), jnp.zeros((D,), jnp.float32), jnp.zeros((D,), jnp.float32))
    carry, (out_bands, grad_bands) = lax.scan(band_step, start_carry, (bands, cot_bands, jnp.arange(count_bands, dtype=jnp.int32)))
    proj_sum, bias_full, gain_sum, shift_sum = carry
    bias_sum = jnp.dot(bias_full, onehot, precision=lax.Precision.HIGHEST)
    out = jnp.roll(from_bands(out_bands, LAT, LON, WIN), (half_window, half_window), axis=(0, 1))
    d_tokens = jnp.roll(from_bands(grad_bands, LAT, LON, WIN), (half_window, half_window), axis=(0, 1))
    squares = jnp.sum(proj_sum * proj_sum) + jnp.sum(bias_sum * bias_sum) + jnp.sum(gain_sum * gain_sum) + jnp.sum(shift_sum * shift_sum)
    factor = jnp.minimum(1.0, jnp.sqrt(PARAMS / (squares + clip_epsilon)))
    return (out, d_tokens, factor * proj_sum, (factor * bias_sum).reshape(HEADS, SPAN, SPAN), factor * gain_sum, factor * shift_sum)
```

```python
import functools

import jax
import jax.numpy as jnp
from jax import lax
from jax.experimental import pallas as pl
from jax.experimental.pallas import tpu as pltpu
from jax.sharding import PartitionSpec as P

F32 = jnp.float32
BF = jnp.bfloat16
MESH = pl.DeviceIdType.MESH

D = 1536
HEADS = 24
GROUPS = 6
LANES = 256
TOKENS = 256
CELLS = 64
WINDOWS = 4
HALF = 768
PARAMS = 2367768
norm_epsilon = 1e-05
clip_epsilon = 1e-06

ORDERS = (("x", "y", "z"), ("y", "z", "x"), ("z", "x", "y"))


def dot(a, b, ca, cb):
    return lax.dot_general(a, b, (((ca,), (cb,)), ((), ())), preferred_element_type=F32)


def dot_exact(a, b, cb):
    total = None
    for _ in range(3):
        part = a.astype(BF)
        a = a - part.astype(F32)
        term = dot(part, b, 1, cb)
        total = term if total is None else total + term
    return total


def stack(*pieces):
    return jnp.concatenate(pieces, axis=0)


def turn(value):
    return pltpu.roll(value, 4, 0)


def low_rows(columns):
    return lax.broadcasted_iota(jnp.int32, (8, columns), 0) < 4


def halves(ref, rows, cols):
    both = ref[rows, cols].astype(F32)
    return both[:8], both[8:]


def row_halves(block, row, cols):
    both = block[row, :, cols].astype(F32)
    return both[:8], both[8:]


def columns_of(step, width=LANES):
    return pl.ds(pl.multiple_of(step * width, width), width)


def input_strips(block, strips, cols, low):
    for k in range(3):
        a, b, c, d = [row_halves(block, 4 + 4 * k + i, cols)[0] for i in range(4)]
        strips[16 * k : 16 * k + 16, cols] = stack(
            jnp.where(low, a, turn(b)), jnp.where(low, c, turn(d))
        ).astype(BF)
    t = [row_halves(block, r, cols) for r in range(4)]
    wide = [turn(jnp.where(low, t1, t0)) for t0, t1 in t]
    strips[48:64, cols] = stack(wide[0], wide[1]).astype(BF)
    strips[64:80, cols] = stack(wide[2], wide[3]).astype(BF)
    strips[80:96, cols] = stack(
        jnp.where(low, turn(t[0][1]), t[1][1]), jnp.where(low, turn(t[2][1]), t[3][1])
    ).astype(BF)
    strips[96:112, cols] = stack(
        jnp.where(low, t[0][0], turn(t[1][0])), jnp.where(low, t[2][0], turn(t[3][0]))
    ).astype(BF)


def input_windows(block, came, flat, cols, low):
    for k in range(3):
        pairs = halves(came, slice(16 * k, 16 * k + 16), cols)
        for i in range(2):
            r = 4 * k + 2 * i
            s = pairs[i]
            at = (r // 8) * 128 + (r % 8) * 8
            t0, t1 = row_halves(block, r + 4, cols)
            u0, u1 = row_halves(block, r + 5, cols)
            flat[at : at + 16, cols] = stack(
                turn(jnp.where(low, t1, t0)), turn(jnp.where(low, u1, u0))
            ).astype(BF)
            flat[at + 64 : at + 80, cols] = stack(
                jnp.where(low, turn(t1), turn(s)), jnp.where(low, turn(u1), s)
            ).astype(BF)
    side = halves(came, slice(80, 96), cols)
    corner = halves(came, slice(96, 112), cols)
    for i in range(2):
        at = 128 + 32 + 16 * i
        flat[at : at + 16, cols] = came[48 + 16 * i : 64 + 16 * i, cols]
        s, d = side[i], corner[i]
        flat[at + 64 : at + 80, cols] = stack(
            jnp.where(low, s, turn(d)), jnp.where(low, turn(s), d)
        ).astype(BF)


def output_strips(flat, strips, cols, low):
    for k in range(3):
        parts = []
        for i in range(4):
            r = 4 * k + i
            at = (r // 8) * 128 + 64 + (r % 8) * 8
            parts.append(flat[at : at + 8, cols])
        a, b, c, d = parts
        strips[16 * k : 16 * k + 16, cols] = stack(
            jnp.where(low, turn(a), b), jnp.where(low, turn(c), d)
        ).astype(BF)
    strips[48:80, cols] = flat[160:192, cols].astype(BF)
    a, b, c, d = [flat[224 + 8 * i : 232 + 8 * i, cols] for i in range(4)]
    strips[80:96, cols] = stack(
        jnp.where(low, a, turn(b)), jnp.where(low, c, turn(d))
    ).astype(BF)
    strips[96:112, cols] = stack(
        jnp.where(low, turn(a), b), jnp.where(low, turn(c), d)
    ).astype(BF)


def output_block(flat, came, block, cols, low):
    for k in range(3):
        pairs = halves(came, slice(16 * k, 16 * k + 16), cols)
        for i in range(4):
            r = 4 * k + i
            s = pairs[i // 2]
            s = s if i % 2 == 0 else turn(s)
            at = (r // 8) * 128 + (r % 8) * 8
            a = turn(flat[at : at + 8, cols])
            b = turn(flat[at + 64 : at + 72, cols])
            block[r + 4, :, cols] = stack(jnp.where(low, s, a), jnp.where(low, a, b)).astype(BF)
    side = halves(came, slice(80, 96), cols)
    corner = halves(came, slice(96, 112), cols)
    for i in range(2):
        wides = halves(came, slice(48 + 16 * i, 64 + 16 * i), cols)
        s, d = side[i], corner[i]
        for k in range(2):
            wide = turn(wides[k])
            at_low = d if k == 0 else turn(d)
            at_high = turn(s) if k == 0 else s
            block[2 * i + k, :, cols] = stack(
                jnp.where(low, at_low, wide), jnp.where(low, wide, at_high)
            ).astype(BF)


def block_diagonal(value, lane_head):
    zero = jnp.zeros_like(value)
    return stack(*[jnp.where(lane_head == h, value, zero) for h in range(4)])


def diagonal(product, left):
    tiles = []
    for t in range(2):
        cols = slice(128 * t, 128 * t + 128)
        tiles.append(
            jnp.where(
                left,
                product[128 * t : 128 * t + 64, cols],
                product[128 * t + 64 : 128 * t + 128, cols],
            )
        )
    return jnp.concatenate(tiles, axis=1)


def sublayer(
    tok_h, wq_h, rel_ref, pw_h, gain_ref, shift_ref, cot_h,
    out_h, dtok_h, dpw_ref, drel_ref, dgain_ref, dshift_ref,
    tok_v, cot_v, w_v, pw_v, x_v, c_v, qkv_v, pt_v, mix_v, mixt_v, proj_v, flat_v,
    dp_v, dps_v, dmix_v, dqkv_v, oblk_v, dblk_v,
    e_v, wb_v, bt_v, mask_v, u_v, acc_v,
    send_x, came_x, send_c, came_c, send_o, came_o, send_d, came_d,
    p_v, r1a, r1c, s2a, s2b, s2c, r2a, r2b, r2c, s3a, s3b, s3c, r3, fin_v,
    sm_v, sq_v,
    load_sem, w_sem, store_sem, halo_send, halo_recv, mix_send, mix_recv, dp_sem,
    rs_send, rs_recv, sm_send, sm_recv, sq_send, sq_recv, fin_sem,
):
    lon = lax.axis_index("lon")
    lat = lax.axis_index("lat")
    core = lax.rem(lat, 2)
    at = {
        "x": lax.rem(lon // 4, 4),
        "y": lax.rem(lon, 4),
        "z": (lon // 16) * 2 + lat // 2,
    }

    def device(chip, on_core):
        z = chip["z"]
        return {
            "lon": (z // 2) * 16 + chip["x"] * 4 + chip["y"],
            "lat": lax.rem(z, 2) * 2 + on_core,
        }

    def along(axis, steps):
        chip = dict(at)
        chip[axis] = lax.rem(at[axis] + steps, 4)
        return device(chip, core)

    sibling = device(at, 1 - core)

    def shifted(lat_steps, lon_steps):
        return {
            "lon": lax.rem(lon + lon_steps + 32, 32),
            "lat": lax.rem(lat + lat_steps + 4, 4),
        }

    def remote(src, dst, send, recv, target):
        return pltpu.make_async_remote_copy(
            src_ref=src, dst_ref=dst, send_sem=send, recv_sem=recv,
            device_id=target, device_id_type=MESH,
        )

    load_tok = pltpu.make_async_copy(tok_h, tok_v, load_sem.at[0])
    load_cot = pltpu.make_async_copy(cot_h, cot_v, load_sem.at[1])
    load_pw = pltpu.make_async_copy(pw_h, pw_v, load_sem.at[2])

    def load_w(chunk):
        cols = columns_of(chunk)
        return pltpu.make_async_copy(wq_h.at[:, cols], w_v.at[:, cols], w_sem.at[chunk])

    load_tok.start()
    load_cot.start()

    partners = [shifted(0, 1), shifted(0, -1), shifted(1, 0), shifted(-1, 0), shifted(1, 1), shifted(-1, -1)]
    partners += [along(axis, steps) for axis in "xyz" for steps in (1, 2, 3)] + [sibling]
    barrier = pltpu.get_barrier_semaphore()
    for partner in partners:
        pl.semaphore_signal(barrier, inc=1, device_id=partner, device_id_type=MESH)

    for g in range(GROUPS):
        for part in range(3):
            load_w(part * GROUPS + g).start()
    load_pw.start()

    low = low_rows(LANES)

    def each_column(body):
        lax.fori_loop(0, GROUPS, lambda n, _: (body(columns_of(n)), 0)[1], 0)

    def halo(strips, came, which, sign):
        rows = (slice(0, 48), slice(48, 96), slice(96, 112))
        targets = (shifted(0, sign), shifted(sign, 0), shifted(sign, sign))
        return [
            remote(
                strips.at[rows[i]], came.at[rows[i]],
                halo_send.at[which, i], halo_recv.at[which, i], targets[i],
            )
            for i in range(3)
        ]

    load_tok.wait()
    each_column(lambda cols: input_strips(tok_v, send_x, cols, low))
    pl.semaphore_wait(barrier, len(partners))
    halo_x = halo(send_x, came_x, 0, -1)
    for copy in halo_x:
        copy.start()
    load_cot.wait()
    each_column(lambda cols: input_strips(cot_v, send_c, cols, low))
    halo_c = halo(send_c, came_c, 1, -1)
    for copy in halo_c:
        copy.start()

    spot = lax.broadcasted_iota(jnp.int32, (128, LANES), 0)
    slot = lax.broadcasted_iota(jnp.int32, (128, LANES), 1)
    for cj in range(8):
        hit = ((spot >> 3) == (slot >> 4)) & ((spot & 7) - cj + 7 == (slot & 15))
        e_v[128 * cj : 128 * cj + 128, :] = jnp.where(hit, 1.0, 0.0).astype(BF)
    rel = rel_ref[...]
    for cj in range(8):
        wb_v[:, cj, :] = dot_exact(rel, e_v[128 * cj : 128 * cj + 128, :], 1)
    left8 = lax.broadcasted_iota(jnp.int32, (8, 128), 1) < 64

    def bias_step(g, _):
        for t in range(2):
            first = wb_v[g * 4 + 2 * t]
            second = wb_v[g * 4 + 2 * t + 1]
            for rj in range(8):
                shift = (7 - rj) * 8
                bt_v[g, 8 * rj : 8 * rj + 8, 128 * t : 128 * t + 128] = jnp.where(
                    left8,
                    pltpu.roll(first, (128 - shift) % 128, 1),
                    pltpu.roll(second, (192 - shift) % 128, 1),
                )
        return 0

    lax.fori_loop(0, GROUPS, bias_step, 0)
    j_upper = lax.broadcasted_iota(jnp.int32, (CELLS, LANES), 0) < 32
    i_upper = (lax.broadcasted_iota(jnp.int32, (CELLS, LANES), 1) & 63) < 32
    crossing = (j_upper != i_upper) & (lat == 3)
    mask_v[...] = jnp.where(crossing, -jnp.inf, 0.0)

    for copy in halo_x:
        copy.wait()
    each_column(lambda cols: input_windows(tok_v, came_x, x_v, cols, low))

    def qkv_step(g, _):
        for part in range(3):
            chunk = part * GROUPS + g
            load_w(chunk).wait()
            value = dot(x_v[...], w_v[:, columns_of(chunk)], 1, 0).astype(BF)
            if part == 0:
                value = value * jnp.asarray(0.125, BF)
            qkv_v[chunk] = value
        return 0

    lax.fori_loop(0, GROUPS, qkv_step, 0)

    lane_head = lax.broadcasted_iota(jnp.int32, (CELLS, LANES), 1) >> 6
    left = lax.broadcasted_iota(jnp.int32, (CELLS, 128), 1) < 64

    def mix_copy(g):
        rows = columns_of(g)
        return remote(
            mixt_v.at[0, rows], mixt_v.at[1, rows], mix_send.at[g], mix_recv.at[g], sibling
        )

    def forward_step(g, _):
        for w in range(WINDOWS):
            rows = slice(CELLS * w, CELLS * w + CELLS)
            q, k, v = [qkv_v[part * GROUPS + g, rows, :] for part in range(3)]
            scores = dot(k, block_diagonal(q, lane_head), 1, 1) + bt_v[g]
            if w >= 2:
                scores = scores + mask_v[...]
            peak = jnp.max(scores, axis=0, keepdims=True)
            raised = jnp.exp(scores - peak)
            shares = raised * (1.0 / jnp.sum(raised, axis=0, keepdims=True))
            pt_v[g, w] = shares
            mixed = diagonal(dot(shares.astype(BF), v, 0, 0), left)
            mix_v[rows, columns_of(g)] = mixed.astype(BF)
        mixt_v[0, columns_of(g), :] = mix_v[:, columns_of(g)].T
        mix_copy(g).start()
        return 0

    lax.fori_loop(0, GROUPS, forward_step, 0)

    def project_step(n, _):
        cols = columns_of(n)
        proj_v[:, cols] = dot(mix_v[...], pw_v[:, cols], 1, 0)
        return 0

    load_pw.wait()
    lax.fori_loop(0, GROUPS, project_step, 0)

    for copy in halo_c:
        copy.wait()
    each_column(lambda cols: input_windows(cot_v, came_c, c_v, cols, low))

    acc_v[...] = jnp.zeros_like(acc_v)

    def norm_step(m, _):
        rows = pl.ds(pl.multiple_of(m * 16, 16), 16)
        projected = proj_v[rows, :]
        centre = projected - jnp.mean(projected, axis=1, keepdims=True)
        inverse = lax.rsqrt(jnp.mean(centre * centre, axis=1, keepdims=True) + norm_epsilon)
        normed = centre * inverse
        flat_v[rows, :] = x_v[rows, :].astype(F32) + normed * gain_ref[...] + shift_ref[...]
        upstream = c_v[rows, :].astype(F32)
        product = upstream * normed
        acc_v[0] += product[:8] + product[8:]
        acc_v[1] += upstream[:8] + upstream[8:]
        d_normed = upstream * gain_ref[...]
        inner = d_normed - jnp.mean(d_normed, axis=1, keepdims=True)
        inner = inner - normed * jnp.mean(d_normed * normed, axis=1, keepdims=True)
        dp_v[rows, :] = (inverse * inner).astype(BF)
        return 0

    lax.fori_loop(0, TOKENS // 16, norm_step, 0)

    other_half = pl.ds(pl.multiple_of((1 - core) * HALF, HALF), HALF)
    dp_copy = remote(dp_v.at[:, other_half], dps_v, dp_sem.at[0], dp_sem.at[1], sibling)
    dp_copy.start()

    each_column(lambda cols: output_strips(flat_v, send_o, cols, low))
    halo_o = halo(send_o, came_o, 2, 1)
    for copy in halo_o:
        copy.start()

    def d_mixed_step(n, _):
        dmix_v[n] = dot(dp_v[...], pw_v[columns_of(n), :], 1, 1).astype(BF)
        return 0

    lax.fori_loop(0, GROUPS, d_mixed_step, 0)

    dp_copy.wait()
    for g in range(GROUPS):
        mix_copy(g).wait()

    def slot_of(buffer, lead, axes, axis, index):
        if axis == "z":
            places = {"h": index // 2, "l": lax.rem(index, 2)}
        else:
            places = {axis: index}
        return buffer.at[lead + tuple(places.get(name, slice(None)) for name in axes)]

    stages = (
        ((p_v, (0,), "hxyl"), (p_v, (1,), "hxyl"), (p_v, (2,), "hxyl")),
        ((s2a, (), "hyl"), (s2b, (), "hxl"), (s2c, (), "xy")),
        ((s3a, (), "hl"), (s3b, (), "x"), (s3c, (), "y")),
    )
    arrivals = (
        (r1a.at[0], r1a.at[1], r1c),
        (r2a, r2b, r2c),
        (r3.at[0], r3.at[1], r3.at[2]),
    )

    def scatter_copies(stage, part):
        buffer, lead, axes = stages[stage][part]
        axis = ORDERS[part][stage]
        copies = []
        for steps in (1, 2, 3):
            index = lax.rem(at[axis] + steps, 4)
            copies.append(
                remote(
                    slot_of(buffer, lead, axes, axis, index),
                    arrivals[stage][part].at[steps - 1],
                    rs_send.at[stage, part, steps - 1],
                    rs_recv.at[stage, part, steps - 1],
                    along(axis, steps),
                )
            )
        return copies

    def scatter_start(stage, part):
        for copy in scatter_copies(stage, part):
            copy.start()

    def scatter_sum(stage, part):
        for copy in scatter_copies(stage, part):
            copy.wait()
        buffer, lead, axes = stages[stage][part]
        axis = ORDERS[part][stage]
        total = slot_of(buffer, lead, axes, axis, at[axis])[...].astype(F32)
        for steps in range(3):
            total = total + arrivals[stage][part][steps].astype(F32)
        if stage < 2:
            target = stages[stage + 1][part][0]
            target[...] = total.astype(target.dtype)
            scatter_start(stage + 1, part)
        else:
            fin_v[0, :, LANES * part : LANES * part + 128] = total[:24]
            fin_v[0, :, LANES * part + 128 : LANES * part + 256] = total[24:]

    for part in range(3):
        own = dp_v[:, pl.ds(pl.multiple_of(core * HALF + part * LANES, LANES), LANES)]
        other = dps_v[:, LANES * part : LANES * part + LANES]
        for mb in range(4):
            rows = slice(384 * mb, 384 * mb + 384)
            value = dot(mixt_v[0, rows, :], own, 1, 0) + dot(mixt_v[1, rows, :], other, 1, 0)
            value = jnp.concatenate(
                [value[:, :128].reshape(16, 24, 128), value[:, 128:].reshape(16, 24, 128)], axis=1
            )
            p_v[part, mb // 2, 2 * (mb % 2) : 2 * (mb % 2) + 2] = value.astype(BF).reshape(
                2, 4, 2, 48, 128
            )
        scatter_start(0, part)

    def backward_step(g, _):
        total = None
        for w in range(WINDOWS):
            rows = slice(CELLS * w, CELLS * w + CELLS)
            q, k, v = [qkv_v[part * GROUPS + g, rows, :] for part in range(3)]
            d_out = block_diagonal(dmix_v[g, rows, :], lane_head)
            shares = pt_v[g, w]
            d_shares = dot(v, d_out, 1, 1)
            d_scores = shares * (d_shares - jnp.sum(shares * d_shares, axis=0, keepdims=True))
            total = d_scores if total is None else total + d_scores
            low_scores = d_scores.astype(BF)
            dq = diagonal(dot(low_scores, k, 0, 0), left) * 0.125
            dk = dot(low_scores, block_diagonal(q, lane_head), 1, 0)
            dv = dot(shares.astype(BF), d_out, 1, 0)
            for part, value in enumerate((dq, dk, dv)):
                dqkv_v[rows, columns_of(part * GROUPS + g)] = value.astype(BF)
        for t in range(2):
            sums = [None, None]
            for rj in range(8):
                shift = (7 - rj) * 8
                piece = total[8 * rj : 8 * rj + 8, 128 * t : 128 * t + 128]
                pair = (
                    pltpu.roll(jnp.where(left8, piece, 0.0), shift, 1),
                    pltpu.roll(jnp.where(left8, 0.0, piece), shift + 64, 1),
                )
                sums = [b if a is None else a + b for a, b in zip(sums, pair)]
            u_v[g * 4 + 2 * t] = sums[0]
            u_v[g * 4 + 2 * t + 1] = sums[1]
        return 0

    lax.fori_loop(0, GROUPS, backward_step, 0)

    small = None
    for cj in range(8):
        term = dot_exact(u_v[:, cj, :], e_v[128 * cj : 128 * cj + 128, :], 0)
        small = term if small is None else small + term
    gain_sum = jnp.sum(acc_v[0], axis=0, keepdims=True)
    shift_sum = jnp.sum(acc_v[1], axis=0, keepdims=True)
    zero2 = jnp.zeros((2, LANES), F32)
    small = stack(
        small,
        *[gain_sum[:, LANES * n : LANES * n + LANES] for n in range(GROUPS)], zero2,
        *[shift_sum[:, LANES * n : LANES * n + LANES] for n in range(GROUPS)], zero2,
    )

    def sum_copies(buffer, send, recv, stage):
        if stage == 0:
            return [remote(
                buffer.at[0, core], buffer.at[0, core], send.at[0, 0], recv.at[0, 0], sibling
            )]
        axis = "xyz"[stage - 1]
        return [
            remote(
                buffer.at[stage, at[axis]], buffer.at[stage, at[axis]],
                send.at[stage, steps - 1], recv.at[stage, steps - 1], along(axis, steps),
            )
            for steps in (1, 2, 3)
        ]

    def sum_start(buffer, send, recv, stage, value):
        place = core if stage == 0 else at["xyz"[stage - 1]]
        buffer[stage, place] = value
        for copy in sum_copies(buffer, send, recv, stage):
            copy.start()

    def sum_finish(buffer, send, recv, stage):
        for copy in sum_copies(buffer, send, recv, stage):
            copy.wait()
        total = buffer[stage, 0] + buffer[stage, 1]
        if stage > 0:
            total = total + buffer[stage, 2] + buffer[stage, 3]
        return total

    sum_start(sm_v, sm_send, sm_recv, 0, small)

    def d_token_step(n, _):
        cols = columns_of(n)
        flat_v[:, cols] = c_v[:, cols].astype(F32) + dot(dqkv_v[...], w_v[cols, :], 1, 1)
        output_strips(flat_v, send_d, cols, low)
        return 0

    for copy in halo_o:
        copy.wait()
    each_column(lambda cols: output_block(flat_v, came_o, oblk_v, cols, low))
    store_out = pltpu.make_async_copy(oblk_v, out_h, store_sem.at[0])
    store_out.start()

    for part in range(3):
        scatter_sum(0, part)
    lax.fori_loop(0, 2, d_token_step, 0)
    sum_start(sm_v, sm_send, sm_recv, 1, sum_finish(sm_v, sm_send, sm_recv, 0))
    for part in range(3):
        scatter_sum(1, part)
    lax.fori_loop(2, 4, d_token_step, 0)
    sum_start(sm_v, sm_send, sm_recv, 2, sum_finish(sm_v, sm_send, sm_recv, 1))
    for part in range(3):
        scatter_sum(2, part)
    fin_copy = remote(fin_v.at[0], fin_v.at[1], fin_sem.at[0], fin_sem.at[1], sibling)
    fin_copy.start()
    squares = fin_v[0] * fin_v[0]
    squares = squares[:8] + squares[8:16] + squares[16:]
    squares = sum(squares[:, 128 * n : 128 * n + 128] for n in range(6))
    sum_start(sq_v, sq_send, sq_recv, 0, squares)
    lax.fori_loop(4, 6, d_token_step, 0)
    halo_d = halo(send_d, came_d, 3, 1)
    for copy in halo_d:
        copy.start()
    sum_start(sm_v, sm_send, sm_recv, 3, sum_finish(sm_v, sm_send, sm_recv, 2))
    for stage in (1, 2, 3):
        sum_start(sq_v, sq_send, sq_recv, stage, sum_finish(sq_v, sq_send, sq_recv, stage - 1))

    for copy in halo_d:
        copy.wait()
    each_column(lambda cols: output_block(flat_v, came_d, dblk_v, cols, low))
    store_dtok = pltpu.make_async_copy(dblk_v, dtok_h, store_sem.at[1])
    store_dtok.start()

    small = sum_finish(sm_v, sm_send, sm_recv, 3)
    squares = sum_finish(sq_v, sq_send, sq_recv, 3)
    total = jnp.sum(squares, axis=(0, 1), keepdims=True)
    total = total + jnp.sum(small * small, axis=(0, 1), keepdims=True)
    factor = jnp.minimum(1.0, jnp.sqrt(PARAMS / (total + clip_epsilon)))
    drel_ref[...] = small[:24] * factor
    for n in range(GROUPS):
        dgain_ref[:, LANES * n : LANES * n + LANES] = small[24 + n : 25 + n] * factor
        dshift_ref[:, LANES * n : LANES * n + LANES] = small[32 + n : 33 + n] * factor
    fin_copy.wait()
    own, other = fin_v[0] * factor, fin_v[1] * factor
    own = jnp.where(core == 0, own[:12], own[12:])
    other = jnp.where(core == 0, other[:12], other[12:])
    dpw_ref[:, :HALF] = jnp.where(core == 0, own, other)
    dpw_ref[:, HALF:] = jnp.where(core == 0, other, own)
    store_out.wait()
    store_dtok.wait()


def on_device(tokens, qkv_weight, rel_bias, proj_weight, norm_gain, norm_shift, cotangent):
    rel = jnp.pad(rel_bias, ((0, 0), (0, 1), (0, 1))).reshape(HEADS, 256)
    anywhere = pl.BlockSpec(memory_space=pl.ANY)
    vmem = pl.BlockSpec(memory_space=pltpu.VMEM)
    dma = pltpu.SemaphoreType.DMA
    strips = [pltpu.VMEM((112, D), BF)] * 8
    scratch = [
        pltpu.VMEM((16, 16, D), BF),
        pltpu.VMEM((16, 16, D), BF),
        pltpu.VMEM((D, 3 * D), BF),
        pltpu.VMEM((D, D), BF),
        pltpu.VMEM((TOKENS, D), BF),
        pltpu.VMEM((TOKENS, D), BF),
        pltpu.VMEM((18, TOKENS, LANES), BF),
        pltpu.VMEM((GROUPS, WINDOWS, CELLS, LANES), F32),
        pltpu.VMEM((TOKENS, D), BF),
        pltpu.VMEM((2, D, TOKENS), BF),
        pltpu.VMEM((TOKENS, D), F32),
        pltpu.VMEM((TOKENS, D), F32),
        pltpu.VMEM((TOKENS, D), BF),
        pltpu.VMEM((TOKENS, HALF), BF),
        pltpu.VMEM((GROUPS, TOKENS, LANES), BF),
        pltpu.VMEM((TOKENS, 3 * D), BF),
        pltpu.VMEM((16, 16, D), BF),
        pltpu.VMEM((16, 16, D), BF),
        pltpu.VMEM((1024, LANES), BF),
        pltpu.VMEM((HEADS, 8, 128), F32),
        pltpu.VMEM((GROUPS, CELLS, LANES), F32),
        pltpu.VMEM((CELLS, LANES), F32),
        pltpu.VMEM((HEADS, 8, 128), F32),
        pltpu.VMEM((2, 8, D), F32),
        *strips,
        pltpu.VMEM((3, 2, 4, 4, 2, 48, 128), BF),
        pltpu.VMEM((2, 3, 2, 4, 2, 48, 128), BF),
        pltpu.VMEM((3, 4, 4, 48, 128), BF),
        pltpu.VMEM((2, 4, 2, 48, 128), BF),
        pltpu.VMEM((2, 4, 2, 48, 128), BF),
        pltpu.VMEM((4, 4, 48, 128), BF),
        pltpu.VMEM((3, 2, 2, 48, 128), BF),
        pltpu.VMEM((3, 4, 48, 128), BF),
        pltpu.VMEM((3, 4, 48, 128), BF),
        pltpu.VMEM((2, 2, 48, 128), F32),
        pltpu.VMEM((4, 48, 128), F32),
        pltpu.VMEM((4, 48, 128), F32),
        pltpu.VMEM((3, 3, 48, 128), F32),
        pltpu.VMEM((2, 24, HALF), F32),
        pltpu.VMEM((4, 4, 40, LANES), F32),
        pltpu.VMEM((4, 4, 8, 128), F32),
        dma((3,)),
        dma((18,)),
        dma((2,)),
        dma((4, 3)),
        dma((4, 3)),
        dma((GROUPS,)),
        dma((GROUPS,)),
        dma((2,)),
        dma((3, 3, 3)),
        dma((3, 3, 3)),
        dma((4, 3)),
        dma((4, 3)),
        dma((4, 3)),
        dma((4, 3)),
        dma((2,)),
    ]
    out, d_tokens, d_proj, d_rel, d_gain, d_shift = pl.pallas_call(
        sublayer,
        out_shape=(
            jax.ShapeDtypeStruct((16, 16, D), BF),
            jax.ShapeDtypeStruct((16, 16, D), BF),
            jax.ShapeDtypeStruct((12, D), F32),
            jax.ShapeDtypeStruct((HEADS, LANES), F32),
            jax.ShapeDtypeStruct((1, D), F32),
            jax.ShapeDtypeStruct((1, D), F32),
        ),
        in_specs=[anywhere, anywhere, vmem, anywhere, vmem, vmem, anywhere],
        out_specs=(anywhere, anywhere, vmem, vmem, vmem, vmem),
        scratch_shapes=scratch,
        compiler_params=pltpu.CompilerParams(
            collective_id=0, has_side_effects=True, vmem_limit_bytes=60 * 2**20
        ),
        name="sublayer",
    )(
        tokens, qkv_weight, rel, proj_weight,
        norm_gain.reshape(1, D), norm_shift.reshape(1, D), cotangent,
    )
    d_rel = d_rel.reshape(HEADS, 16, 16)[:, :15, :15]
    return out, d_tokens, d_proj, d_rel, d_gain.reshape(D), d_shift.reshape(D)


def solution(mesh):
    in_specs = (P("lat", "lon", None), P(), P(), P(), P(), P(), P("lat", "lon", None))
    out_specs = (
        P("lat", "lon", None),
        P("lat", "lon", None),
        P(("lon", "lat"), None),
        P(),
        P(),
        P(),
    )
    return jax.shard_map(
        on_device, mesh=mesh, in_specs=in_specs, out_specs=out_specs, check_vma=False
    )
```

```python
import functools

import jax
import jax.numpy as jnp
from jax import lax
from jax.experimental import pallas as pl
from jax.experimental.pallas import tpu as pltpu
from jax.sharding import PartitionSpec as P

F32 = jnp.float32
BF = jnp.bfloat16
MESH = pl.DeviceIdType.MESH

D = 1536
HEADS = 24
GROUPS = 6
LANES = 256
TOKENS = 256
CELLS = 64
WINDOWS = 4
HALF = 768
PARAMS = 2367768
norm_epsilon = 1e-05
clip_epsilon = 1e-06

ORDERS = (("x", "y", "z"), ("y", "z", "x"), ("z", "x", "y"))


def dot(a, b, ca, cb):
    return lax.dot_general(a, b, (((ca,), (cb,)), ((), ())), preferred_element_type=F32)


def dot_exact(a, b, ca, cb):
    total = None
    for _ in range(3):
        part = a.astype(BF)
        a = a - part.astype(F32)
        term = dot(part, b, ca, cb)
        total = term if total is None else total + term
    return total


def stack(*pieces):
    return jnp.concatenate(pieces, axis=0)


def turn(value):
    return pltpu.roll(value, 4, 0)


def low_rows(columns):
    return lax.broadcasted_iota(jnp.int32, (8, columns), 0) < 4


def halves(ref, rows, cols):
    both = ref[rows, cols].astype(F32)
    return both[:8], both[8:]


def row_halves(block, row, cols):
    both = block[row, :, cols].astype(F32)
    return both[:8], both[8:]


def columns_of(step, width=LANES):
    return pl.ds(pl.multiple_of(step * width, width), width)


def input_strips(block, strips, cols, low):
    for k in range(3):
        a, b, c, d = [row_halves(block, 4 + 4 * k + i, cols)[0] for i in range(4)]
        strips[16 * k : 16 * k + 16, cols] = stack(
            jnp.where(low, a, turn(b)), jnp.where(low, c, turn(d))
        ).astype(BF)
    t = [row_halves(block, r, cols) for r in range(4)]
    wide = [turn(jnp.where(low, t1, t0)) for t0, t1 in t]
    strips[48:64, cols] = stack(wide[0], wide[1]).astype(BF)
    strips[64:80, cols] = stack(wide[2], wide[3]).astype(BF)
    strips[80:96, cols] = stack(
        jnp.where(low, turn(t[0][1]), t[1][1]), jnp.where(low, turn(t[2][1]), t[3][1])
    ).astype(BF)
    strips[96:112, cols] = stack(
        jnp.where(low, t[0][0], turn(t[1][0])), jnp.where(low, t[2][0], turn(t[3][0]))
    ).astype(BF)


def input_windows(block, came, flat, cols, low):
    for k in range(3):
        pairs = halves(came, slice(16 * k, 16 * k + 16), cols)
        for i in range(2):
            r = 4 * k + 2 * i
            s = pairs[i]
            at = (r // 8) * 128 + (r % 8) * 8
            t0, t1 = row_halves(block, r + 4, cols)
            u0, u1 = row_halves(block, r + 5, cols)
            flat[at : at + 16, cols] = stack(
                turn(jnp.where(low, t1, t0)), turn(jnp.where(low, u1, u0))
            ).astype(BF)
            flat[at + 64 : at + 80, cols] = stack(
                jnp.where(low, turn(t1), turn(s)), jnp.where(low, turn(u1), s)
            ).astype(BF)
    side = halves(came, slice(80, 96), cols)
    corner = halves(came, slice(96, 112), cols)
    for i in range(2):
        at = 128 + 32 + 16 * i
        flat[at : at + 16, cols] = came[48 + 16 * i : 64 + 16 * i, cols]
        s, d = side[i], corner[i]
        flat[at + 64 : at + 80, cols] = stack(
            jnp.where(low, s, turn(d)), jnp.where(low, turn(s), d)
        ).astype(BF)


def output_strips(flat, strips, cols, low):
    for k in range(3):
        parts = []
        for i in range(4):
            r = 4 * k + i
            at = (r // 8) * 128 + 64 + (r % 8) * 8
            parts.append(flat[at : at + 8, cols])
        a, b, c, d = parts
        strips[16 * k : 16 * k + 16, cols] = stack(
            jnp.where(low, turn(a), b), jnp.where(low, turn(c), d)
        ).astype(BF)
    strips[48:80, cols] = flat[160:192, cols].astype(BF)
    a, b, c, d = [flat[224 + 8 * i : 232 + 8 * i, cols] for i in range(4)]
    strips[80:96, cols] = stack(
        jnp.where(low, a, turn(b)), jnp.where(low, c, turn(d))
    ).astype(BF)
    strips[96:112, cols] = stack(
        jnp.where(low, turn(a), b), jnp.where(low, turn(c), d)
    ).astype(BF)


def output_block(flat, came, block, cols, low):
    for k in range(3):
        pairs = halves(came, slice(16 * k, 16 * k + 16), cols)
        for i in range(4):
            r = 4 * k + i
            s = pairs[i // 2]
            s = s if i % 2 == 0 else turn(s)
            at = (r // 8) * 128 + (r % 8) * 8
            a = turn(flat[at : at + 8, cols])
            b = turn(flat[at + 64 : at + 72, cols])
            block[r + 4, :, cols] = stack(jnp.where(low, s, a), jnp.where(low, a, b)).astype(BF)
    side = halves(came, slice(80, 96), cols)
    corner = halves(came, slice(96, 112), cols)
    for i in range(2):
        wides = halves(came, slice(48 + 16 * i, 64 + 16 * i), cols)
        s, d = side[i], corner[i]
        for k in range(2):
            wide = turn(wides[k])
            at_low = d if k == 0 else turn(d)
            at_high = turn(s) if k == 0 else s
            block[2 * i + k, :, cols] = stack(
                jnp.where(low, at_low, wide), jnp.where(low, wide, at_high)
            ).astype(BF)


def block_diagonal(value, lane_head):
    zero = jnp.zeros_like(value)
    return stack(*[jnp.where(lane_head == h, value, zero) for h in range(4)])


def diagonal(product, left):
    tiles = []
    for t in range(2):
        cols = slice(128 * t, 128 * t + 128)
        tiles.append(
            jnp.where(
                left,
                product[128 * t : 128 * t + 64, cols],
                product[128 * t + 64 : 128 * t + 128, cols],
            )
        )
    return jnp.concatenate(tiles, axis=1)


def sublayer(
    tok_h, wq_h, rel_ref, pw_h, gain_ref, shift_ref, cot_h,
    out_h, dtok_h, dpw_ref, drel_ref, dgain_ref, dshift_ref,
    tok_v, cot_v, w_v, pw_v, x_v, c_v, qkv_v, pt_v, mix_v, mixt_v, proj_v, flat_v,
    dp_v, dps_v, dmix_v, dqkv_v, oblk_v, dblk_v,
    e_v, rel_v, gain_v, shift_v, wb_v, bt_v, mask_v, u_v, acc_v,
    send_x, came_x, send_c, came_c, send_o, came_o, send_d, came_d,
    p_v, r1a, r1c, s2a, s2b, s2c, r2a, r2b, r2c, s3a, s3b, s3c, r3, fin_v,
    sm_v, sq1_v, sq2_v,
    load_sem, w_sem, store_sem, halo_send, halo_recv, mix_send, mix_recv, dp_send, dp_recv,
    rs_send, rs_recv, sm_send, sm_recv, sq_send, sq_recv, last_send, last_recv, last_store, fin_sem,
):
    lon = lax.axis_index("lon")
    lat = lax.axis_index("lat")
    core = lax.rem(lat, 2)
    at = {
        "x": lax.rem(lon // 4, 4),
        "y": lax.rem(lon, 4),
        "z": (lon // 16) * 2 + lat // 2,
    }

    def device(chip, on_core):
        z = chip["z"]
        return {
            "lon": (z // 2) * 16 + chip["x"] * 4 + chip["y"],
            "lat": lax.rem(z, 2) * 2 + on_core,
        }

    def along(axis, steps):
        chip = dict(at)
        chip[axis] = lax.rem(at[axis] + steps, 4)
        return device(chip, core)

    sibling = device(at, 1 - core)

    def shifted(lat_steps, lon_steps):
        return {
            "lon": lax.rem(lon + lon_steps + 32, 32),
            "lat": lax.rem(lat + lat_steps + 4, 4),
        }

    def remote(src, dst, send, recv, target):
        return pltpu.make_async_remote_copy(
            src_ref=src, dst_ref=dst, send_sem=send, recv_sem=recv,
            device_id=target, device_id_type=MESH,
        )

    load_tok = pltpu.make_async_copy(tok_h, tok_v, load_sem.at[0])
    load_cot = pltpu.make_async_copy(cot_h, cot_v, load_sem.at[1])
    load_pw = pltpu.make_async_copy(pw_h, pw_v, load_sem.at[2])

    def load_w(chunk):
        cols = columns_of(chunk)
        return pltpu.make_async_copy(wq_h.at[:, cols], w_v.at[:, cols], w_sem.at[chunk])

    load_tok.start()
    load_cot.start()

    partners = [shifted(0, 1), shifted(0, -1), shifted(1, 0), shifted(-1, 0), shifted(1, 1), shifted(-1, -1)]
    for k in range(1, 16):
        chip = dict(at)
        chip["x"] = lax.rem(at["x"] + k // 4, 4)
        chip["y"] = lax.rem(at["y"] + k % 4, 4)
        partners.append(device(chip, core))
    for k in range(1, 8):
        chip = dict(at)
        chip["z"] = lax.rem(at["z"] + k // 2, 4)
        partners.append(device(chip, core if k % 2 == 0 else 1 - core))
    barrier = pltpu.get_barrier_semaphore()
    for partner in partners:
        pl.semaphore_signal(barrier, inc=1, device_id=partner, device_id_type=MESH)

    for g in range(GROUPS):
        for part in range(3):
            load_w(part * GROUPS + g).start()
    load_pw.start()

    low = low_rows(LANES)

    def each_column(body):
        lax.fori_loop(0, GROUPS, lambda n, _: (body(columns_of(n)), 0)[1], 0)

    def halo(strips, came, which, sign):
        rows = (slice(0, 48), slice(48, 96), slice(96, 112))
        targets = (shifted(0, sign), shifted(sign, 0), shifted(sign, sign))
        return [
            remote(
                strips.at[rows[i]], came.at[rows[i]],
                halo_send.at[which, i], halo_recv.at[which, i], targets[i],
            )
            for i in range(3)
        ]

    load_tok.wait()
    each_column(lambda cols: input_strips(tok_v, send_x, cols, low))
    pl.semaphore_wait(barrier, len(partners))
    halo_x = halo(send_x, came_x, 0, -1)
    for copy in halo_x:
        copy.start()
    load_cot.wait()
    each_column(lambda cols: input_strips(cot_v, send_c, cols, low))
    halo_c = halo(send_c, came_c, 1, -1)
    for copy in halo_c:
        copy.start()

    spot = lax.broadcasted_iota(jnp.int32, (128, LANES), 0)
    slot = lax.broadcasted_iota(jnp.int32, (128, LANES), 1)
    for cj in range(8):
        hit = ((spot >> 3) == (slot >> 4)) & ((spot & 7) - cj + 7 == (slot & 15))
        e_v[128 * cj : 128 * cj + 128, :] = jnp.where(hit, 1.0, 0.0).astype(BF)
    rel_v[...] = jnp.zeros_like(rel_v)
    for a in range(15):
        rel_v[16 * a : 16 * a + 15, :] = rel_ref[a]
    rel = rel_v[...]
    for cj in range(8):
        wb_v[:, cj, :] = dot_exact(rel, e_v[128 * cj : 128 * cj + 128, :], 0, 1)
    left8 = lax.broadcasted_iota(jnp.int32, (8, 128), 1) < 64

    def bias_step(g, _):
        for t in range(2):
            first = wb_v[g * 4 + 2 * t]
            second = wb_v[g * 4 + 2 * t + 1]
            for rj in range(8):
                shift = (7 - rj) * 8
                bt_v[g, 8 * rj : 8 * rj + 8, 128 * t : 128 * t + 128] = jnp.where(
                    left8,
                    pltpu.roll(first, (128 - shift) % 128, 1),
                    pltpu.roll(second, (192 - shift) % 128, 1),
                )
        return 0

    lax.fori_loop(0, GROUPS, bias_step, 0)
    j_upper = lax.broadcasted_iota(jnp.int32, (CELLS, LANES), 0) < 32
    i_upper = (lax.broadcasted_iota(jnp.int32, (CELLS, LANES), 1) & 63) < 32
    crossing = (j_upper != i_upper) & (lat == 3)
    mask_v[...] = jnp.where(crossing, -jnp.inf, 0.0)

    for copy in halo_x:
        copy.wait()
    each_column(lambda cols: input_windows(tok_v, came_x, x_v, cols, low))

    lane_head = lax.broadcasted_iota(jnp.int32, (CELLS, LANES), 1) >> 6
    left = lax.broadcasted_iota(jnp.int32, (CELLS, 128), 1) < 64

    def mix_copy(g):
        rows = columns_of(g)
        return remote(
            mixt_v.at[0, rows], mixt_v.at[1, rows], mix_send.at[g], mix_recv.at[g], sibling
        )

    def make_qkv(g):
        for part in range(3):
            chunk = part * GROUPS + g
            value = dot(x_v[...], w_v[:, columns_of(chunk)], 1, 0).astype(BF)
            if part == 0:
                value = value * jnp.asarray(0.125, BF)
            qkv_v[chunk] = value

    def wait_weights(g):
        for part in range(3):
            load_w(part * GROUPS + g).wait()

    def attend(g):
        bias = bt_v[g]
        masked = bias + mask_v[...]
        mixed = []
        for w in range(WINDOWS):
            rows = slice(CELLS * w, CELLS * w + CELLS)
            q, k, v = [qkv_v[part * GROUPS + g, rows, :] for part in range(3)]
            scores = dot(k, block_diagonal(q, lane_head), 1, 1) + (bias if w < 2 else masked)
            peak = jnp.max(scores, axis=0, keepdims=True)
            raised = jnp.exp(scores - peak)
            shares = raised * (1.0 / jnp.sum(raised, axis=0, keepdims=True))
            pt_v[g, w] = shares
            mixed.append(diagonal(dot(shares.astype(BF), v, 0, 0), left).astype(BF))
        mixed = stack(*mixed)
        mix_v[:, columns_of(g)] = mixed
        mixt_v[0, columns_of(g), :] = mixed.T

    def forward_step(g, _):
        wait_weights(g + 1)
        attend(g)
        make_qkv(g + 1)
        mix_copy(g).start()
        return 0

    wait_weights(0)
    make_qkv(0)
    lax.fori_loop(0, GROUPS - 1, forward_step, 0)
    attend(GROUPS - 1)
    mix_copy(GROUPS - 1).start()

    def project_step(n, _):
        cols = columns_of(n)
        proj_v[:, cols] = dot(mix_v[...], pw_v[:, cols], 1, 0)
        return 0

    load_pw.wait()
    lax.fori_loop(0, GROUPS, project_step, 0)

    for copy in halo_c:
        copy.wait()
    each_column(lambda cols: input_windows(cot_v, came_c, c_v, cols, low))

    acc_v[...] = jnp.zeros_like(acc_v)
    gain = gain_ref[...].reshape(1, D)
    shift = shift_ref[...].reshape(1, D)
    gain_v[...] = gain
    shift_v[...] = shift

    other_half = pl.ds(pl.multiple_of((1 - core) * HALF, HALF), HALF)

    def dp_copy(m):
        rows = pl.ds(pl.multiple_of(m * CELLS, CELLS), CELLS)
        return remote(dp_v.at[rows, other_half], dps_v.at[rows], dp_send.at[m], dp_recv.at[m], sibling)

    def norm_step(m, _):
        sums = [None, None]
        for part in range(4):
            rows = pl.ds(pl.multiple_of(m * CELLS + 16 * part, 16), 16)
            projected = proj_v[rows, :]
            centre = projected - jnp.mean(projected, axis=1, keepdims=True)
            inverse = lax.rsqrt(jnp.mean(centre * centre, axis=1, keepdims=True) + norm_epsilon)
            normed = centre * inverse
            flat_v[rows, :] = x_v[rows, :].astype(F32) + normed * gain_v[...] + shift_v[...]
            upstream = c_v[rows, :].astype(F32)
            product = upstream * normed
            terms = (product[:8] + product[8:], upstream[:8] + upstream[8:])
            sums = [b if a is None else a + b for a, b in zip(sums, terms)]
            d_normed = upstream * gain_v[...]
            inner = d_normed - jnp.mean(d_normed, axis=1, keepdims=True)
            inner = inner - normed * jnp.mean(d_normed * normed, axis=1, keepdims=True)
            dp_v[rows, :] = (inverse * inner).astype(BF)
        acc_v[0] += sums[0]
        acc_v[1] += sums[1]
        dp_copy(m).start()
        return 0

    lax.fori_loop(0, TOKENS // CELLS, norm_step, 0)

    for m in range(WINDOWS):
        dp_copy(m).wait()
    for g in range(GROUPS):
        mix_copy(g).wait()

    def slot_of(buffer, lead, axes, axis, index):
        if axis == "z":
            places = {"h": index // 2, "l": lax.rem(index, 2)}
        else:
            places = {axis: index}
        return buffer.at[lead + tuple(places.get(name, slice(None)) for name in axes)]

    stages = (
        ((p_v, (0,), "hxyl"), (p_v, (1,), "hxyl"), (p_v, (2,), "hxyl")),
        ((s2a, (), "hyl"), (s2b, (), "hxl"), (s2c, (), "xy")),
        ((s3a, (), "hl"), (s3b, (), "x"), (s3c, (), "y")),
    )
    arrivals = (
        (r1a.at[0], r1a.at[1], r1c),
        (r2a, r2b, r2c),
        (r3.at[0], r3.at[1], r3.at[2]),
    )

    def scatter_copies(stage, part):
        buffer, lead, axes = stages[stage][part]
        axis = ORDERS[part][stage]
        copies = []
        for steps in (1, 2, 3):
            index = lax.rem(at[axis] + steps, 4)
            copies.append(
                remote(
                    slot_of(buffer, lead, axes, axis, index),
                    arrivals[stage][part].at[steps - 1],
                    rs_send.at[stage, part, steps - 1],
                    rs_recv.at[stage, part, steps - 1],
                    along(axis, steps),
                )
            )
        return copies

    def scatter_start(stage, part):
        for copy in scatter_copies(stage, part):
            copy.start()

    def scatter_sum(stage, part):
        for copy in scatter_copies(stage, part):
            copy.wait()
        buffer, lead, axes = stages[stage][part]
        axis = ORDERS[part][stage]
        total = slot_of(buffer, lead, axes, axis, at[axis])[...].astype(F32)
        for steps in range(3):
            total = total + arrivals[stage][part][steps].astype(F32)
        if stage < 2:
            target = stages[stage + 1][part][0]
            target[...] = total.astype(target.dtype)
            scatter_start(stage + 1, part)
        else:
            fin_v[0, :, LANES * part : LANES * part + 128] = total[:24]
            fin_v[0, :, LANES * part + 128 : LANES * part + 256] = total[24:]

    for part in range(3):
        own = dp_v[:, pl.ds(pl.multiple_of(core * HALF + part * LANES, LANES), LANES)]
        other = dps_v[:, LANES * part : LANES * part + LANES]
        for mb in range(4):
            rows = slice(384 * mb, 384 * mb + 384)
            value = dot(mixt_v[0, rows, :], own, 1, 0) + dot(mixt_v[1, rows, :], other, 1, 0)
            value = jnp.concatenate(
                [value[:, :128].reshape(16, 24, 128), value[:, 128:].reshape(16, 24, 128)], axis=1
            )
            p_v[part, mb // 2, 2 * (mb % 2) : 2 * (mb % 2) + 2] = value.astype(BF).reshape(
                2, 4, 2, 48, 128
            )
        scatter_start(0, part)

    each_column(lambda cols: output_strips(flat_v, send_o, cols, low))
    halo_o = halo(send_o, came_o, 2, 1)
    for copy in halo_o:
        copy.start()

    def d_mixed_step(n, _):
        dmix_v[n] = dot(dp_v[...], pw_v[columns_of(n), :], 1, 1).astype(BF)
        return 0

    lax.fori_loop(0, GROUPS, d_mixed_step, 0)

    def backward_step(g, _):
        total = None
        for w in range(WINDOWS):
            rows = slice(CELLS * w, CELLS * w + CELLS)
            q, k, v = [qkv_v[part * GROUPS + g, rows, :] for part in range(3)]
            d_out = block_diagonal(dmix_v[g, rows, :], lane_head)
            shares = pt_v[g, w]
            d_shares = dot(v, d_out, 1, 1)
            d_scores = shares * (d_shares - jnp.sum(shares * d_shares, axis=0, keepdims=True))
            total = d_scores if total is None else total + d_scores
            low_scores = d_scores.astype(BF)
            dq = diagonal(dot(low_scores, k, 0, 0), left) * 0.125
            dk = dot(low_scores, block_diagonal(q, lane_head), 1, 0)
            dv = dot(shares.astype(BF), d_out, 1, 0)
            for part, value in enumerate((dq, dk, dv)):
                dqkv_v[rows, columns_of(part * GROUPS + g)] = value.astype(BF)
        for t in range(2):
            sums = [None, None]
            for rj in range(8):
                shift = (7 - rj) * 8
                piece = total[8 * rj : 8 * rj + 8, 128 * t : 128 * t + 128]
                pair = (
                    pltpu.roll(jnp.where(left8, piece, 0.0), shift, 1),
                    pltpu.roll(jnp.where(left8, 0.0, piece), shift + 64, 1),
                )
                sums = [b if a is None else a + b for a, b in zip(sums, pair)]
            u_v[g * 4 + 2 * t] = sums[0]
            u_v[g * 4 + 2 * t + 1] = sums[1]
        return 0

    lax.fori_loop(0, GROUPS, backward_step, 0)

    small = None
    for cj in range(8):
        term = dot_exact(u_v[:, cj, :], e_v[128 * cj : 128 * cj + 128, :], 1, 0)
        small = term if small is None else small + term
    gain_sum = jnp.sum(acc_v[0], axis=0, keepdims=True)
    shift_sum = jnp.sum(acc_v[1], axis=0, keepdims=True)
    zero2 = jnp.zeros((2, LANES), F32)
    small = stack(
        small,
        *[gain_sum[:, LANES * n : LANES * n + LANES] for n in range(GROUPS)], zero2,
        *[shift_sum[:, LANES * n : LANES * n + LANES] for n in range(GROUPS)], zero2,
    )

    def sum_copies(buffer, send, recv, stage):
        if stage == 0:
            return [remote(
                buffer.at[0, core], buffer.at[0, core], send.at[0, 0], recv.at[0, 0], sibling
            )]
        axis = "xyz"[stage - 1]
        return [
            remote(
                buffer.at[stage, at[axis]], buffer.at[stage, at[axis]],
                send.at[stage, steps - 1], recv.at[stage, steps - 1], along(axis, steps),
            )
            for steps in (1, 2, 3)
        ]

    def sum_start(buffer, send, recv, stage, value):
        place = core if stage == 0 else at["xyz"[stage - 1]]
        buffer[stage, place] = value
        for copy in sum_copies(buffer, send, recv, stage):
            copy.start()

    def sum_finish(buffer, send, recv, stage):
        for copy in sum_copies(buffer, send, recv, stage):
            copy.wait()
        total = buffer[stage, 0] + buffer[stage, 1]
        if stage > 0:
            total = total + buffer[stage, 2] + buffer[stage, 3]
        return total

    sum_start(sm_v, sm_send, sm_recv, 0, small)

    def squares_copies(stage):
        copies = []
        if stage == 1:
            mine = sq1_v.at[at["x"] * 4 + at["y"]]
            for k in range(1, 16):
                chip = dict(at)
                chip["x"] = lax.rem(at["x"] + k // 4, 4)
                chip["y"] = lax.rem(at["y"] + k % 4, 4)
                copies.append(
                    remote(mine, mine, sq_send.at[0, k - 1], sq_recv.at[0, k - 1], device(chip, core))
                )
        else:
            mine = sq2_v.at[at["z"] * 2 + core]
            for k in range(1, 8):
                chip = dict(at)
                chip["z"] = lax.rem(at["z"] + k // 2, 4)
                on_core = core if k % 2 == 0 else 1 - core
                copies.append(
                    remote(mine, mine, sq_send.at[1, k - 1], sq_recv.at[1, k - 1], device(chip, on_core))
                )
        return copies

    def squares_start(stage, value):
        if stage == 1:
            sq1_v[at["x"] * 4 + at["y"]] = value
        else:
            sq2_v[at["z"] * 2 + core] = value
        for copy in squares_copies(stage):
            copy.start()

    def squares_finish(stage):
        for copy in squares_copies(stage):
            copy.wait()
        buffer, count = (sq1_v, 16) if stage == 1 else (sq2_v, 8)
        total = buffer[0]
        for k in range(1, count):
            total = total + buffer[k]
        return total

    def halo_d(n):
        cols = columns_of(n)
        rows = (slice(0, 48), slice(48, 96), slice(96, 112))
        targets = (shifted(0, 1), shifted(1, 0), shifted(1, 1))
        return [
            remote(
                send_d.at[rows[i], cols], came_d.at[rows[i], cols],
                last_send.at[n, i], last_recv.at[n, i], targets[i],
            )
            for i in range(3)
        ]

    def store_d(n):
        cols = columns_of(n)
        return pltpu.make_async_copy(dblk_v.at[:, :, cols], dtok_h.at[:, :, cols], last_store.at[n])

    def last_step(n, _):
        for copy in halo_d(n):
            copy.wait()
        output_block(flat_v, came_d, dblk_v, columns_of(n), low)
        store_d(n).start()
        return 0

    def d_token_step(n, _):
        cols = columns_of(n)
        flat_v[:, cols] = c_v[:, cols].astype(F32) + dot(dqkv_v[...], w_v[cols, :], 1, 1)
        output_strips(flat_v, send_d, cols, low)
        for copy in halo_d(n):
            copy.start()
        return 0

    for copy in halo_o:
        copy.wait()
    each_column(lambda cols: output_block(flat_v, came_o, oblk_v, cols, low))
    store_out = pltpu.make_async_copy(oblk_v, out_h, store_sem.at[0])
    store_out.start()

    for part in range(3):
        scatter_sum(0, part)
    lax.fori_loop(0, 2, d_token_step, 0)
    sum_start(sm_v, sm_send, sm_recv, 1, sum_finish(sm_v, sm_send, sm_recv, 0))
    for part in range(3):
        scatter_sum(1, part)
    lax.fori_loop(2, 4, d_token_step, 0)
    sum_start(sm_v, sm_send, sm_recv, 2, sum_finish(sm_v, sm_send, sm_recv, 1))
    for part in range(3):
        scatter_sum(2, part)
    fin_copy = remote(fin_v.at[0], fin_v.at[1], fin_sem.at[0], fin_sem.at[1], sibling)
    fin_copy.start()
    squares = fin_v[0] * fin_v[0]
    squares = squares[:8] + squares[8:16] + squares[16:]
    squares = sum(squares[:, 128 * n : 128 * n + 128] for n in range(6))
    squares_start(1, squares)
    lax.fori_loop(4, 6, d_token_step, 0)
    sum_start(sm_v, sm_send, sm_recv, 3, sum_finish(sm_v, sm_send, sm_recv, 2))
    squares = squares_finish(1)
    squares_start(2, squares)
    lax.fori_loop(0, GROUPS, last_step, 0)

    small = sum_finish(sm_v, sm_send, sm_recv, 3)
    squares = squares_finish(2)
    total = jnp.sum(squares, axis=(0, 1), keepdims=True)
    total = total + jnp.sum(small * small, axis=(0, 1), keepdims=True)
    factor = jnp.minimum(1.0, jnp.sqrt(PARAMS / (total + clip_epsilon)))
    drel = (small[:24] * factor).T
    for a in range(15):
        drel_ref[a] = drel[16 * a : 16 * a + 15]
    for n in range(GROUPS):
        dgain_ref[LANES * n : LANES * n + LANES] = (small[24 + n : 25 + n] * factor).reshape(LANES)
        dshift_ref[LANES * n : LANES * n + LANES] = (small[32 + n : 33 + n] * factor).reshape(LANES)
    fin_copy.wait()
    own, other = fin_v[0] * factor, fin_v[1] * factor
    own = jnp.where(core == 0, own[:12], own[12:])
    other = jnp.where(core == 0, other[:12], other[12:])
    dpw_ref[:, :HALF] = jnp.where(core == 0, own, other)
    dpw_ref[:, HALF:] = jnp.where(core == 0, other, own)
    store_out.wait()
    for n in range(GROUPS):
        store_d(n).wait()


def hand_over(*refs):
    sems = refs[12]
    copies = [pltpu.make_async_copy(refs[i], refs[6 + i], sems.at[i]) for i in range(6)]
    for copy in copies:
        copy.start()
    for copy in copies:
        copy.wait()


def on_device(tokens, qkv_weight, rel_bias, proj_weight, norm_gain, norm_shift, cotangent):
    anywhere = pl.BlockSpec(memory_space=pl.ANY)
    vmem = pl.BlockSpec(memory_space=pltpu.VMEM)
    dma = pltpu.SemaphoreType.DMA
    strips = [pltpu.VMEM((112, D), BF)] * 8
    scratch = [
        pltpu.VMEM((16, 16, D), BF),
        pltpu.VMEM((16, 16, D), BF),
        pltpu.VMEM((D, 3 * D), BF),
        pltpu.VMEM((D, D), BF),
        pltpu.VMEM((TOKENS, D), BF),
        pltpu.VMEM((TOKENS, D), BF),
        pltpu.VMEM((18, TOKENS, LANES), BF),
        pltpu.VMEM((GROUPS, WINDOWS, CELLS, LANES), F32),
        pltpu.VMEM((TOKENS, D), BF),
        pltpu.VMEM((2, D, TOKENS), BF),
        pltpu.VMEM((TOKENS, D), F32),
        pltpu.VMEM((TOKENS, D), F32),
        pltpu.VMEM((TOKENS, D), BF),
        pltpu.VMEM((TOKENS, HALF), BF),
        pltpu.VMEM((GROUPS, TOKENS, LANES), BF),
        pltpu.VMEM((TOKENS, 3 * D), BF),
        pltpu.VMEM((16, 16, D), BF),
        pltpu.VMEM((16, 16, D), BF),
        pltpu.VMEM((1024, LANES), BF),
        pltpu.VMEM((LANES, HEADS), F32),
        pltpu.VMEM((1, D), F32),
        pltpu.VMEM((1, D), F32),
        pltpu.VMEM((HEADS, 8, 128), F32),
        pltpu.VMEM((GROUPS, CELLS, LANES), F32),
        pltpu.VMEM((CELLS, LANES), F32),
        pltpu.VMEM((HEADS, 8, 128), F32),
        pltpu.VMEM((2, 8, D), F32),
        *strips,
        pltpu.VMEM((3, 2, 4, 4, 2, 48, 128), BF),
        pltpu.VMEM((2, 3, 2, 4, 2, 48, 128), BF),
        pltpu.VMEM((3, 4, 4, 48, 128), BF),
        pltpu.VMEM((2, 4, 2, 48, 128), BF),
        pltpu.VMEM((2, 4, 2, 48, 128), BF),
        pltpu.VMEM((4, 4, 48, 128), BF),
        pltpu.VMEM((3, 2, 2, 48, 128), BF),
        pltpu.VMEM((3, 4, 48, 128), BF),
        pltpu.VMEM((3, 4, 48, 128), BF),
        pltpu.VMEM((2, 2, 48, 128), F32),
        pltpu.VMEM((4, 48, 128), F32),
        pltpu.VMEM((4, 48, 128), F32),
        pltpu.VMEM((3, 3, 48, 128), F32),
        pltpu.VMEM((2, 24, HALF), F32),
        pltpu.VMEM((4, 4, 40, LANES), F32),
        pltpu.VMEM((16, 8, 128), F32),
        pltpu.VMEM((8, 8, 128), F32),
        dma((3,)),
        dma((18,)),
        dma((1,)),
        dma((3, 3)),
        dma((3, 3)),
        dma((GROUPS,)),
        dma((GROUPS,)),
        dma((WINDOWS,)),
        dma((WINDOWS,)),
        dma((3, 3, 3)),
        dma((3, 3, 3)),
        dma((4, 3)),
        dma((4, 3)),
        dma((2, 15)),
        dma((2, 15)),
        dma((GROUPS, 3)),
        dma((GROUPS, 3)),
        dma((GROUPS,)),
        dma((2,)),
    ]
    results = pl.pallas_call(
        sublayer,
        out_shape=(
            jax.ShapeDtypeStruct((16, 16, D), BF),
            jax.ShapeDtypeStruct((16, 16, D), BF),
            jax.ShapeDtypeStruct((12, D), F32),
            jax.ShapeDtypeStruct((15, 15, HEADS), F32),
            jax.ShapeDtypeStruct((D,), F32),
            jax.ShapeDtypeStruct((D,), F32),
        ),
        in_specs=[anywhere, anywhere, vmem, anywhere, vmem, vmem, anywhere],
        out_specs=(anywhere, anywhere, vmem, vmem, vmem, vmem),
        scratch_shapes=scratch,
        compiler_params=pltpu.CompilerParams(
            collective_id=0, has_side_effects=True, vmem_limit_bytes=60 * 2**20
        ),
        name="sublayer",
    )(
        tokens, qkv_weight, rel_bias.transpose(1, 2, 0), proj_weight, norm_gain, norm_shift, cotangent,
    )
    out, d_tokens, d_proj, d_rel, d_gain, d_shift = pl.pallas_call(
        hand_over,
        out_shape=tuple(jax.ShapeDtypeStruct(r.shape, r.dtype) for r in results),
        in_specs=[anywhere] * 6,
        out_specs=(anywhere,) * 6,
        scratch_shapes=[dma((6,))],
        compiler_params=pltpu.CompilerParams(vmem_limit_bytes=60 * 2**20),
        name="hand_over",
    )(*results)
    return out, d_tokens, d_proj, d_rel.transpose(2, 0, 1), d_gain, d_shift


def solution(mesh):
    in_specs = (P("lat", "lon", None), P(), P(), P(), P(), P(), P("lat", "lon", None))
    out_specs = (
        P("lat", "lon", None),
        P("lat", "lon", None),
        P(("lon", "lat"), None),
        P(),
        P(),
        P(),
    )
    return jax.shard_map(
        on_device, mesh=mesh, in_specs=in_specs, out_specs=out_specs, check_vma=False
    )
```

```python
import functools

import jax
import jax.numpy as jnp
from jax import lax
from jax.experimental import pallas as pl
from jax.experimental.pallas import tpu as pltpu
from jax.sharding import PartitionSpec as P

F32 = jnp.float32
BF = jnp.bfloat16
MESH = pl.DeviceIdType.MESH

D = 1536
HEADS = 24
GROUPS = 6
LANES = 256
TOKENS = 256
CELLS = 64
WINDOWS = 4
HALF = 768
PARAMS = 2367768
norm_epsilon = 1e-05
clip_epsilon = 1e-06

ORDERS = (("x", "y", "z"), ("y", "z", "x"), ("z", "x", "y"))


def dot(a, b, ca, cb):
    return lax.dot_general(a, b, (((ca,), (cb,)), ((), ())), preferred_element_type=F32)


def dot_exact(a, b, ca, cb):
    total = None
    for _ in range(3):
        part = a.astype(BF)
        a = a - part.astype(F32)
        term = dot(part, b, ca, cb)
        total = term if total is None else total + term
    return total


def stack(*pieces):
    return jnp.concatenate(pieces, axis=0)


def turn(value):
    return pltpu.roll(value, 4, 0)


def low_rows(columns):
    return lax.broadcasted_iota(jnp.int32, (8, columns), 0) < 4


def halves(ref, rows, cols):
    both = ref[rows, cols].astype(F32)
    return both[:8], both[8:]


def row_halves(block, row, cols):
    both = block[row, :, cols].astype(F32)
    return both[:8], both[8:]


def columns_of(step, width=LANES):
    return pl.ds(pl.multiple_of(step * width, width), width)


def pack_first(a, b):
    return jnp.where(low_rows(a.shape[1]), a, turn(b))


def pack_last(a, b):
    return jnp.where(low_rows(a.shape[1]), turn(a), b)


def four_pairs(pack, values):
    return stack(pack(values[0], values[1]), pack(values[2], values[3])).astype(BF)


STRIPS = (slice(0, 32), slice(32, 48), slice(48, 96), slice(96, 112))
STRIP_STEPS = ((0, 1), (0, -1), (1, 0), (1, -1))


def input_strips(block, strips, cols, low):
    for k in range(2):
        rows = [row_halves(block, 4 + 4 * k + i, cols)[0] for i in range(4)]
        strips[16 * k : 16 * k + 16, cols] = four_pairs(pack_first, rows)
    rows = [row_halves(block, 12 + i, cols)[1] for i in range(4)]
    strips[32:48, cols] = four_pairs(pack_last, rows)
    t = [row_halves(block, r, cols) for r in range(4)]
    wide = [turn(jnp.where(low, t1, t0)) for t0, t1 in t]
    strips[48:64, cols] = stack(wide[0], wide[1]).astype(BF)
    strips[64:80, cols] = stack(wide[2], wide[3]).astype(BF)
    strips[80:96, cols] = four_pairs(pack_first, [t0 for t0, _ in t])
    strips[96:112, cols] = four_pairs(pack_last, [t1 for _, t1 in t])


def own_windows(block, flat, cols, low):
    for r, at in ((4, 0), (6, 16), (8, 32), (10, 48), (12, 192), (14, 208)):
        t0, t1 = row_halves(block, r, cols)
        u0, u1 = row_halves(block, r + 1, cols)
        flat[at : at + 16, cols] = stack(
            turn(jnp.where(low, t1, t0)), turn(jnp.where(low, u1, u0))
        ).astype(BF)


def input_windows(block, came, flat, cols, low):
    for k in range(2):
        pairs = halves(came, slice(16 * k, 16 * k + 16), cols)
        for i in range(2):
            r = 4 * k + 2 * i
            s = pairs[i]
            t1 = row_halves(block, r + 4, cols)[1]
            u1 = row_halves(block, r + 5, cols)[1]
            flat[64 + 8 * r : 80 + 8 * r, cols] = stack(
                jnp.where(low, turn(t1), turn(s)), jnp.where(low, turn(u1), s)
            ).astype(BF)
    west = halves(came, slice(32, 48), cols)
    side = halves(came, slice(80, 96), cols)
    corner = halves(came, slice(96, 112), cols)
    for i in range(2):
        t0 = row_halves(block, 12 + 2 * i, cols)[0]
        u0 = row_halves(block, 13 + 2 * i, cols)[0]
        s = west[i]
        flat[128 + 16 * i : 144 + 16 * i, cols] = stack(
            jnp.where(low, s, turn(t0)), jnp.where(low, turn(s), turn(u0))
        ).astype(BF)
        s, d = side[i], corner[i]
        flat[160 + 16 * i : 176 + 16 * i, cols] = stack(
            jnp.where(low, d, turn(s)), jnp.where(low, turn(d), s)
        ).astype(BF)
        flat[224 + 16 * i : 240 + 16 * i, cols] = came[48 + 16 * i : 64 + 16 * i, cols]


def output_strips(flat, strips, cols):
    def rows_of(start):
        return [flat[start + 8 * i : start + 8 * i + 8, cols] for i in range(4)]

    for k in range(2):
        strips[16 * k : 16 * k + 16, cols] = four_pairs(pack_last, rows_of(64 + 32 * k))
    strips[32:48, cols] = four_pairs(pack_first, rows_of(128))
    strips[48:80, cols] = flat[224:256, cols].astype(BF)
    strips[80:96, cols] = four_pairs(pack_last, rows_of(160))
    strips[96:112, cols] = four_pairs(pack_first, rows_of(160))


def output_block(flat, came, block, cols, low):
    for k in range(2):
        pairs = halves(came, slice(16 * k, 16 * k + 16), cols)
        for i in range(4):
            r = 4 * k + i
            s = pairs[i // 2]
            s = s if i % 2 == 0 else turn(s)
            a = turn(flat[8 * r : 8 * r + 8, cols])
            b = turn(flat[64 + 8 * r : 72 + 8 * r, cols])
            block[r + 4, :, cols] = stack(jnp.where(low, s, a), jnp.where(low, a, b)).astype(BF)
    east = halves(came, slice(32, 48), cols)
    side = halves(came, slice(80, 96), cols)
    corner = halves(came, slice(96, 112), cols)
    for i in range(2):
        wides = halves(came, slice(48 + 16 * i, 64 + 16 * i), cols)
        for k in range(2):
            r = 2 * i + k
            a = turn(flat[128 + 8 * r : 136 + 8 * r, cols])
            b = turn(flat[192 + 8 * r : 200 + 8 * r, cols])
            s = turn(east[i]) if k == 0 else east[i]
            block[12 + r, :, cols] = stack(jnp.where(low, a, b), jnp.where(low, b, s)).astype(BF)
            wide = turn(wides[k])
            at_low = side[i] if k == 0 else turn(side[i])
            at_high = turn(corner[i]) if k == 0 else corner[i]
            block[r, :, cols] = stack(
                jnp.where(low, at_low, wide), jnp.where(low, wide, at_high)
            ).astype(BF)


def block_diagonal(value, lane_head):
    zero = jnp.zeros_like(value)
    return stack(*[jnp.where(lane_head == h, value, zero) for h in range(4)])


def diagonal(product, left):
    tiles = []
    for t in range(2):
        cols = slice(128 * t, 128 * t + 128)
        tiles.append(
            jnp.where(
                left,
                product[128 * t : 128 * t + 64, cols],
                product[128 * t + 64 : 128 * t + 128, cols],
            )
        )
    return jnp.concatenate(tiles, axis=1)


def sublayer(
    tok_h, wq_h, rel_ref, pw_h, gain_ref, shift_ref, cot_h,
    out_h, dtok_h, dpw_ref, drel_ref, dgain_ref, dshift_ref,
    tok_v, cot_v, w_v, pw_v, x_v, c_v, qkv_v, pt_v, mix_v, mixt_v, proj_v, flat_v,
    dp_v, dps_v, dmix_v, dqkv_v, oblk_v, dblk_v,
    e_v, rel_v, gain_v, shift_v, wb_v, bt_v, mask_v, u_v, acc_v,
    send_x, came_x, send_c, came_c, send_o, came_o, send_d, came_d,
    p_v, r1a, r1c, s2a, s2b, s2c, r2a, r2b, r2c, s3a, s3b, s3c, r3, fin_v,
    sm_v, sq_v,
    load_sem, w_sem, store_sem, halo_send, halo_recv, mix_send, mix_recv, dp_send, dp_recv,
    rs_send, rs_recv, sm_send, sm_recv, sq_send, sq_recv, last_store, fin_sem,
):
    lon = lax.axis_index("lon")
    lat = lax.axis_index("lat")
    core = lax.rem(lat, 2)
    at = {
        "x": lax.rem(lon // 4, 4),
        "y": lax.rem(lon, 4),
        "z": (lon // 16) * 2 + lat // 2,
    }

    def device(chip, on_core):
        z = chip["z"]
        return {
            "lon": (z // 2) * 16 + chip["x"] * 4 + chip["y"],
            "lat": lax.rem(z, 2) * 2 + on_core,
        }

    def along(axis, steps, on_core=core):
        chip = dict(at)
        chip[axis] = lax.rem(at[axis] + steps, 4)
        return device(chip, on_core)

    sibling = device(at, 1 - core)

    def shifted(lat_steps, lon_steps):
        return {
            "lon": lax.rem(lon + lon_steps + 32, 32),
            "lat": lax.rem(lat + lat_steps + 4, 4),
        }

    def remote(src, dst, send, recv, target):
        return pltpu.make_async_remote_copy(
            src_ref=src, dst_ref=dst, send_sem=send, recv_sem=recv,
            device_id=target, device_id_type=MESH,
        )

    load_tok = pltpu.make_async_copy(tok_h, tok_v, load_sem.at[0])
    load_cot = pltpu.make_async_copy(cot_h, cot_v, load_sem.at[1])
    load_pw = pltpu.make_async_copy(pw_h, pw_v, load_sem.at[2])

    def load_w(chunk):
        cols = columns_of(chunk)
        return pltpu.make_async_copy(wq_h.at[:, cols], w_v.at[:, cols], w_sem.at[chunk])

    load_tok.start()
    load_cot.start()

    partners = [shifted(0, 1), shifted(0, -1), shifted(1, 0), shifted(-1, 0), shifted(1, -1), shifted(-1, 1)]
    circles = [[along(axis, steps) for steps in (1, 2, 3)] for axis in "xy"]
    circles.append(
        [sibling] + [along("z", steps) for steps in (1, 2, 3)] + [along("z", steps, 1 - core) for steps in (1, 2, 3)]
    )
    partners += circles[0] + circles[1] + circles[2]
    barrier = pltpu.get_barrier_semaphore()
    for partner in partners:
        pl.semaphore_signal(barrier, inc=1, device_id=partner, device_id_type=MESH)

    for g in range(GROUPS):
        for part in range(3):
            load_w(part * GROUPS + g).start()
    load_pw.start()

    low = low_rows(LANES)

    def each_column(body):
        lax.fori_loop(0, GROUPS, lambda n, _: (body(columns_of(n)), 0)[1], 0)

    def halo(strips, came, which, sign, cols=slice(None)):
        return [
            remote(
                strips.at[rows, cols], came.at[rows, cols],
                halo_send.at[which, i], halo_recv.at[which, i],
                shifted(sign * STRIP_STEPS[i][0], sign * STRIP_STEPS[i][1]),
            )
            for i, rows in enumerate(STRIPS)
        ]

    load_tok.wait()
    each_column(lambda cols: input_strips(tok_v, send_x, cols, low))
    pl.semaphore_wait(barrier, len(partners))
    halo_x = halo(send_x, came_x, 0, -1)
    for copy in halo_x:
        copy.start()
    each_column(lambda cols: own_windows(tok_v, x_v, cols, low))
    load_cot.wait()
    each_column(lambda cols: input_strips(cot_v, send_c, cols, low))
    halo_c = halo(send_c, came_c, 1, -1)
    for copy in halo_c:
        copy.start()
    each_column(lambda cols: own_windows(cot_v, c_v, cols, low))

    spot = lax.broadcasted_iota(jnp.int32, (128, LANES), 0)
    slot = lax.broadcasted_iota(jnp.int32, (128, LANES), 1)
    for cj in range(8):
        hit = ((spot >> 3) == (slot >> 4)) & ((spot & 7) - cj + 7 == (slot & 15))
        e_v[128 * cj : 128 * cj + 128, :] = jnp.where(hit, 1.0, 0.0).astype(BF)
    rel_v[...] = jnp.zeros_like(rel_v)
    for a in range(15):
        rel_v[16 * a : 16 * a + 15, :] = rel_ref[a]
    rel = rel_v[...]
    for cj in range(8):
        wb_v[:, cj, :] = dot_exact(rel, e_v[128 * cj : 128 * cj + 128, :], 0, 1)
    left8 = lax.broadcasted_iota(jnp.int32, (8, 128), 1) < 64

    def bias_step(g, _):
        for t in range(2):
            first = wb_v[g * 4 + 2 * t]
            second = wb_v[g * 4 + 2 * t + 1]
            for rj in range(8):
                shift = (7 - rj) * 8
                bt_v[g, 8 * rj : 8 * rj + 8, 128 * t : 128 * t + 128] = jnp.where(
                    left8,
                    pltpu.roll(first, (128 - shift) % 128, 1),
                    pltpu.roll(second, (192 - shift) % 128, 1),
                )
        return 0

    lax.fori_loop(0, GROUPS, bias_step, 0)
    j_upper = lax.broadcasted_iota(jnp.int32, (CELLS, LANES), 0) < 32
    i_upper = (lax.broadcasted_iota(jnp.int32, (CELLS, LANES), 1) & 63) < 32
    crossing = (j_upper != i_upper) & (lat == 3)
    mask_v[...] = jnp.where(crossing, -jnp.inf, 0.0)

    for copy in halo_x:
        copy.wait()
    each_column(lambda cols: input_windows(tok_v, came_x, x_v, cols, low))

    lane_head = lax.broadcasted_iota(jnp.int32, (CELLS, LANES), 1) >> 6
    left = lax.broadcasted_iota(jnp.int32, (CELLS, 128), 1) < 64

    def mix_copy(g):
        rows = columns_of(g)
        return remote(
            mixt_v.at[0, rows], mixt_v.at[1, rows], mix_send.at[g], mix_recv.at[g], sibling
        )

    def make_qkv(g):
        for part in range(3):
            chunk = part * GROUPS + g
            value = dot(x_v[...], w_v[:, columns_of(chunk)], 1, 0).astype(BF)
            if part == 0:
                value = value * jnp.asarray(0.125, BF)
            qkv_v[chunk] = value

    def wait_weights(g):
        for part in range(3):
            load_w(part * GROUPS + g).wait()

    def attend(g):
        bias = bt_v[g]
        masked = bias + mask_v[...]
        mixed = []
        for w in range(WINDOWS):
            rows = slice(CELLS * w, CELLS * w + CELLS)
            q, k, v = [qkv_v[part * GROUPS + g, rows, :] for part in range(3)]
            scores = dot(k, block_diagonal(q, lane_head), 1, 1) + (bias if w < 2 else masked)
            peak = jnp.max(scores, axis=0, keepdims=True)
            raised = jnp.exp(scores - peak)
            shares = raised * (1.0 / jnp.sum(raised, axis=0, keepdims=True))
            pt_v[g, w] = shares
            mixed.append(diagonal(dot(shares.astype(BF), v, 0, 0), left).astype(BF))
        mixed = stack(*mixed)
        mix_v[:, columns_of(g)] = mixed
        mixt_v[0, columns_of(g), :] = mixed.T

    def forward_step(g, _):
        wait_weights(g + 1)
        attend(g)
        make_qkv(g + 1)
        mix_copy(g).start()
        return 0

    wait_weights(0)
    make_qkv(0)
    lax.fori_loop(0, GROUPS - 1, forward_step, 0)
    attend(GROUPS - 1)
    mix_copy(GROUPS - 1).start()

    def project_step(n, _):
        cols = columns_of(n)
        proj_v[:, cols] = dot(mix_v[...], pw_v[:, cols], 1, 0)
        return 0

    load_pw.wait()
    lax.fori_loop(0, GROUPS, project_step, 0)

    for copy in halo_c:
        copy.wait()
    each_column(lambda cols: input_windows(cot_v, came_c, c_v, cols, low))

    acc_v[...] = jnp.zeros_like(acc_v)
    gain = gain_ref[...].reshape(1, D)
    shift = shift_ref[...].reshape(1, D)
    gain_v[...] = gain
    shift_v[...] = shift

    other_half = pl.ds(pl.multiple_of((1 - core) * HALF, HALF), HALF)

    def dp_copy(m):
        rows = pl.ds(pl.multiple_of(m * CELLS, CELLS), CELLS)
        return remote(dp_v.at[rows, other_half], dps_v.at[rows], dp_send.at[m], dp_recv.at[m], sibling)

    def norm_step(m, _):
        sums = [None, None]
        for part in range(4):
            rows = pl.ds(pl.multiple_of(m * CELLS + 16 * part, 16), 16)
            projected = proj_v[rows, :]
            centre = projected - jnp.mean(projected, axis=1, keepdims=True)
            inverse = lax.rsqrt(jnp.mean(centre * centre, axis=1, keepdims=True) + norm_epsilon)
            normed = centre * inverse
            flat_v[rows, :] = x_v[rows, :].astype(F32) + normed * gain_v[...] + shift_v[...]
            upstream = c_v[rows, :].astype(F32)
            product = upstream * normed
            terms = (product[:8] + product[8:], upstream[:8] + upstream[8:])
            sums = [b if a is None else a + b for a, b in zip(sums, terms)]
            d_normed = upstream * gain_v[...]
            inner = d_normed - jnp.mean(d_normed, axis=1, keepdims=True)
            inner = inner - normed * jnp.mean(d_normed * normed, axis=1, keepdims=True)
            dp_v[rows, :] = (inverse * inner).astype(BF)
        acc_v[0] += sums[0]
        acc_v[1] += sums[1]
        dp_copy(m).start()
        return 0

    lax.fori_loop(0, TOKENS // CELLS, norm_step, 0)

    each_column(lambda cols: output_strips(flat_v, send_o, cols))
    halo_o = halo(send_o, came_o, 2, 1)
    for copy in halo_o:
        copy.start()

    for m in range(WINDOWS):
        dp_copy(m).wait()
    for g in range(GROUPS):
        mix_copy(g).wait()

    def slot_of(buffer, lead, axes, axis, index):
        if axis == "z":
            places = {"h": index // 2, "l": lax.rem(index, 2)}
        else:
            places = {axis: index}
        return buffer.at[lead + tuple(places.get(name, slice(None)) for name in axes)]

    stages = (
        ((p_v, (0,), "hxyl"), (p_v, (1,), "hxyl"), (p_v, (2,), "hxyl")),
        ((s2a, (), "hyl"), (s2b, (), "hxl"), (s2c, (), "xy")),
        ((s3a, (), "hl"), (s3b, (), "x"), (s3c, (), "y")),
    )
    arrivals = (
        (r1a.at[0], r1a.at[1], r1c),
        (r2a, r2b, r2c),
        (r3.at[0], r3.at[1], r3.at[2]),
    )

    pieces = (slice(0, 32), slice(32, 48))

    def scatter_copies(stage, part, piece):
        buffer, lead, axes = stages[stage][part]
        axis = ORDERS[part][stage]
        rows = pieces[piece]
        whole = (slice(None),) * (len(axes) - (2 if axis == "z" else 1))
        copies = []
        for steps in (1, 2, 3):
            index = lax.rem(at[axis] + steps, 4)
            copies.append(
                remote(
                    slot_of(buffer, lead, axes, axis, index).at[whole + (rows,)],
                    arrivals[stage][part].at[(steps - 1,) + whole + (rows,)],
                    rs_send.at[stage, part, 3 * piece + steps - 1],
                    rs_recv.at[stage, part, 3 * piece + steps - 1],
                    along(axis, steps),
                )
            )
        return copies

    def scatter_start(stage, part, piece):
        for copy in scatter_copies(stage, part, piece):
            copy.start()

    def scatter_sum(stage, part, piece):
        for copy in scatter_copies(stage, part, piece):
            copy.wait()
        buffer, lead, axes = stages[stage][part]
        axis = ORDERS[part][stage]
        rows = pieces[piece]
        whole = (slice(None),) * (len(axes) - (2 if axis == "z" else 1))
        total = slot_of(buffer, lead, axes, axis, at[axis])[whole + (rows,)].astype(F32)
        for steps in range(3):
            total = total + arrivals[stage][part][(steps,) + whole + (rows,)].astype(F32)
        if stage < 2:
            target = stages[stage + 1][part][0]
            target[whole + (rows,)] = total.astype(target.dtype)
            scatter_start(stage + 1, part, piece)
        elif piece == 0:
            fin_v[0, :, LANES * part : LANES * part + 128] = total[:24]
            fin_v[0, :8, LANES * part + 128 : LANES * part + 256] = total[24:]
        else:
            fin_v[0, 8:, LANES * part + 128 : LANES * part + 256] = total

    def scatter_sums(stage, piece):
        for part in range(3):
            scatter_sum(stage, part, piece)

    for part in range(3):
        own = dp_v[:, pl.ds(pl.multiple_of(core * HALF + part * LANES, LANES), LANES)]
        other = dps_v[:, LANES * part : LANES * part + LANES]
        for mb in range(4):
            rows = slice(384 * mb, 384 * mb + 384)
            value = dot(mixt_v[0, rows, :], own, 1, 0) + dot(mixt_v[1, rows, :], other, 1, 0)
            value = jnp.concatenate(
                [value[:, :128].reshape(16, 24, 128), value[:, 128:].reshape(16, 24, 128)], axis=1
            )
            p_v[part, mb // 2, 2 * (mb % 2) : 2 * (mb % 2) + 2] = value.astype(BF).reshape(
                2, 4, 2, 48, 128
            )
        scatter_start(0, part, 0)
    for part in range(3):
        scatter_start(0, part, 1)

    def d_mixed_step(n, _):
        dmix_v[n] = dot(dp_v[...], pw_v[columns_of(n), :], 1, 1).astype(BF)
        return 0

    lax.fori_loop(0, GROUPS, d_mixed_step, 0)

    def backward_step(g, _):
        total = None
        for w in range(WINDOWS):
            rows = slice(CELLS * w, CELLS * w + CELLS)
            q, k, v = [qkv_v[part * GROUPS + g, rows, :] for part in range(3)]
            d_out = block_diagonal(dmix_v[g, rows, :], lane_head)
            shares = pt_v[g, w]
            d_shares = dot(v, d_out, 1, 1)
            d_scores = shares * (d_shares - jnp.sum(shares * d_shares, axis=0, keepdims=True))
            total = d_scores if total is None else total + d_scores
            low_scores = d_scores.astype(BF)
            dq = diagonal(dot(low_scores, k, 0, 0), left) * 0.125
            dk = dot(low_scores, block_diagonal(q, lane_head), 1, 0)
            dv = dot(shares.astype(BF), d_out, 1, 0)
            for part, value in enumerate((dq, dk, dv)):
                dqkv_v[rows, columns_of(part * GROUPS + g)] = value.astype(BF)
        for t in range(2):
            sums = [None, None]
            for rj in range(8):
                shift = (7 - rj) * 8
                piece = total[8 * rj : 8 * rj + 8, 128 * t : 128 * t + 128]
                pair = (
                    pltpu.roll(jnp.where(left8, piece, 0.0), shift, 1),
                    pltpu.roll(jnp.where(left8, 0.0, piece), shift + 64, 1),
                )
                sums = [b if a is None else a + b for a, b in zip(sums, pair)]
            u_v[g * 4 + 2 * t] = sums[0]
            u_v[g * 4 + 2 * t + 1] = sums[1]
        return 0

    lax.fori_loop(0, 4, backward_step, 0)
    scatter_sums(0, 0)
    lax.fori_loop(4, GROUPS, backward_step, 0)
    scatter_sums(0, 1)

    small = None
    for cj in range(8):
        term = dot_exact(u_v[:, cj, :], e_v[128 * cj : 128 * cj + 128, :], 1, 0)
        small = term if small is None else small + term
    gain_sum = jnp.sum(acc_v[0], axis=0, keepdims=True)
    shift_sum = jnp.sum(acc_v[1], axis=0, keepdims=True)
    zero2 = jnp.zeros((2, LANES), F32)
    small = stack(
        small,
        *[gain_sum[:, LANES * n : LANES * n + LANES] for n in range(GROUPS)], zero2,
        *[shift_sum[:, LANES * n : LANES * n + LANES] for n in range(GROUPS)], zero2,
    )

    def sum_copies(buffer, send, recv, stage):
        if stage == 0:
            return [remote(
                buffer.at[0, core], buffer.at[0, core], send.at[0, 0], recv.at[0, 0], sibling
            )]
        axis = "xyz"[stage - 1]
        return [
            remote(
                buffer.at[stage, at[axis]], buffer.at[stage, at[axis]],
                send.at[stage, steps - 1], recv.at[stage, steps - 1], along(axis, steps),
            )
            for steps in (1, 2, 3)
        ]

    def sum_start(buffer, send, recv, stage, value):
        place = core if stage == 0 else at["xyz"[stage - 1]]
        buffer[stage, place] = value
        for copy in sum_copies(buffer, send, recv, stage):
            copy.start()

    def sum_finish(buffer, send, recv, stage):
        for copy in sum_copies(buffer, send, recv, stage):
            copy.wait()
        total = buffer[stage, 0] + buffer[stage, 1]
        if stage > 0:
            total = total + buffer[stage, 2] + buffer[stage, 3]
        return total

    sum_start(sm_v, sm_send, sm_recv, 0, small)

    def squares_place(stage):
        return (at["x"], at["y"], at["z"] * 2 + core)[stage]

    def squares_copies(stage):
        mine = sq_v.at[stage, squares_place(stage)]
        return [
            remote(mine, mine, sq_send.at[stage, i], sq_recv.at[stage, i], target)
            for i, target in enumerate(circles[stage])
        ]

    def squares_start(stage, value):
        sq_v[stage, squares_place(stage)] = value
        for copy in squares_copies(stage):
            copy.start()

    def squares_finish(stage):
        for copy in squares_copies(stage):
            copy.wait()
        total = sq_v[stage, 0]
        for k in range(1, 4 if stage < 2 else 8):
            total = total + sq_v[stage, k]
        return total

    def halo_d(n):
        return halo(send_d, came_d, 3 + n, 1, columns_of(n))

    def store_d(n):
        cols = columns_of(n)
        return pltpu.make_async_copy(dblk_v.at[:, :, cols], dtok_h.at[:, :, cols], last_store.at[n])

    def last_step(n, _):
        for copy in halo_d(n):
            copy.wait()
        output_block(flat_v, came_d, dblk_v, columns_of(n), low)
        store_d(n).start()
        return 0

    def d_token_step(n, _):
        cols = columns_of(n)
        flat_v[:, cols] = c_v[:, cols].astype(F32) + dot(dqkv_v[...], w_v[cols, :], 1, 1)
        output_strips(flat_v, send_d, cols)
        for copy in halo_d(n):
            copy.start()
        return 0

    for copy in halo_o:
        copy.wait()
    each_column(lambda cols: output_block(flat_v, came_o, oblk_v, cols, low))
    store_out = pltpu.make_async_copy(oblk_v, out_h, store_sem.at[0])
    store_out.start()

    scatter_sums(1, 0)
    lax.fori_loop(0, 1, d_token_step, 0)
    sum_start(sm_v, sm_send, sm_recv, 1, sum_finish(sm_v, sm_send, sm_recv, 0))
    scatter_sums(1, 1)
    scatter_sums(2, 0)
    lax.fori_loop(1, 3, d_token_step, 0)
    scatter_sums(2, 1)
    fin_copy = remote(fin_v.at[0], fin_v.at[1], fin_sem.at[0], fin_sem.at[1], sibling)
    fin_copy.start()
    squares = fin_v[0] * fin_v[0]
    squares = squares[:8] + squares[8:16] + squares[16:]
    squares = sum(squares[:, 128 * n : 128 * n + 128] for n in range(6))
    squares_start(0, squares)
    sum_start(sm_v, sm_send, sm_recv, 2, sum_finish(sm_v, sm_send, sm_recv, 1))
    lax.fori_loop(3, 4, d_token_step, 0)
    squares_start(1, squares_finish(0))
    sum_start(sm_v, sm_send, sm_recv, 3, sum_finish(sm_v, sm_send, sm_recv, 2))
    lax.fori_loop(4, 6, d_token_step, 0)
    squares_start(2, squares_finish(1))
    lax.fori_loop(0, GROUPS, last_step, 0)

    small = sum_finish(sm_v, sm_send, sm_recv, 3)
    squares = squares_finish(2)
    total = jnp.sum(squares, axis=(0, 1), keepdims=True)
    total = total + jnp.sum(small * small, axis=(0, 1), keepdims=True)
    factor = jnp.minimum(1.0, jnp.sqrt(PARAMS / (total + clip_epsilon)))
    drel = (small[:24] * factor).T
    for a in range(15):
        drel_ref[a] = drel[16 * a : 16 * a + 15]
    for n in range(GROUPS):
        dgain_ref[LANES * n : LANES * n + LANES] = (small[24 + n : 25 + n] * factor).reshape(LANES)
        dshift_ref[LANES * n : LANES * n + LANES] = (small[32 + n : 33 + n] * factor).reshape(LANES)
    fin_copy.wait()
    own, other = fin_v[0] * factor, fin_v[1] * factor
    own = jnp.where(core == 0, own[:12], own[12:])
    other = jnp.where(core == 0, other[:12], other[12:])
    dpw_ref[:, :HALF] = jnp.where(core == 0, own, other)
    dpw_ref[:, HALF:] = jnp.where(core == 0, other, own)
    store_out.wait()
    for n in range(GROUPS):
        store_d(n).wait()


def hand_over(*refs):
    source, target, held, load_sem, store_sem = refs[:6], refs[6:12], refs[12:18], refs[18], refs[19]
    loads = [pltpu.make_async_copy(source[i], held[i], load_sem.at[i]) for i in range(6)]
    stores = [pltpu.make_async_copy(held[i], target[i], store_sem.at[i]) for i in range(6)]
    for load in loads:
        load.start()
    for load, store in zip(loads, stores):
        load.wait()
        store.start()
    for store in stores:
        store.wait()


def on_device(tokens, qkv_weight, rel_bias, proj_weight, norm_gain, norm_shift, cotangent):
    anywhere = pl.BlockSpec(memory_space=pl.ANY)
    vmem = pl.BlockSpec(memory_space=pltpu.VMEM)
    dma = pltpu.SemaphoreType.DMA
    strips = [pltpu.VMEM((112, D), BF)] * 8
    scratch = [
        pltpu.VMEM((16, 16, D), BF),
        pltpu.VMEM((16, 16, D), BF),
        pltpu.VMEM((D, 3 * D), BF),
        pltpu.VMEM((D, D), BF),
        pltpu.VMEM((TOKENS, D), BF),
        pltpu.VMEM((TOKENS, D), BF),
        pltpu.VMEM((18, TOKENS, LANES), BF),
        pltpu.VMEM((GROUPS, WINDOWS, CELLS, LANES), F32),
        pltpu.VMEM((TOKENS, D), BF),
        pltpu.VMEM((2, D, TOKENS), BF),
        pltpu.VMEM((TOKENS, D), F32),
        pltpu.VMEM((TOKENS, D), F32),
        pltpu.VMEM((TOKENS, D), BF),
        pltpu.VMEM((TOKENS, HALF), BF),
        pltpu.VMEM((GROUPS, TOKENS, LANES), BF),
        pltpu.VMEM((TOKENS, 3 * D), BF),
        pltpu.VMEM((16, 16, D), BF),
        pltpu.VMEM((16, 16, D), BF),
        pltpu.VMEM((1024, LANES), BF),
        pltpu.VMEM((LANES, HEADS), F32),
        pltpu.VMEM((1, D), F32),
        pltpu.VMEM((1, D), F32),
        pltpu.VMEM((HEADS, 8, 128), F32),
        pltpu.VMEM((GROUPS, CELLS, LANES), F32),
        pltpu.VMEM((CELLS, LANES), F32),
        pltpu.VMEM((HEADS, 8, 128), F32),
        pltpu.VMEM((2, 8, D), F32),
        *strips,
        pltpu.VMEM((3, 2, 4, 4, 2, 48, 128), BF),
        pltpu.VMEM((2, 3, 2, 4, 2, 48, 128), BF),
        pltpu.VMEM((3, 4, 4, 48, 128), BF),
        pltpu.VMEM((2, 4, 2, 48, 128), BF),
        pltpu.VMEM((2, 4, 2, 48, 128), BF),
        pltpu.VMEM((4, 4, 48, 128), BF),
        pltpu.VMEM((3, 2, 2, 48, 128), BF),
        pltpu.VMEM((3, 4, 48, 128), BF),
        pltpu.VMEM((3, 4, 48, 128), BF),
        pltpu.VMEM((2, 2, 48, 128), F32),
        pltpu.VMEM((4, 48, 128), F32),
        pltpu.VMEM((4, 48, 128), F32),
        pltpu.VMEM((3, 3, 48, 128), F32),
        pltpu.VMEM((2, 24, HALF), F32),
        pltpu.VMEM((4, 4, 40, LANES), F32),
        pltpu.VMEM((3, 8, 8, 128), F32),
        dma((3,)),
        dma((18,)),
        dma((1,)),
        dma((3 + GROUPS, 4)),
        dma((3 + GROUPS, 4)),
        dma((GROUPS,)),
        dma((GROUPS,)),
        dma((WINDOWS,)),
        dma((WINDOWS,)),
        dma((3, 3, 6)),
        dma((3, 3, 6)),
        dma((4, 3)),
        dma((4, 3)),
        dma((3, 7)),
        dma((3, 7)),
        dma((GROUPS,)),
        dma((2,)),
    ]
    results = pl.pallas_call(
        sublayer,
        out_shape=(
            jax.ShapeDtypeStruct((16, 16, D), BF),
            jax.ShapeDtypeStruct((16, 16, D), BF),
            jax.ShapeDtypeStruct((12, D), F32),
            jax.ShapeDtypeStruct((15, 15, HEADS), F32),
            jax.ShapeDtypeStruct((D,), F32),
            jax.ShapeDtypeStruct((D,), F32),
        ),
        in_specs=[anywhere, anywhere, vmem, anywhere, vmem, vmem, anywhere],
        out_specs=(anywhere, anywhere, vmem, vmem, vmem, vmem),
        scratch_shapes=scratch,
        compiler_params=pltpu.CompilerParams(
            collective_id=0, has_side_effects=True, vmem_limit_bytes=60 * 2**20
        ),
        name="sublayer",
    )(
        tokens, qkv_weight, rel_bias.transpose(1, 2, 0), proj_weight, norm_gain, norm_shift, cotangent,
    )
    out, d_tokens, d_proj, d_rel, d_gain, d_shift = pl.pallas_call(
        hand_over,
        out_shape=tuple(jax.ShapeDtypeStruct(r.shape, r.dtype) for r in results),
        in_specs=[anywhere] * 6,
        out_specs=(anywhere,) * 6,
        scratch_shapes=[pltpu.VMEM(r.shape, r.dtype) for r in results] + [dma((6,)), dma((6,))],
        compiler_params=pltpu.CompilerParams(vmem_limit_bytes=60 * 2**20),
        name="hand_over",
    )(*results)
    return out, d_tokens, d_proj, d_rel.transpose(2, 0, 1), d_gain, d_shift


def solution(mesh):
    in_specs = (P("lat", "lon", None), P(), P(), P(), P(), P(), P("lat", "lon", None))
    out_specs = (
        P("lat", "lon", None),
        P("lat", "lon", None),
        P(("lon", "lat"), None),
        P(),
        P(),
        P(),
    )
    return jax.shard_map(
        on_device, mesh=mesh, in_specs=in_specs, out_specs=out_specs, check_vma=False
    )
```

```python
import functools

import jax
import jax.numpy as jnp
from jax import lax
from jax.experimental import pallas as pl
from jax.experimental.pallas import tpu as pltpu
from jax.sharding import PartitionSpec as P

F32 = jnp.float32
BF = jnp.bfloat16
MESH = pl.DeviceIdType.MESH

D = 1536
HEADS = 24
GROUPS = 6
LANES = 256
TOKENS = 256
CELLS = 64
WINDOWS = 4
HALF = 768
PARAMS = 2367768
norm_epsilon = 1e-05
clip_epsilon = 1e-06

ORDERS = (("x", "y", "z"), ("y", "z", "x"), ("z", "x", "y"))


def dot(a, b, ca, cb):
    return lax.dot_general(a, b, (((ca,), (cb,)), ((), ())), preferred_element_type=F32)


def dot_exact(a, b, ca, cb):
    total = None
    for _ in range(3):
        part = a.astype(BF)
        a = a - part.astype(F32)
        term = dot(part, b, ca, cb)
        total = term if total is None else total + term
    return total


def stack(*pieces):
    return jnp.concatenate(pieces, axis=0)


def turn(value):
    return pltpu.roll(value, 4, 0)


def low_rows(columns):
    return lax.broadcasted_iota(jnp.int32, (8, columns), 0) < 4


def halves(ref, rows, cols):
    both = ref[rows, cols].astype(F32)
    return both[:8], both[8:]


def row_halves(block, row, cols):
    both = block[row, :, cols].astype(F32)
    return both[:8], both[8:]


def columns_of(step, width=LANES):
    return pl.ds(pl.multiple_of(step * width, width), width)


def pack_first(a, b):
    return jnp.where(low_rows(a.shape[1]), a, turn(b))


def pack_last(a, b):
    return jnp.where(low_rows(a.shape[1]), turn(a), b)


def four_pairs(pack, values):
    return stack(pack(values[0], values[1]), pack(values[2], values[3])).astype(BF)


STRIPS = (slice(0, 32), slice(32, 48), slice(48, 96), slice(96, 112))
STRIP_STEPS = ((0, 1), (0, -1), (1, 0), (1, -1))


def input_strips(block, strips, cols, low):
    for k in range(2):
        rows = [row_halves(block, 4 + 4 * k + i, cols)[0] for i in range(4)]
        strips[16 * k : 16 * k + 16, cols] = four_pairs(pack_first, rows)
    rows = [row_halves(block, 12 + i, cols)[1] for i in range(4)]
    strips[32:48, cols] = four_pairs(pack_last, rows)
    t = [row_halves(block, r, cols) for r in range(4)]
    wide = [turn(jnp.where(low, t1, t0)) for t0, t1 in t]
    strips[48:64, cols] = stack(wide[0], wide[1]).astype(BF)
    strips[64:80, cols] = stack(wide[2], wide[3]).astype(BF)
    strips[80:96, cols] = four_pairs(pack_first, [t0 for t0, _ in t])
    strips[96:112, cols] = four_pairs(pack_last, [t1 for _, t1 in t])


def own_windows(block, flat, cols, low):
    for r, at in ((4, 0), (6, 16), (8, 32), (10, 48), (12, 192), (14, 208)):
        t0, t1 = row_halves(block, r, cols)
        u0, u1 = row_halves(block, r + 1, cols)
        flat[at : at + 16, cols] = stack(
            turn(jnp.where(low, t1, t0)), turn(jnp.where(low, u1, u0))
        ).astype(BF)


def input_windows(block, came, flat, cols, low):
    for k in range(2):
        pairs = halves(came, slice(16 * k, 16 * k + 16), cols)
        for i in range(2):
            r = 4 * k + 2 * i
            s = pairs[i]
            t1 = row_halves(block, r + 4, cols)[1]
            u1 = row_halves(block, r + 5, cols)[1]
            flat[64 + 8 * r : 80 + 8 * r, cols] = stack(
                jnp.where(low, turn(t1), turn(s)), jnp.where(low, turn(u1), s)
            ).astype(BF)
    west = halves(came, slice(32, 48), cols)
    side = halves(came, slice(80, 96), cols)
    corner = halves(came, slice(96, 112), cols)
    for i in range(2):
        t0 = row_halves(block, 12 + 2 * i, cols)[0]
        u0 = row_halves(block, 13 + 2 * i, cols)[0]
        s = west[i]
        flat[128 + 16 * i : 144 + 16 * i, cols] = stack(
            jnp.where(low, s, turn(t0)), jnp.where(low, turn(s), turn(u0))
        ).astype(BF)
        s, d = side[i], corner[i]
        flat[160 + 16 * i : 176 + 16 * i, cols] = stack(
            jnp.where(low, d, turn(s)), jnp.where(low, turn(d), s)
        ).astype(BF)
        flat[224 + 16 * i : 240 + 16 * i, cols] = came[48 + 16 * i : 64 + 16 * i, cols]


def output_strips(flat, strips, cols):
    def rows_of(start):
        return [flat[start + 8 * i : start + 8 * i + 8, cols] for i in range(4)]

    for k in range(2):
        strips[16 * k : 16 * k + 16, cols] = four_pairs(pack_last, rows_of(64 + 32 * k))
    strips[32:48, cols] = four_pairs(pack_first, rows_of(128))
    strips[48:80, cols] = flat[224:256, cols].astype(BF)
    strips[80:96, cols] = four_pairs(pack_last, rows_of(160))
    strips[96:112, cols] = four_pairs(pack_first, rows_of(160))


def output_block(flat, came, block, cols, low):
    for k in range(2):
        pairs = halves(came, slice(16 * k, 16 * k + 16), cols)
        for i in range(4):
            r = 4 * k + i
            s = pairs[i // 2]
            s = s if i % 2 == 0 else turn(s)
            a = turn(flat[8 * r : 8 * r + 8, cols])
            b = turn(flat[64 + 8 * r : 72 + 8 * r, cols])
            block[r + 4, :, cols] = stack(jnp.where(low, s, a), jnp.where(low, a, b)).astype(BF)
    east = halves(came, slice(32, 48), cols)
    side = halves(came, slice(80, 96), cols)
    corner = halves(came, slice(96, 112), cols)
    for i in range(2):
        wides = halves(came, slice(48 + 16 * i, 64 + 16 * i), cols)
        for k in range(2):
            r = 2 * i + k
            a = turn(flat[128 + 8 * r : 136 + 8 * r, cols])
            b = turn(flat[192 + 8 * r : 200 + 8 * r, cols])
            s = turn(east[i]) if k == 0 else east[i]
            block[12 + r, :, cols] = stack(jnp.where(low, a, b), jnp.where(low, b, s)).astype(BF)
            wide = turn(wides[k])
            at_low = side[i] if k == 0 else turn(side[i])
            at_high = turn(corner[i]) if k == 0 else corner[i]
            block[r, :, cols] = stack(
                jnp.where(low, at_low, wide), jnp.where(low, wide, at_high)
            ).astype(BF)


def block_diagonal(value, lane_head):
    zero = jnp.zeros_like(value)
    return stack(*[jnp.where(lane_head == h, value, zero) for h in range(4)])


def diagonal(product, left):
    tiles = []
    for t in range(2):
        cols = slice(128 * t, 128 * t + 128)
        tiles.append(
            jnp.where(
                left,
                product[128 * t : 128 * t + 64, cols],
                product[128 * t + 64 : 128 * t + 128, cols],
            )
        )
    return jnp.concatenate(tiles, axis=1)


def sublayer(
    tok_h, wq_h, rel_h, pw_h, gain_h, shift_h, cot_h,
    out_h, dtok_h, dpw_ref, drel_ref, dgain_ref, dshift_ref,
    tok_v, cot_v, w_v, pw_v, x_v, c_v, qkv_v, pt_v, mix_v, mixt_v, proj_v, flat_v, dflat_v,
    dp_v, dps_v, dmix_v, dqkv_v, oblk_v, dblk_v,
    rel_ref, gain_ref, shift_ref, e_v, rel_v, gain_v, shift_v, wb_v, bt_v, mask_v, u_v, acc_v,
    send_x, came_x, send_c, came_c, send_o, came_o, send_d, came_d,
    p_v, r1a, r1c, s2a, s2b, s2c, r2a, r2b, r2c, s3a, s3b, s3c, r3, fin_v,
    sm_v, sq_v,
    load_sem, w_sem, store_sem, halo_send, halo_recv, mix_sem, dp_sem,
    rs_send, rs_recv, sm_send, sm_recv, sq_send, sq_recv, fin_sem,
):
    lon = lax.axis_index("lon")
    lat = lax.axis_index("lat")
    core = lax.rem(lat, 2)
    at = {
        "x": lax.rem(lon // 4, 4),
        "y": lax.rem(lon, 4),
        "z": (lon // 16) * 2 + lat // 2,
    }

    def device(chip, on_core):
        z = chip["z"]
        return {
            "lon": (z // 2) * 16 + chip["x"] * 4 + chip["y"],
            "lat": lax.rem(z, 2) * 2 + on_core,
        }

    def along(axis, steps, on_core=core):
        chip = dict(at)
        chip[axis] = lax.rem(at[axis] + steps, 4)
        return device(chip, on_core)

    sibling = device(at, 1 - core)

    def shifted(lat_steps, lon_steps):
        return {
            "lon": lax.rem(lon + lon_steps + 32, 32),
            "lat": lax.rem(lat + lat_steps + 4, 4),
        }

    def remote(src, dst, send, recv, target):
        return pltpu.make_async_remote_copy(
            src_ref=src, dst_ref=dst, send_sem=send, recv_sem=recv,
            device_id=target, device_id_type=MESH,
        )

    def arrive(whole, send, recv):
        group = remote(whole, whole, send, recv, sibling)
        group.wait_send()
        group.wait_recv()

    load_tok = pltpu.make_async_copy(tok_h, tok_v, load_sem.at[0])
    load_cot = pltpu.make_async_copy(cot_h, cot_v, load_sem.at[1])
    load_pw = pltpu.make_async_copy(pw_h, pw_v, load_sem.at[2])

    def load_w(chunk):
        cols = columns_of(chunk)
        return pltpu.make_async_copy(wq_h.at[:, cols], w_v.at[:, cols], w_sem.at[lax.rem(chunk, GROUPS)])

    load_tok.start()
    load_cot.start()
    loads = [
        pltpu.make_async_copy(rel_h, rel_ref, load_sem.at[3]),
        pltpu.make_async_copy(gain_h, gain_ref, load_sem.at[4]),
        pltpu.make_async_copy(shift_h, shift_ref, load_sem.at[5]),
    ]
    for load in loads:
        load.start()

    partners = [shifted(0, 1), shifted(0, -1), shifted(1, 0), shifted(-1, 0), shifted(1, -1), shifted(-1, 1)]
    circles = [[], []]
    for k in range(1, 16):
        chip = dict(at)
        chip["x"] = lax.rem(at["x"] + k // 4, 4)
        chip["y"] = lax.rem(at["y"] + k % 4, 4)
        circles[0].append(device(chip, core))
    circles[1] += [sibling] + [along("z", steps) for steps in (1, 2, 3)]
    circles[1] += [along("z", steps, 1 - core) for steps in (1, 2, 3)]
    partners += circles[0] + circles[1]
    barrier = pltpu.get_barrier_semaphore()
    for partner in partners:
        pl.semaphore_signal(barrier, inc=1, device_id=partner, device_id_type=MESH)

    for g in range(GROUPS):
        for part in range(3):
            load_w(part * GROUPS + g).start()
    load_pw.start()

    low = low_rows(LANES)

    def each_column(body):
        lax.fori_loop(0, GROUPS, lambda n, _: (body(columns_of(n)), 0)[1], 0)

    def halo(strips, came, which, sign, cols=slice(None)):
        return [
            remote(
                strips.at[rows, cols], came.at[rows, cols],
                halo_send.at[which], halo_recv.at[which],
                shifted(sign * STRIP_STEPS[i][0], sign * STRIP_STEPS[i][1]),
            )
            for i, rows in enumerate(STRIPS)
        ]

    load_tok.wait()
    each_column(lambda cols: input_strips(tok_v, send_x, cols, low))
    pl.semaphore_wait(barrier, len(partners))
    halo_x = halo(send_x, came_x, 0, -1)
    for copy in halo_x:
        copy.start()
    each_column(lambda cols: own_windows(tok_v, x_v, cols, low))
    load_cot.wait()
    each_column(lambda cols: input_strips(cot_v, send_c, cols, low))
    halo_c = halo(send_c, came_c, 1, -1)

    spot = lax.broadcasted_iota(jnp.int32, (128, LANES), 0)
    slot = lax.broadcasted_iota(jnp.int32, (128, LANES), 1)
    for cj in range(8):
        hit = ((spot >> 3) == (slot >> 4)) & ((spot & 7) - cj + 7 == (slot & 15))
        e_v[128 * cj : 128 * cj + 128, :] = jnp.where(hit, 1.0, 0.0).astype(BF)
    for load in loads:
        load.wait()
    rel_v[...] = jnp.zeros_like(rel_v)
    for a in range(15):
        rel_v[16 * a : 16 * a + 15, :] = rel_ref[a]
    rel = rel_v[...]
    for cj in range(8):
        wb_v[:, cj, :] = dot_exact(rel, e_v[128 * cj : 128 * cj + 128, :], 0, 1)
    left8 = lax.broadcasted_iota(jnp.int32, (8, 128), 1) < 64

    def bias_step(g, _):
        for t in range(2):
            first = wb_v[g * 4 + 2 * t]
            second = wb_v[g * 4 + 2 * t + 1]
            for rj in range(8):
                shift = (7 - rj) * 8
                bt_v[g, 8 * rj : 8 * rj + 8, 128 * t : 128 * t + 128] = jnp.where(
                    left8,
                    pltpu.roll(first, (128 - shift) % 128, 1),
                    pltpu.roll(second, (192 - shift) % 128, 1),
                )
        return 0

    lax.fori_loop(0, GROUPS, bias_step, 0)
    j_upper = lax.broadcasted_iota(jnp.int32, (CELLS, LANES), 0) < 32
    i_upper = (lax.broadcasted_iota(jnp.int32, (CELLS, LANES), 1) & 63) < 32
    crossing = (j_upper != i_upper) & (lat == 3)
    mask_v[...] = jnp.where(crossing, -jnp.inf, 0.0)

    arrive(came_x, halo_send.at[0], halo_recv.at[0])
    for copy in halo_c:
        copy.start()
    each_column(lambda cols: input_windows(tok_v, came_x, x_v, cols, low))

    lane_head = lax.broadcasted_iota(jnp.int32, (CELLS, LANES), 1) >> 6
    left = lax.broadcasted_iota(jnp.int32, (CELLS, 128), 1) < 64

    def mix_copy(g):
        rows = columns_of(g)
        return remote(
            mixt_v.at[0, rows], mixt_v.at[1, rows], mix_sem.at[0], mix_sem.at[1], sibling
        )

    def make_qkv(g):
        for part in range(3):
            chunk = part * GROUPS + g
            value = dot(x_v[...], w_v[:, columns_of(chunk)], 1, 0).astype(BF)
            if part == 0:
                value = value * jnp.asarray(0.125, BF)
            qkv_v[chunk] = value

    def wait_weights(g):
        three = w_v.at[:, : 3 * LANES]
        pltpu.make_async_copy(three, three, w_sem.at[g]).wait()

    def attend(g):
        bias = bt_v[g]
        masked = bias + mask_v[...]
        mixed = []
        for w in range(WINDOWS):
            rows = slice(CELLS * w, CELLS * w + CELLS)
            q, k, v = [qkv_v[part * GROUPS + g, rows, :] for part in range(3)]
            scores = dot(k, block_diagonal(q, lane_head), 1, 1) + (bias if w < 2 else masked)
            peak = jnp.max(scores, axis=0, keepdims=True)
            raised = jnp.exp(scores - peak)
            shares = raised * (1.0 / jnp.sum(raised, axis=0, keepdims=True))
            pt_v[g, w] = shares
            mixed.append(diagonal(dot(shares.astype(BF), v, 0, 0), left).astype(BF))
        mixed = stack(*mixed)
        mix_v[:, columns_of(g)] = mixed
        mixt_v[0, columns_of(g), :] = mixed.T

    def forward_step(g, _):
        wait_weights(g + 1)
        attend(g)
        make_qkv(g + 1)
        mix_copy(g).start()
        return 0

    wait_weights(0)
    make_qkv(0)
    lax.fori_loop(0, GROUPS - 1, forward_step, 0)
    attend(GROUPS - 1)
    mix_copy(GROUPS - 1).start()

    def project_step(n, _):
        cols = columns_of(n)
        proj_v[:, cols] = dot(mix_v[...], pw_v[:, cols], 1, 0)
        return 0

    load_pw.wait()
    lax.fori_loop(0, GROUPS, project_step, 0)

    each_column(lambda cols: own_windows(cot_v, c_v, cols, low))
    arrive(came_c, halo_send.at[1], halo_recv.at[1])
    each_column(lambda cols: input_windows(cot_v, came_c, c_v, cols, low))

    acc_v[...] = jnp.zeros_like(acc_v)
    gain = gain_ref[...].reshape(1, D)
    shift = shift_ref[...].reshape(1, D)
    gain_v[...] = gain
    shift_v[...] = shift

    other_half = pl.ds(pl.multiple_of((1 - core) * HALF, HALF), HALF)

    def dp_copy(m):
        rows = pl.ds(pl.multiple_of(m * CELLS, CELLS), CELLS)
        return remote(dp_v.at[rows, other_half], dps_v.at[rows], dp_sem.at[0], dp_sem.at[1], sibling)

    def norm_step(m, _):
        sums = [None, None]
        for part in range(4):
            rows = pl.ds(pl.multiple_of(m * CELLS + 16 * part, 16), 16)
            projected = proj_v[rows, :]
            centre = projected - jnp.mean(projected, axis=1, keepdims=True)
            inverse = lax.rsqrt(jnp.mean(centre * centre, axis=1, keepdims=True) + norm_epsilon)
            normed = centre * inverse
            flat_v[rows, :] = x_v[rows, :].astype(F32) + normed * gain_v[...] + shift_v[...]
            upstream = c_v[rows, :].astype(F32)
            product = upstream * normed
            terms = (product[:8] + product[8:], upstream[:8] + upstream[8:])
            sums = [b if a is None else a + b for a, b in zip(sums, terms)]
            d_normed = upstream * gain_v[...]
            inner = d_normed - jnp.mean(d_normed, axis=1, keepdims=True)
            inner = inner - normed * jnp.mean(d_normed * normed, axis=1, keepdims=True)
            dp_v[rows, :] = (inverse * inner).astype(BF)
        acc_v[0] += sums[0]
        acc_v[1] += sums[1]
        dp_copy(m).start()
        return 0

    lax.fori_loop(0, TOKENS // CELLS, norm_step, 0)

    each_column(lambda cols: output_strips(flat_v, send_o, cols))
    for copy in halo(send_o, came_o, 2, 1):
        copy.start()

    arrive(dps_v, dp_sem.at[0], dp_sem.at[1])
    arrive(mixt_v.at[1], mix_sem.at[0], mix_sem.at[1])

    def slot_of(buffer, lead, axes, axis, index):
        if axis == "z":
            places = {"h": index // 2, "l": lax.rem(index, 2)}
        else:
            places = {axis: index}
        return buffer.at[lead + tuple(places.get(name, slice(None)) for name in axes)]

    stages = (
        ((p_v, (0,), "hxyl"), (p_v, (1,), "hxyl"), (p_v, (2,), "hxyl")),
        ((s2a, (), "hyl"), (s2b, (), "hxl"), (s2c, (), "xy")),
        ((s3a, (), "hl"), (s3b, (), "x"), (s3c, (), "y")),
    )
    arrivals = (
        (r1a.at[0], r1a.at[1], r1c),
        (r2a, r2b, r2c),
        (r3.at[0], r3.at[1], r3.at[2]),
    )

    pieces = (slice(0, 32), slice(32, 48), slice(0, 48))

    def scatter_copies(stage, part, piece):
        buffer, lead, axes = stages[stage][part]
        axis = ORDERS[part][stage]
        rows = pieces[piece]
        whole = (slice(None),) * (len(axes) - (2 if axis == "z" else 1))
        copies = []
        for steps in (1, 2, 3):
            index = lax.rem(at[axis] + steps, 4)
            copies.append(
                remote(
                    slot_of(buffer, lead, axes, axis, index).at[whole + (rows,)],
                    arrivals[stage][part].at[(steps - 1,) + whole + (rows,)],
                    rs_send.at[stage, part, piece % 2],
                    rs_recv.at[stage, part, piece % 2],
                    along(axis, steps),
                )
            )
        return copies

    def scatter_start(stage, part, piece):
        for copy in scatter_copies(stage, part, piece):
            copy.start()

    def scatter_sum(stage, part, piece):
        buffer, lead, axes = stages[stage][part]
        axis = ORDERS[part][stage]
        rows = pieces[piece]
        whole = (slice(None),) * (len(axes) - (2 if axis == "z" else 1))
        arrive(
            arrivals[stage][part].at[(slice(None),) + whole + (rows,)],
            rs_send.at[stage, part, piece % 2], rs_recv.at[stage, part, piece % 2],
        )
        total = slot_of(buffer, lead, axes, axis, at[axis])[whole + (rows,)].astype(F32)
        for steps in range(3):
            total = total + arrivals[stage][part][(steps,) + whole + (rows,)].astype(F32)
        if stage < 2:
            target = stages[stage + 1][part][0]
            target[whole + (rows,)] = total.astype(target.dtype)
            if stage == 0:
                scatter_start(1, part, piece)
            elif piece == 1:
                scatter_start(2, part, 2)
        else:
            fin_v[0, :, LANES * part : LANES * part + 128] = total[:24]
            fin_v[0, :, LANES * part + 128 : LANES * part + 256] = total[24:]

    def scatter_sums(stage, piece):
        for part in range(3):
            scatter_sum(stage, part, piece)

    for part in range(3):
        own = dp_v[:, pl.ds(pl.multiple_of(core * HALF + part * LANES, LANES), LANES)]
        other = dps_v[:, LANES * part : LANES * part + LANES]
        for mb in range(4):
            rows = slice(384 * mb, 384 * mb + 384)
            value = dot(mixt_v[0, rows, :], own, 1, 0) + dot(mixt_v[1, rows, :], other, 1, 0)
            value = jnp.concatenate(
                [value[:, :128].reshape(16, 24, 128), value[:, 128:].reshape(16, 24, 128)], axis=1
            )
            p_v[part, mb // 2, 2 * (mb % 2) : 2 * (mb % 2) + 2] = value.astype(BF).reshape(
                2, 4, 2, 48, 128
            )
        scatter_start(0, part, 0)
    for part in range(3):
        scatter_start(0, part, 1)

    def make_d_mixed(g):
        dmix_v[g] = dot(dp_v[...], pw_v[columns_of(g), :], 1, 1).astype(BF)

    def backward(g):
        total = None
        for w in range(WINDOWS):
            rows = slice(CELLS * w, CELLS * w + CELLS)
            q, k, v = [qkv_v[part * GROUPS + g, rows, :] for part in range(3)]
            d_out = block_diagonal(dmix_v[g, rows, :], lane_head)
            shares = pt_v[g, w]
            d_shares = dot(v, d_out, 1, 1)
            d_scores = shares * (d_shares - jnp.sum(shares * d_shares, axis=0, keepdims=True))
            total = d_scores if total is None else total + d_scores
            low_scores = d_scores.astype(BF)
            dq = diagonal(dot(low_scores, k, 0, 0), left) * 0.125
            dk = dot(low_scores, block_diagonal(q, lane_head), 1, 0)
            dv = dot(shares.astype(BF), d_out, 1, 0)
            for part, value in enumerate((dq, dk, dv)):
                dqkv_v[rows, columns_of(part * GROUPS + g)] = value.astype(BF)
        for t in range(2):
            sums = [None, None]
            for rj in range(8):
                shift = (7 - rj) * 8
                piece = total[8 * rj : 8 * rj + 8, 128 * t : 128 * t + 128]
                pair = (
                    pltpu.roll(jnp.where(left8, piece, 0.0), shift, 1),
                    pltpu.roll(jnp.where(left8, 0.0, piece), shift + 64, 1),
                )
                sums = [b if a is None else a + b for a, b in zip(sums, pair)]
            u_v[g * 4 + 2 * t] = sums[0]
            u_v[g * 4 + 2 * t + 1] = sums[1]

    def backward_step(g, _):
        backward(g)
        make_d_mixed(g + 1)
        return 0

    make_d_mixed(0)
    lax.fori_loop(0, GROUPS - 1, backward_step, 0)
    backward(GROUPS - 1)

    scatter_sums(0, 0)
    scatter_sums(0, 1)

    small = None
    for cj in range(8):
        term = dot_exact(u_v[:, cj, :], e_v[128 * cj : 128 * cj + 128, :], 1, 0)
        small = term if small is None else small + term
    gain_sum = jnp.sum(acc_v[0], axis=0, keepdims=True)
    shift_sum = jnp.sum(acc_v[1], axis=0, keepdims=True)
    zero2 = jnp.zeros((2, LANES), F32)
    small = stack(
        small,
        *[gain_sum[:, LANES * n : LANES * n + LANES] for n in range(GROUPS)], zero2,
        *[shift_sum[:, LANES * n : LANES * n + LANES] for n in range(GROUPS)], zero2,
    )

    def sum_copies(buffer, send, recv, stage):
        if stage == 0:
            return [remote(
                buffer.at[0, core], buffer.at[0, core], send.at[0], recv.at[0], sibling
            )]
        axis = "xyz"[stage - 1]
        return [
            remote(
                buffer.at[stage, at[axis]], buffer.at[stage, at[axis]],
                send.at[stage], recv.at[stage], along(axis, steps),
            )
            for steps in (1, 2, 3)
        ]

    def sum_start(buffer, send, recv, stage, value):
        place = core if stage == 0 else at["xyz"[stage - 1]]
        buffer[stage, place] = value
        for copy in sum_copies(buffer, send, recv, stage):
            copy.start()

    def sum_finish(buffer, send, recv, stage):
        arrive(buffer.at[stage, slice(0, 1 if stage == 0 else 3)], send.at[stage], recv.at[stage])
        total = buffer[stage, 0] + buffer[stage, 1]
        if stage > 0:
            total = total + buffer[stage, 2] + buffer[stage, 3]
        return total

    sum_start(sm_v, sm_send, sm_recv, 0, small)

    def squares_place(stage):
        return (at["x"] * 4 + at["y"], at["z"] * 2 + core)[stage]

    def squares_copies(stage):
        mine = sq_v.at[stage, squares_place(stage)]
        return [
            remote(mine, mine, sq_send.at[stage], sq_recv.at[stage], target)
            for target in circles[stage]
        ]

    def squares_start(stage, value):
        sq_v[stage, squares_place(stage)] = value
        for copy in squares_copies(stage):
            copy.start()

    def squares_finish(stage):
        count = (16, 8)[stage]
        arrive(sq_v.at[stage, slice(0, count - 1)], sq_send.at[stage], sq_recv.at[stage])
        total = sq_v[stage, 0]
        for k in range(1, count):
            total = total + sq_v[stage, k]
        return total

    def halo_d(n):
        return halo(send_d, came_d, 3 + n, 1, columns_of(n))

    def store_d(n):
        cols = columns_of(n)
        return pltpu.make_async_copy(dblk_v.at[:, :, cols], dtok_h.at[:, :, cols], store_sem.at[1])

    def last_step(n, _):
        arrive(came_d.at[:, columns_of(n)], halo_send.at[3 + n], halo_recv.at[3 + n])
        output_block(dflat_v, came_d, dblk_v, columns_of(n), low)
        store_d(n).start()
        return 0

    def d_token_step(n, _):
        cols = columns_of(n)
        dflat_v[:, cols] = c_v[:, cols].astype(F32) + dot(dqkv_v[...], w_v[cols, :], 1, 1)
        output_strips(dflat_v, send_d, cols)
        for copy in halo_d(n):
            copy.start()
        return 0

    lax.fori_loop(0, 1, d_token_step, 0)
    scatter_sums(1, 0)
    scatter_sums(1, 1)
    sum_start(sm_v, sm_send, sm_recv, 1, sum_finish(sm_v, sm_send, sm_recv, 0))
    lax.fori_loop(1, 4, d_token_step, 0)
    scatter_sums(2, 2)
    fin_copy = remote(fin_v.at[0], fin_v.at[1], fin_sem.at[0], fin_sem.at[1], sibling)
    fin_copy.start()
    squares = fin_v[0] * fin_v[0]
    squares = squares[:8] + squares[8:16] + squares[16:]
    squares = sum(squares[:, 128 * n : 128 * n + 128] for n in range(6))
    squares_start(0, squares)
    sum_start(sm_v, sm_send, sm_recv, 2, sum_finish(sm_v, sm_send, sm_recv, 1))
    lax.fori_loop(4, 6, d_token_step, 0)
    squares_start(1, squares_finish(0))
    sum_start(sm_v, sm_send, sm_recv, 3, sum_finish(sm_v, sm_send, sm_recv, 2))
    arrive(came_o, halo_send.at[2], halo_recv.at[2])
    each_column(lambda cols: output_block(flat_v, came_o, oblk_v, cols, low))
    store_out = pltpu.make_async_copy(oblk_v, out_h, store_sem.at[0])
    store_out.start()
    lax.fori_loop(0, GROUPS, last_step, 0)

    small = sum_finish(sm_v, sm_send, sm_recv, 3)
    squares = squares_finish(1)
    total = jnp.sum(squares, axis=(0, 1), keepdims=True)
    total = total + jnp.sum(small * small, axis=(0, 1), keepdims=True)
    factor = jnp.minimum(1.0, jnp.sqrt(PARAMS / (total + clip_epsilon)))
    drel = (small[:24] * factor).T
    for a in range(15):
        drel_ref[a] = drel[16 * a : 16 * a + 15]
    for n in range(GROUPS):
        dgain_ref[LANES * n : LANES * n + LANES] = (small[24 + n : 25 + n] * factor).reshape(LANES)
        dshift_ref[LANES * n : LANES * n + LANES] = (small[32 + n : 33 + n] * factor).reshape(LANES)
    fin_copy.wait()
    own, other = fin_v[0] * factor, fin_v[1] * factor
    own = jnp.where(core == 0, own[:12], own[12:])
    other = jnp.where(core == 0, other[:12], other[12:])
    dpw_ref[:, :HALF] = jnp.where(core == 0, own, other)
    dpw_ref[:, HALF:] = jnp.where(core == 0, other, own)
    store_out.wait()
    pltpu.make_async_copy(dblk_v, dtok_h, store_sem.at[1]).wait()


def hand_over(*refs):
    source, target, held, load_sem, store_sem = refs[:6], refs[6:12], refs[12:18], refs[18], refs[19]
    loads = [pltpu.make_async_copy(source[i], held[i], load_sem.at[i]) for i in range(6)]
    stores = [pltpu.make_async_copy(held[i], target[i], store_sem.at[i]) for i in range(6)]
    for load in loads:
        load.start()
    for load, store in zip(loads, stores):
        load.wait()
        store.start()
    for store in stores:
        store.wait()


def on_device(tokens, qkv_weight, rel_bias, proj_weight, norm_gain, norm_shift, cotangent):
    anywhere = pl.BlockSpec(memory_space=pl.ANY)
    vmem = pl.BlockSpec(memory_space=pltpu.VMEM)
    dma = pltpu.SemaphoreType.DMA
    strips = [pltpu.VMEM((112, D), BF)] * 8
    scratch = [
        pltpu.VMEM((16, 16, D), BF),
        pltpu.VMEM((16, 16, D), BF),
        pltpu.VMEM((D, 3 * D), BF),
        pltpu.VMEM((D, D), BF),
        pltpu.VMEM((TOKENS, D), BF),
        pltpu.VMEM((TOKENS, D), BF),
        pltpu.VMEM((18, TOKENS, LANES), BF),
        pltpu.VMEM((GROUPS, WINDOWS, CELLS, LANES), F32),
        pltpu.VMEM((TOKENS, D), BF),
        pltpu.VMEM((2, D, TOKENS), BF),
        pltpu.VMEM((TOKENS, D), F32),
        pltpu.VMEM((TOKENS, D), F32),
        pltpu.VMEM((TOKENS, D), F32),
        pltpu.VMEM((TOKENS, D), BF),
        pltpu.VMEM((TOKENS, HALF), BF),
        pltpu.VMEM((GROUPS, TOKENS, LANES), BF),
        pltpu.VMEM((TOKENS, 3 * D), BF),
        pltpu.VMEM((16, 16, D), BF),
        pltpu.VMEM((16, 16, D), BF),
        pltpu.VMEM((15, 15, HEADS), F32),
        pltpu.VMEM((D,), F32),
        pltpu.VMEM((D,), F32),
        pltpu.VMEM((1024, LANES), BF),
        pltpu.VMEM((LANES, HEADS), F32),
        pltpu.VMEM((1, D), F32),
        pltpu.VMEM((1, D), F32),
        pltpu.VMEM((HEADS, 8, 128), F32),
        pltpu.VMEM((GROUPS, CELLS, LANES), F32),
        pltpu.VMEM((CELLS, LANES), F32),
        pltpu.VMEM((HEADS, 8, 128), F32),
        pltpu.VMEM((2, 8, D), F32),
        *strips,
        pltpu.VMEM((3, 2, 4, 4, 2, 48, 128), BF),
        pltpu.VMEM((2, 3, 2, 4, 2, 48, 128), BF),
        pltpu.VMEM((3, 4, 4, 48, 128), BF),
        pltpu.VMEM((2, 4, 2, 48, 128), BF),
        pltpu.VMEM((2, 4, 2, 48, 128), BF),
        pltpu.VMEM((4, 4, 48, 128), BF),
        pltpu.VMEM((3, 2, 2, 48, 128), BF),
        pltpu.VMEM((3, 4, 48, 128), BF),
        pltpu.VMEM((3, 4, 48, 128), BF),
        pltpu.VMEM((2, 2, 48, 128), F32),
        pltpu.VMEM((4, 48, 128), F32),
        pltpu.VMEM((4, 48, 128), F32),
        pltpu.VMEM((3, 3, 48, 128), F32),
        pltpu.VMEM((2, 24, HALF), F32),
        pltpu.VMEM((4, 4, 40, LANES), F32),
        pltpu.VMEM((2, 16, 8, 128), F32),
        dma((6,)),
        dma((GROUPS,)),
        dma((2,)),
        dma((3 + GROUPS,)),
        dma((3 + GROUPS,)),
        dma((2,)),
        dma((2,)),
        dma((3, 3, 2)),
        dma((3, 3, 2)),
        dma((4,)),
        dma((4,)),
        dma((2,)),
        dma((2,)),
        dma((2,)),
    ]
    results = pl.pallas_call(
        sublayer,
        out_shape=(
            jax.ShapeDtypeStruct((16, 16, D), BF),
            jax.ShapeDtypeStruct((16, 16, D), BF),
            jax.ShapeDtypeStruct((12, D), F32),
            jax.ShapeDtypeStruct((15, 15, HEADS), F32),
            jax.ShapeDtypeStruct((D,), F32),
            jax.ShapeDtypeStruct((D,), F32),
        ),
        in_specs=[anywhere] * 7,
        out_specs=(anywhere, anywhere, vmem, vmem, vmem, vmem),
        scratch_shapes=scratch,
        compiler_params=pltpu.CompilerParams(
            collective_id=0, has_side_effects=True, vmem_limit_bytes=60 * 2**20
        ),
        name="sublayer",
    )(
        tokens, qkv_weight, rel_bias.transpose(1, 2, 0), proj_weight, norm_gain, norm_shift, cotangent,
    )
    out, d_tokens, d_proj, d_rel, d_gain, d_shift = pl.pallas_call(
        hand_over,
        out_shape=tuple(jax.ShapeDtypeStruct(r.shape, r.dtype) for r in results),
        in_specs=[anywhere] * 6,
        out_specs=(anywhere,) * 6,
        scratch_shapes=[pltpu.VMEM(r.shape, r.dtype) for r in results] + [dma((6,)), dma((6,))],
        compiler_params=pltpu.CompilerParams(vmem_limit_bytes=60 * 2**20),
        name="hand_over",
    )(*results)
    return out, d_tokens, d_proj, d_rel.transpose(2, 0, 1), d_gain, d_shift


def solution(mesh):
    in_specs = (P("lat", "lon", None), P(), P(), P(), P(), P(), P("lat", "lon", None))
    out_specs = (
        P("lat", "lon", None),
        P("lat", "lon", None),
        P(("lon", "lat"), None),
        P(),
        P(),
        P(),
    )
    return jax.shard_map(
        on_device, mesh=mesh, in_specs=in_specs, out_specs=out_specs, check_vma=False
    )
```

```python
import functools

import jax
import jax.numpy as jnp
from jax import lax
from jax.experimental import pallas as pl
from jax.experimental.pallas import tpu as pltpu
from jax.sharding import PartitionSpec as P

F32 = jnp.float32
BF = jnp.bfloat16
MESH = pl.DeviceIdType.MESH

D = 1536
HEADS = 24
GROUPS = 6
LANES = 256
TOKENS = 256
CELLS = 64
WINDOWS = 4
HALF = 768
PARAMS = 2367768
norm_epsilon = 1e-05
clip_epsilon = 1e-06

ORDERS = (("x", "y", "z"), ("y", "z", "x"), ("z", "x", "y"))


def dot(a, b, ca, cb):
    return lax.dot_general(a, b, (((ca,), (cb,)), ((), ())), preferred_element_type=F32)


def dot_exact(a, b, ca, cb):
    total = None
    for _ in range(3):
        part = a.astype(BF)
        a = a - part.astype(F32)
        term = dot(part, b, ca, cb)
        total = term if total is None else total + term
    return total


def stack(*pieces):
    return jnp.concatenate(pieces, axis=0)


def turn(value):
    return pltpu.roll(value, 4, 0)


def low_rows(columns):
    return lax.broadcasted_iota(jnp.int32, (8, columns), 0) < 4


def halves(ref, rows, cols):
    both = ref[rows, cols].astype(F32)
    return both[:8], both[8:]


def row_halves(block, row, cols):
    both = block[row, :, cols].astype(F32)
    return both[:8], both[8:]


def columns_of(step, width=LANES):
    return pl.ds(pl.multiple_of(step * width, width), width)


def pack_first(a, b):
    return jnp.where(low_rows(a.shape[1]), a, turn(b))


def pack_last(a, b):
    return jnp.where(low_rows(a.shape[1]), turn(a), b)


def four_pairs(pack, values):
    return stack(pack(values[0], values[1]), pack(values[2], values[3])).astype(BF)


STRIPS = (slice(0, 32), slice(32, 48), slice(48, 96), slice(96, 112))
STRIP_STEPS = ((0, 1), (0, -1), (1, 0), (1, -1))


def input_strips(block, strips, cols, low):
    for k in range(2):
        rows = [row_halves(block, 4 + 4 * k + i, cols)[0] for i in range(4)]
        strips[16 * k : 16 * k + 16, cols] = four_pairs(pack_first, rows)
    rows = [row_halves(block, 12 + i, cols)[1] for i in range(4)]
    strips[32:48, cols] = four_pairs(pack_last, rows)
    t = [row_halves(block, r, cols) for r in range(4)]
    wide = [turn(jnp.where(low, t1, t0)) for t0, t1 in t]
    strips[48:64, cols] = stack(wide[0], wide[1]).astype(BF)
    strips[64:80, cols] = stack(wide[2], wide[3]).astype(BF)
    strips[80:96, cols] = four_pairs(pack_first, [t0 for t0, _ in t])
    strips[96:112, cols] = four_pairs(pack_last, [t1 for _, t1 in t])


def own_windows(block, flat, cols, low):
    for r, at in ((4, 0), (6, 16), (8, 32), (10, 48), (12, 192), (14, 208)):
        t0, t1 = row_halves(block, r, cols)
        u0, u1 = row_halves(block, r + 1, cols)
        flat[at : at + 16, cols] = stack(
            turn(jnp.where(low, t1, t0)), turn(jnp.where(low, u1, u0))
        ).astype(BF)


def input_windows(block, came, flat, cols, low):
    for k in range(2):
        pairs = halves(came, slice(16 * k, 16 * k + 16), cols)
        for i in range(2):
            r = 4 * k + 2 * i
            s = pairs[i]
            t1 = row_halves(block, r + 4, cols)[1]
            u1 = row_halves(block, r + 5, cols)[1]
            flat[64 + 8 * r : 80 + 8 * r, cols] = stack(
                jnp.where(low, turn(t1), turn(s)), jnp.where(low, turn(u1), s)
            ).astype(BF)
    west = halves(came, slice(32, 48), cols)
    side = halves(came, slice(80, 96), cols)
    corner = halves(came, slice(96, 112), cols)
    for i in range(2):
        t0 = row_halves(block, 12 + 2 * i, cols)[0]
        u0 = row_halves(block, 13 + 2 * i, cols)[0]
        s = west[i]
        flat[128 + 16 * i : 144 + 16 * i, cols] = stack(
            jnp.where(low, s, turn(t0)), jnp.where(low, turn(s), turn(u0))
        ).astype(BF)
        s, d = side[i], corner[i]
        flat[160 + 16 * i : 176 + 16 * i, cols] = stack(
            jnp.where(low, d, turn(s)), jnp.where(low, turn(d), s)
        ).astype(BF)
        flat[224 + 16 * i : 240 + 16 * i, cols] = came[48 + 16 * i : 64 + 16 * i, cols]


def output_strips(flat, strips, cols):
    def rows_of(start):
        return [flat[start + 8 * i : start + 8 * i + 8, cols] for i in range(4)]

    for k in range(2):
        strips[16 * k : 16 * k + 16, cols] = four_pairs(pack_last, rows_of(64 + 32 * k))
    strips[32:48, cols] = four_pairs(pack_first, rows_of(128))
    strips[48:80, cols] = flat[224:256, cols].astype(BF)
    strips[80:96, cols] = four_pairs(pack_last, rows_of(160))
    strips[96:112, cols] = four_pairs(pack_first, rows_of(160))


def output_block(flat, came, block, cols, low):
    for k in range(2):
        pairs = halves(came, slice(16 * k, 16 * k + 16), cols)
        for i in range(4):
            r = 4 * k + i
            s = pairs[i // 2]
            s = s if i % 2 == 0 else turn(s)
            a = turn(flat[8 * r : 8 * r + 8, cols])
            b = turn(flat[64 + 8 * r : 72 + 8 * r, cols])
            block[r + 4, :, cols] = stack(jnp.where(low, s, a), jnp.where(low, a, b)).astype(BF)
    east = halves(came, slice(32, 48), cols)
    side = halves(came, slice(80, 96), cols)
    corner = halves(came, slice(96, 112), cols)
    for i in range(2):
        wides = halves(came, slice(48 + 16 * i, 64 + 16 * i), cols)
        for k in range(2):
            r = 2 * i + k
            a = turn(flat[128 + 8 * r : 136 + 8 * r, cols])
            b = turn(flat[192 + 8 * r : 200 + 8 * r, cols])
            s = turn(east[i]) if k == 0 else east[i]
            block[12 + r, :, cols] = stack(jnp.where(low, a, b), jnp.where(low, b, s)).astype(BF)
            wide = turn(wides[k])
            at_low = side[i] if k == 0 else turn(side[i])
            at_high = turn(corner[i]) if k == 0 else corner[i]
            block[r, :, cols] = stack(
                jnp.where(low, at_low, wide), jnp.where(low, wide, at_high)
            ).astype(BF)


def block_diagonal(value, lane_head):
    zero = jnp.zeros_like(value)
    return stack(*[jnp.where(lane_head == h, value, zero) for h in range(4)])


def diagonal(product, left):
    tiles = []
    for t in range(2):
        cols = slice(128 * t, 128 * t + 128)
        tiles.append(
            jnp.where(
                left,
                product[128 * t : 128 * t + 64, cols],
                product[128 * t + 64 : 128 * t + 128, cols],
            )
        )
    return jnp.concatenate(tiles, axis=1)


def sublayer(
    tok_h, wq_h, rel_h, pw_h, gain_h, shift_h, cot_h,
    out_h, dtok_h, dpw_ref, drel_ref, dgain_ref, dshift_ref,
    tok_v, cot_v, w_v, pw_v, x_v, c_v, qkv_v, pt_v, mix_v, mixt_v, proj_v, flat_v, dflat_v,
    dp_v, dps_v, dmix_v, dqkv_v, oblk_v, dblk_v,
    rel_ref, gain_ref, shift_ref, e_v, rel_v, gain_v, shift_v, wb_v, bt_v, mask_v, u_v, acc_v,
    send_x, came_x, send_c, came_c, send_o, came_o, send_d, came_d,
    p_v, r1a, r1c, s2a, s2b, s2c, r2a, r2b, r2c, s3a, s3b, s3c, r3, fin_v,
    sm_v, sq_v,
    load_sem, w_sem, store_sem, halo_send, halo_recv, mix_sem, dp_sem,
    rs_send, rs_recv, sm_send, sm_recv, sq_send, sq_recv, fin_sem,
):
    lon = lax.axis_index("lon")
    lat = lax.axis_index("lat")
    core = lax.rem(lat, 2)
    at = {
        "x": lax.rem(lon // 4, 4),
        "y": lax.rem(lon, 4),
        "z": (lon // 16) * 2 + lat // 2,
    }

    def device(chip, on_core):
        z = chip["z"]
        return {
            "lon": (z // 2) * 16 + chip["x"] * 4 + chip["y"],
            "lat": lax.rem(z, 2) * 2 + on_core,
        }

    def along(axis, steps, on_core=core):
        chip = dict(at)
        chip[axis] = lax.rem(at[axis] + steps, 4)
        return device(chip, on_core)

    sibling = device(at, 1 - core)

    def shifted(lat_steps, lon_steps):
        return {
            "lon": lax.rem(lon + lon_steps + 32, 32),
            "lat": lax.rem(lat + lat_steps + 4, 4),
        }

    def remote(src, dst, send, recv, target):
        return pltpu.make_async_remote_copy(
            src_ref=src, dst_ref=dst, send_sem=send, recv_sem=recv,
            device_id=target, device_id_type=MESH,
        )

    def arrive(whole, send, recv):
        group = remote(whole, whole, send, recv, sibling)
        group.wait_send()
        group.wait_recv()

    load_tok = pltpu.make_async_copy(tok_h, tok_v, load_sem.at[0])
    load_cot = pltpu.make_async_copy(cot_h, cot_v, load_sem.at[1])
    load_pw = pltpu.make_async_copy(pw_h, pw_v, load_sem.at[2])

    def load_w(g, part):
        source = wq_h.at[:, columns_of(part * GROUPS + g)]
        return pltpu.make_async_copy(source, w_v.at[:, columns_of(3 * g + part)], w_sem.at[g])

    load_tok.start()
    load_cot.start()
    loads = [
        pltpu.make_async_copy(rel_h, rel_ref, load_sem.at[3]),
        pltpu.make_async_copy(gain_h, gain_ref, load_sem.at[4]),
        pltpu.make_async_copy(shift_h, shift_ref, load_sem.at[5]),
    ]
    for load in loads:
        load.start()

    partners = [shifted(0, 1), shifted(0, -1), shifted(1, 0), shifted(-1, 0), shifted(1, -1), shifted(-1, 1)]
    circles = [[], []]
    for k in range(1, 16):
        chip = dict(at)
        chip["x"] = lax.rem(at["x"] + k // 4, 4)
        chip["y"] = lax.rem(at["y"] + k % 4, 4)
        circles[0].append(device(chip, core))
    circles[1] += [sibling] + [along("z", steps) for steps in (1, 2, 3)]
    circles[1] += [along("z", steps, 1 - core) for steps in (1, 2, 3)]
    partners += circles[0] + circles[1]
    barrier = pltpu.get_barrier_semaphore()
    for partner in partners:
        pl.semaphore_signal(barrier, inc=1, device_id=partner, device_id_type=MESH)

    for g in range(GROUPS):
        for part in range(3):
            load_w(g, part).start()
    load_pw.start()

    low = low_rows(LANES)

    def each_column(body):
        lax.fori_loop(0, GROUPS, lambda n, _: (body(columns_of(n)), 0)[1], 0)

    def halo(strips, came, which, sign, cols=slice(None)):
        return [
            remote(
                strips.at[rows, cols], came.at[rows, cols],
                halo_send.at[which], halo_recv.at[which],
                shifted(sign * STRIP_STEPS[i][0], sign * STRIP_STEPS[i][1]),
            )
            for i, rows in enumerate(STRIPS)
        ]

    load_tok.wait()
    each_column(lambda cols: input_strips(tok_v, send_x, cols, low))
    pl.semaphore_wait(barrier, len(partners))
    halo_x = halo(send_x, came_x, 0, -1)
    for copy in halo_x:
        copy.start()
    each_column(lambda cols: own_windows(tok_v, x_v, cols, low))
    load_cot.wait()
    each_column(lambda cols: input_strips(cot_v, send_c, cols, low))
    halo_c = halo(send_c, came_c, 1, -1)

    spot = lax.broadcasted_iota(jnp.int32, (128, LANES), 0)
    slot = lax.broadcasted_iota(jnp.int32, (128, LANES), 1)
    for cj in range(8):
        hit = ((spot >> 3) == (slot >> 4)) & ((spot & 7) - cj + 7 == (slot & 15))
        e_v[128 * cj : 128 * cj + 128, :] = jnp.where(hit, 1.0, 0.0).astype(BF)
    for load in loads:
        load.wait()
    rel_v[...] = jnp.zeros_like(rel_v)
    for a in range(15):
        rel_v[16 * a : 16 * a + 15, :] = rel_ref[a]
    rel = rel_v[...]
    for cj in range(8):
        wb_v[:, cj, :] = dot_exact(rel, e_v[128 * cj : 128 * cj + 128, :], 0, 1)
    left8 = lax.broadcasted_iota(jnp.int32, (8, 128), 1) < 64

    def bias_step(g, _):
        for t in range(2):
            first = wb_v[g * 4 + 2 * t]
            second = wb_v[g * 4 + 2 * t + 1]
            for rj in range(8):
                shift = (7 - rj) * 8
                bt_v[g, 8 * rj : 8 * rj + 8, 128 * t : 128 * t + 128] = jnp.where(
                    left8,
                    pltpu.roll(first, (128 - shift) % 128, 1),
                    pltpu.roll(second, (192 - shift) % 128, 1),
                )
        return 0

    lax.fori_loop(0, GROUPS, bias_step, 0)
    j_upper = lax.broadcasted_iota(jnp.int32, (CELLS, LANES), 0) < 32
    i_upper = (lax.broadcasted_iota(jnp.int32, (CELLS, LANES), 1) & 63) < 32
    crossing = (j_upper != i_upper) & (lat == 3)
    mask_v[...] = jnp.where(crossing, -jnp.inf, 0.0)

    arrive(came_x, halo_send.at[0], halo_recv.at[0])
    for copy in halo_c:
        copy.start()
    each_column(lambda cols: input_windows(tok_v, came_x, x_v, cols, low))

    lane_head = lax.broadcasted_iota(jnp.int32, (CELLS, LANES), 1) >> 6
    left = lax.broadcasted_iota(jnp.int32, (CELLS, 128), 1) < 64

    def mix_copy(g):
        rows = columns_of(g)
        return remote(
            mixt_v.at[0, rows], mixt_v.at[1, rows], mix_sem.at[0], mix_sem.at[1], sibling
        )

    def make_qkv(g):
        whole = dot(x_v[...], w_v[:, columns_of(g, HALF)], 1, 0).astype(BF)
        for part in range(3):
            value = whole[:, LANES * part : LANES * part + LANES]
            if part == 0:
                value = value * jnp.asarray(0.125, BF)
            qkv_v[part * GROUPS + g] = value

    def wait_weights(g):
        three = w_v.at[:, : 3 * LANES]
        pltpu.make_async_copy(three, three, w_sem.at[g]).wait()

    def attend(g):
        bias = bt_v[g]
        masked = bias + mask_v[...]
        mixed = []
        for w in range(WINDOWS):
            rows = slice(CELLS * w, CELLS * w + CELLS)
            q, k, v = [qkv_v[part * GROUPS + g, rows, :] for part in range(3)]
            scores = dot(k, block_diagonal(q, lane_head), 1, 1) + (bias if w < 2 else masked)
            peak = jnp.max(scores, axis=0, keepdims=True)
            raised = jnp.exp(scores - peak)
            shares = raised * (1.0 / jnp.sum(raised, axis=0, keepdims=True))
            pt_v[g, w] = shares
            mixed.append(diagonal(dot(shares.astype(BF), v, 0, 0), left).astype(BF))
        mixed = stack(*mixed)
        mix_v[:, columns_of(g)] = mixed
        mixt_v[0, columns_of(g), :] = mixed.T

    def forward_step(g, _):
        wait_weights(g + 1)
        attend(g)
        make_qkv(g + 1)
        mix_copy(g).start()
        return 0

    wait_weights(0)
    make_qkv(0)
    lax.fori_loop(0, GROUPS - 1, forward_step, 0)
    attend(GROUPS - 1)
    mix_copy(GROUPS - 1).start()

    def project_step(n, _):
        cols = columns_of(n, HALF)
        proj_v[:, cols] = dot(mix_v[...], pw_v[:, cols], 1, 0)
        return 0

    load_pw.wait()
    lax.fori_loop(0, 2, project_step, 0)

    each_column(lambda cols: own_windows(cot_v, c_v, cols, low))
    arrive(came_c, halo_send.at[1], halo_recv.at[1])
    each_column(lambda cols: input_windows(cot_v, came_c, c_v, cols, low))

    acc_v[...] = jnp.zeros_like(acc_v)
    gain = gain_ref[...].reshape(1, D)
    shift = shift_ref[...].reshape(1, D)
    gain_v[...] = gain
    shift_v[...] = shift

    other_half = pl.ds(pl.multiple_of((1 - core) * HALF, HALF), HALF)

    def dp_copy(m):
        rows = pl.ds(pl.multiple_of(m * CELLS, CELLS), CELLS)
        return remote(dp_v.at[rows, other_half], dps_v.at[rows], dp_sem.at[0], dp_sem.at[1], sibling)

    def norm_step(m, _):
        sums = [None, None]
        for part in range(4):
            rows = pl.ds(pl.multiple_of(m * CELLS + 16 * part, 16), 16)
            projected = proj_v[rows, :]
            centre = projected - jnp.mean(projected, axis=1, keepdims=True)
            inverse = lax.rsqrt(jnp.mean(centre * centre, axis=1, keepdims=True) + norm_epsilon)
            normed = centre * inverse
            flat_v[rows, :] = x_v[rows, :].astype(F32) + normed * gain_v[...] + shift_v[...]
            upstream = c_v[rows, :].astype(F32)
            product = upstream * normed
            terms = (product[:8] + product[8:], upstream[:8] + upstream[8:])
            sums = [b if a is None else a + b for a, b in zip(sums, terms)]
            d_normed = upstream * gain_v[...]
            inner = d_normed - jnp.mean(d_normed, axis=1, keepdims=True)
            inner = inner - normed * jnp.mean(d_normed * normed, axis=1, keepdims=True)
            dp_v[rows, :] = (inverse * inner).astype(BF)
        acc_v[0] += sums[0]
        acc_v[1] += sums[1]
        dp_copy(m).start()
        return 0

    lax.fori_loop(0, TOKENS // CELLS, norm_step, 0)

    each_column(lambda cols: output_strips(flat_v, send_o, cols))
    for copy in halo(send_o, came_o, 2, 1):
        copy.start()

    arrive(dps_v, dp_sem.at[0], dp_sem.at[1])
    arrive(mixt_v.at[1], mix_sem.at[0], mix_sem.at[1])

    def slot_of(buffer, lead, axes, axis, index):
        if axis == "z":
            places = {"h": index // 2, "l": lax.rem(index, 2)}
        else:
            places = {axis: index}
        return buffer.at[lead + tuple(places.get(name, slice(None)) for name in axes)]

    stages = (
        ((p_v, (0,), "hxyl"), (p_v, (1,), "hxyl"), (p_v, (2,), "hxyl")),
        ((s2a, (), "hyl"), (s2b, (), "hxl"), (s2c, (), "xy")),
        ((s3a, (), "hl"), (s3b, (), "x"), (s3c, (), "y")),
    )
    arrivals = (
        (r1a.at[0], r1a.at[1], r1c),
        (r2a, r2b, r2c),
        (r3.at[0], r3.at[1], r3.at[2]),
    )

    def scatter_copies(stage, part):
        buffer, lead, axes = stages[stage][part]
        axis = ORDERS[part][stage]
        copies = []
        for steps in (1, 2, 3):
            index = lax.rem(at[axis] + steps, 4)
            copies.append(
                remote(
                    slot_of(buffer, lead, axes, axis, index),
                    arrivals[stage][part].at[steps - 1],
                    rs_send.at[stage, part],
                    rs_recv.at[stage, part],
                    along(axis, steps),
                )
            )
        return copies

    def scatter_start(stage, part):
        for copy in scatter_copies(stage, part):
            copy.start()

    def scatter_sum(stage, part):
        buffer, lead, axes = stages[stage][part]
        axis = ORDERS[part][stage]
        came = arrivals[stage][part]
        arrive(came, rs_send.at[stage, part], rs_recv.at[stage, part])
        total = slot_of(buffer, lead, axes, axis, at[axis])[...].astype(F32)
        for steps in range(3):
            total = total + came[steps].astype(F32)
        if stage < 2:
            target = stages[stage + 1][part][0]
            target[...] = total.astype(target.dtype)
            scatter_start(stage + 1, part)
        else:
            fin_v[0, :, LANES * part : LANES * part + 128] = total[:24]
            fin_v[0, :, LANES * part + 128 : LANES * part + 256] = total[24:]

    def scatter_sums(stage):
        for part in range(3):
            scatter_sum(stage, part)

    for part in range(3):
        own = dp_v[:, pl.ds(pl.multiple_of(core * HALF + part * LANES, LANES), LANES)]
        other = dps_v[:, LANES * part : LANES * part + LANES]
        for mb in range(4):
            rows = slice(384 * mb, 384 * mb + 384)
            value = dot(mixt_v[0, rows, :], own, 1, 0) + dot(mixt_v[1, rows, :], other, 1, 0)
            value = jnp.concatenate(
                [value[:, :128].reshape(16, 24, 128), value[:, 128:].reshape(16, 24, 128)], axis=1
            )
            p_v[part, mb // 2, 2 * (mb % 2) : 2 * (mb % 2) + 2] = value.astype(BF).reshape(
                2, 4, 2, 48, 128
            )
        scatter_start(0, part)

    def make_d_mixed(g):
        dmix_v[g] = dot(dp_v[...], pw_v[columns_of(g), :], 1, 1).astype(BF)

    def backward(g):
        total = None
        for w in range(WINDOWS):
            rows = slice(CELLS * w, CELLS * w + CELLS)
            q, k, v = [qkv_v[part * GROUPS + g, rows, :] for part in range(3)]
            d_out = block_diagonal(dmix_v[g, rows, :], lane_head)
            shares = pt_v[g, w]
            d_shares = dot(v, d_out, 1, 1)
            d_scores = shares * (d_shares - jnp.sum(shares * d_shares, axis=0, keepdims=True))
            total = d_scores if total is None else total + d_scores
            low_scores = d_scores.astype(BF)
            dq = diagonal(dot(low_scores, k, 0, 0), left) * 0.125
            dk = dot(low_scores, block_diagonal(q, lane_head), 1, 0)
            dv = dot(shares.astype(BF), d_out, 1, 0)
            for part, value in enumerate((dq, dk, dv)):
                dqkv_v[rows, columns_of(3 * g + part)] = value.astype(BF)
        for t in range(2):
            sums = [None, None]
            for rj in range(8):
                shift = (7 - rj) * 8
                piece = total[8 * rj : 8 * rj + 8, 128 * t : 128 * t + 128]
                pair = (
                    pltpu.roll(jnp.where(left8, piece, 0.0), shift, 1),
                    pltpu.roll(jnp.where(left8, 0.0, piece), shift + 64, 1),
                )
                sums = [b if a is None else a + b for a, b in zip(sums, pair)]
            u_v[g * 4 + 2 * t] = sums[0]
            u_v[g * 4 + 2 * t + 1] = sums[1]

    def backward_step(g, _):
        backward(g)
        make_d_mixed(g + 1)
        return 0

    make_d_mixed(0)
    lax.fori_loop(0, GROUPS - 1, backward_step, 0)
    backward(GROUPS - 1)

    small = None
    for cj in range(8):
        term = dot_exact(u_v[:, cj, :], e_v[128 * cj : 128 * cj + 128, :], 1, 0)
        small = term if small is None else small + term
    gain_sum = jnp.sum(acc_v[0], axis=0, keepdims=True)
    shift_sum = jnp.sum(acc_v[1], axis=0, keepdims=True)
    zero2 = jnp.zeros((2, LANES), F32)
    small = stack(
        small,
        *[gain_sum[:, LANES * n : LANES * n + LANES] for n in range(GROUPS)], zero2,
        *[shift_sum[:, LANES * n : LANES * n + LANES] for n in range(GROUPS)], zero2,
    )

    def sum_copies(buffer, send, recv, stage):
        if stage == 0:
            return [remote(
                buffer.at[0, core], buffer.at[0, core], send.at[0], recv.at[0], sibling
            )]
        axis = "xyz"[stage - 1]
        return [
            remote(
                buffer.at[stage, at[axis]], buffer.at[stage, at[axis]],
                send.at[stage], recv.at[stage], along(axis, steps),
            )
            for steps in (1, 2, 3)
        ]

    def sum_start(buffer, send, recv, stage, value):
        place = core if stage == 0 else at["xyz"[stage - 1]]
        buffer[stage, place] = value
        for copy in sum_copies(buffer, send, recv, stage):
            copy.start()

    def sum_finish(buffer, send, recv, stage):
        arrive(buffer.at[stage, slice(0, 1 if stage == 0 else 3)], send.at[stage], recv.at[stage])
        total = buffer[stage, 0] + buffer[stage, 1]
        if stage > 0:
            total = total + buffer[stage, 2] + buffer[stage, 3]
        return total

    sum_start(sm_v, sm_send, sm_recv, 0, small)

    def squares_place(stage):
        return (at["x"] * 4 + at["y"], at["z"] * 2 + core)[stage]

    def squares_copies(stage):
        mine = sq_v.at[stage, squares_place(stage)]
        return [
            remote(mine, mine, sq_send.at[stage], sq_recv.at[stage], target)
            for target in circles[stage]
        ]

    def squares_start(stage, value):
        sq_v[stage, squares_place(stage)] = value
        for copy in squares_copies(stage):
            copy.start()

    def squares_finish(stage):
        count = (16, 8)[stage]
        arrive(sq_v.at[stage, slice(0, count - 1)], sq_send.at[stage], sq_recv.at[stage])
        total = sq_v[stage, 0]
        for k in range(1, count):
            total = total + sq_v[stage, k]
        return total

    def halo_d(n):
        return halo(send_d, came_d, 3 + n, 1, columns_of(n, 512))

    def store_d(n):
        cols = columns_of(n, 512)
        return pltpu.make_async_copy(dblk_v.at[:, :, cols], dtok_h.at[:, :, cols], store_sem.at[1])

    def last_step(n, _):
        arrive(came_d.at[:, columns_of(n, 512)], halo_send.at[3 + n], halo_recv.at[3 + n])
        output_block(dflat_v, came_d, dblk_v, columns_of(n, 512), low_rows(512))
        store_d(n).start()
        return 0

    def d_token_step(n, _):
        cols = columns_of(n, 512)
        dflat_v[:, cols] = c_v[:, cols].astype(F32) + dot(dqkv_v[...], w_v[cols, :], 1, 1)
        output_strips(dflat_v, send_d, cols)
        for copy in halo_d(n):
            copy.start()
        return 0

    scatter_sums(0)
    lax.fori_loop(0, 1, d_token_step, 0)
    scatter_sums(1)
    sum_start(sm_v, sm_send, sm_recv, 1, sum_finish(sm_v, sm_send, sm_recv, 0))
    lax.fori_loop(1, 3, d_token_step, 0)
    scatter_sums(2)
    fin_copy = remote(fin_v.at[0], fin_v.at[1], fin_sem.at[0], fin_sem.at[1], sibling)
    fin_copy.start()
    squares = fin_v[0] * fin_v[0]
    squares = squares[:8] + squares[8:16] + squares[16:]
    squares = sum(squares[:, 128 * n : 128 * n + 128] for n in range(6))
    squares_start(0, squares)
    sum_start(sm_v, sm_send, sm_recv, 2, sum_finish(sm_v, sm_send, sm_recv, 1))
    arrive(came_o, halo_send.at[2], halo_recv.at[2])
    each_column(lambda cols: output_block(flat_v, came_o, oblk_v, cols, low))
    store_out = pltpu.make_async_copy(oblk_v, out_h, store_sem.at[0])
    store_out.start()
    squares_start(1, squares_finish(0))
    sum_start(sm_v, sm_send, sm_recv, 3, sum_finish(sm_v, sm_send, sm_recv, 2))
    lax.fori_loop(0, 3, last_step, 0)

    small = sum_finish(sm_v, sm_send, sm_recv, 3)
    small_total = jnp.sum(small * small, axis=(0, 1), keepdims=True)
    drel = small[:24].T
    fin_copy.wait()
    own = jnp.where(core == 0, fin_v[0, :12], fin_v[0, 12:])
    other = jnp.where(core == 0, fin_v[1, :12], fin_v[1, 12:])
    first, second = jnp.where(core == 0, own, other), jnp.where(core == 0, other, own)
    squares = squares_finish(1)
    total = jnp.sum(squares, axis=(0, 1), keepdims=True) + small_total
    factor = jnp.minimum(1.0, jnp.sqrt(PARAMS / (total + clip_epsilon)))
    dpw_ref[:, :HALF] = first * factor
    dpw_ref[:, HALF:] = second * factor
    drel = drel * factor
    for a in range(15):
        drel_ref[a] = drel[16 * a : 16 * a + 15]
    for n in range(GROUPS):
        dgain_ref[LANES * n : LANES * n + LANES] = (small[24 + n : 25 + n] * factor).reshape(LANES)
        dshift_ref[LANES * n : LANES * n + LANES] = (small[32 + n : 33 + n] * factor).reshape(LANES)
    store_out.wait()
    pltpu.make_async_copy(dblk_v, dtok_h, store_sem.at[1]).wait()


def hand_over(*refs):
    source, target, held, load_sem, store_sem = refs[:6], refs[6:12], refs[12:18], refs[18], refs[19]
    loads = [pltpu.make_async_copy(source[i], held[i], load_sem.at[i]) for i in range(6)]
    stores = [pltpu.make_async_copy(held[i], target[i], store_sem.at[i]) for i in range(6)]
    for load in loads:
        load.start()
    for load, store in zip(loads, stores):
        load.wait()
        store.start()
    for store in stores:
        store.wait()


def on_device(tokens, qkv_weight, rel_bias, proj_weight, norm_gain, norm_shift, cotangent):
    anywhere = pl.BlockSpec(memory_space=pl.ANY)
    vmem = pl.BlockSpec(memory_space=pltpu.VMEM)
    dma = pltpu.SemaphoreType.DMA
    strips = [pltpu.VMEM((112, D), BF)] * 8
    scratch = [
        pltpu.VMEM((16, 16, D), BF),
        pltpu.VMEM((16, 16, D), BF),
        pltpu.VMEM((D, 3 * D), BF),
        pltpu.VMEM((D, D), BF),
        pltpu.VMEM((TOKENS, D), BF),
        pltpu.VMEM((TOKENS, D), BF),
        pltpu.VMEM((18, TOKENS, LANES), BF),
        pltpu.VMEM((GROUPS, WINDOWS, CELLS, LANES), F32),
        pltpu.VMEM((TOKENS, D), BF),
        pltpu.VMEM((2, D, TOKENS), BF),
        pltpu.VMEM((TOKENS, D), F32),
        pltpu.VMEM((TOKENS, D), F32),
        pltpu.VMEM((TOKENS, D), F32),
        pltpu.VMEM((TOKENS, D), BF),
        pltpu.VMEM((TOKENS, HALF), BF),
        pltpu.VMEM((GROUPS, TOKENS, LANES), BF),
        pltpu.VMEM((TOKENS, 3 * D), BF),
        pltpu.VMEM((16, 16, D), BF),
        pltpu.VMEM((16, 16, D), BF),
        pltpu.VMEM((15, 15, HEADS), F32),
        pltpu.VMEM((D,), F32),
        pltpu.VMEM((D,), F32),
        pltpu.VMEM((1024, LANES), BF),
        pltpu.VMEM((LANES, HEADS), F32),
        pltpu.VMEM((1, D), F32),
        pltpu.VMEM((1, D), F32),
        pltpu.VMEM((HEADS, 8, 128), F32),
        pltpu.VMEM((GROUPS, CELLS, LANES), F32),
        pltpu.VMEM((CELLS, LANES), F32),
        pltpu.VMEM((HEADS, 8, 128), F32),
        pltpu.VMEM((2, 8, D), F32),
        *strips,
        pltpu.VMEM((3, 2, 4, 4, 2, 48, 128), BF),
        pltpu.VMEM((2, 3, 2, 4, 2, 48, 128), BF),
        pltpu.VMEM((3, 4, 4, 48, 128), BF),
        pltpu.VMEM((2, 4, 2, 48, 128), BF),
        pltpu.VMEM((2, 4, 2, 48, 128), BF),
        pltpu.VMEM((4, 4, 48, 128), BF),
        pltpu.VMEM((3, 2, 2, 48, 128), BF),
        pltpu.VMEM((3, 4, 48, 128), BF),
        pltpu.VMEM((3, 4, 48, 128), BF),
        pltpu.VMEM((2, 2, 48, 128), BF),
        pltpu.VMEM((4, 48, 128), BF),
        pltpu.VMEM((4, 48, 128), BF),
        pltpu.VMEM((3, 3, 48, 128), BF),
        pltpu.VMEM((2, 24, HALF), F32),
        pltpu.VMEM((4, 4, 40, LANES), F32),
        pltpu.VMEM((2, 16, 8, 128), F32),
        dma((6,)),
        dma((GROUPS,)),
        dma((2,)),
        dma((6,)),
        dma((6,)),
        dma((2,)),
        dma((2,)),
        dma((3, 3)),
        dma((3, 3)),
        dma((4,)),
        dma((4,)),
        dma((2,)),
        dma((2,)),
        dma((2,)),
    ]
    results = pl.pallas_call(
        sublayer,
        out_shape=(
            jax.ShapeDtypeStruct((16, 16, D), BF),
            jax.ShapeDtypeStruct((16, 16, D), BF),
            jax.ShapeDtypeStruct((12, D), F32),
            jax.ShapeDtypeStruct((15, 15, HEADS), F32),
            jax.ShapeDtypeStruct((D,), F32),
            jax.ShapeDtypeStruct((D,), F32),
        ),
        in_specs=[anywhere] * 7,
        out_specs=(anywhere, anywhere, vmem, vmem, vmem, vmem),
        scratch_shapes=scratch,
        compiler_params=pltpu.CompilerParams(
            collective_id=0, has_side_effects=True, vmem_limit_bytes=60 * 2**20
        ),
        name="sublayer",
    )(
        tokens, qkv_weight, rel_bias.transpose(1, 2, 0), proj_weight, norm_gain, norm_shift, cotangent,
    )
    out, d_tokens, d_proj, d_rel, d_gain, d_shift = pl.pallas_call(
        hand_over,
        out_shape=tuple(jax.ShapeDtypeStruct(r.shape, r.dtype) for r in results),
        in_specs=[anywhere] * 6,
        out_specs=(anywhere,) * 6,
        scratch_shapes=[pltpu.VMEM(r.shape, r.dtype) for r in results] + [dma((6,)), dma((6,))],
        compiler_params=pltpu.CompilerParams(vmem_limit_bytes=60 * 2**20),
        name="hand_over",
    )(*results)
    return out, d_tokens, d_proj, d_rel.transpose(2, 0, 1), d_gain, d_shift


def solution(mesh):
    in_specs = (P("lat", "lon", None), P(), P(), P(), P(), P(), P("lat", "lon", None))
    out_specs = (
        P("lat", "lon", None),
        P("lat", "lon", None),
        P(("lon", "lat"), None),
        P(),
        P(),
        P(),
    )
    return jax.shard_map(
        on_device, mesh=mesh, in_specs=in_specs, out_specs=out_specs, check_vma=False
    )
```

```python
import functools

import jax
import jax.numpy as jnp
from jax import lax
from jax.experimental import pallas as pl
from jax.experimental.pallas import tpu as pltpu
from jax.sharding import PartitionSpec as P

F32 = jnp.float32
BF = jnp.bfloat16
MESH = pl.DeviceIdType.MESH

D = 1536
HEADS = 24
GROUPS = 6
LANES = 256
TOKENS = 256
CELLS = 64
WINDOWS = 4
HALF = 768
PARAMS = 2367768
norm_epsilon = 1e-05
clip_epsilon = 1e-06

ORDERS = (("x", "y", "z"), ("y", "z", "x"), ("z", "x", "y"))


def dot(a, b, ca, cb):
    return lax.dot_general(a, b, (((ca,), (cb,)), ((), ())), preferred_element_type=F32)


def dot_exact(a, b, ca, cb):
    total = None
    for _ in range(3):
        part = a.astype(BF)
        a = a - part.astype(F32)
        term = dot(part, b, ca, cb)
        total = term if total is None else total + term
    return total


def stack(*pieces):
    return jnp.concatenate(pieces, axis=0)


def turn(value):
    return pltpu.roll(value, 4, 0)


def low_rows(columns):
    return lax.broadcasted_iota(jnp.int32, (8, columns), 0) < 4


def halves(ref, rows, cols):
    both = ref[rows, cols].astype(F32)
    return both[:8], both[8:]


def row_halves(block, row, cols):
    both = block[row, :, cols].astype(F32)
    return both[:8], both[8:]


def columns_of(step, width=LANES):
    return pl.ds(pl.multiple_of(step * width, width), width)


def pack_first(a, b):
    return jnp.where(low_rows(a.shape[1]), a, turn(b))


def pack_last(a, b):
    return jnp.where(low_rows(a.shape[1]), turn(a), b)


def four_pairs(pack, values):
    return stack(pack(values[0], values[1]), pack(values[2], values[3])).astype(BF)


STRIPS = (slice(0, 32), slice(32, 48), slice(48, 96), slice(96, 112))
STRIP_STEPS = ((0, 1), (0, -1), (1, 0), (1, -1))


def input_strips(block, strips, cols, low):
    for k in range(2):
        rows = [row_halves(block, 4 + 4 * k + i, cols)[0] for i in range(4)]
        strips[16 * k : 16 * k + 16, cols] = four_pairs(pack_first, rows)
    rows = [row_halves(block, 12 + i, cols)[1] for i in range(4)]
    strips[32:48, cols] = four_pairs(pack_last, rows)
    t = [row_halves(block, r, cols) for r in range(4)]
    wide = [turn(jnp.where(low, t1, t0)) for t0, t1 in t]
    strips[48:64, cols] = stack(wide[0], wide[1]).astype(BF)
    strips[64:80, cols] = stack(wide[2], wide[3]).astype(BF)
    strips[80:96, cols] = four_pairs(pack_first, [t0 for t0, _ in t])
    strips[96:112, cols] = four_pairs(pack_last, [t1 for _, t1 in t])


def own_windows(block, flat, cols, low):
    for r, at in ((4, 0), (6, 16), (8, 32), (10, 48), (12, 192), (14, 208)):
        t0, t1 = row_halves(block, r, cols)
        u0, u1 = row_halves(block, r + 1, cols)
        flat[at : at + 16, cols] = stack(
            turn(jnp.where(low, t1, t0)), turn(jnp.where(low, u1, u0))
        ).astype(BF)


def input_windows(block, came, flat, cols, low):
    for k in range(2):
        pairs = halves(came, slice(16 * k, 16 * k + 16), cols)
        for i in range(2):
            r = 4 * k + 2 * i
            s = pairs[i]
            t1 = row_halves(block, r + 4, cols)[1]
            u1 = row_halves(block, r + 5, cols)[1]
            flat[64 + 8 * r : 80 + 8 * r, cols] = stack(
                jnp.where(low, turn(t1), turn(s)), jnp.where(low, turn(u1), s)
            ).astype(BF)
    west = halves(came, slice(32, 48), cols)
    side = halves(came, slice(80, 96), cols)
    corner = halves(came, slice(96, 112), cols)
    for i in range(2):
        t0 = row_halves(block, 12 + 2 * i, cols)[0]
        u0 = row_halves(block, 13 + 2 * i, cols)[0]
        s = west[i]
        flat[128 + 16 * i : 144 + 16 * i, cols] = stack(
            jnp.where(low, s, turn(t0)), jnp.where(low, turn(s), turn(u0))
        ).astype(BF)
        s, d = side[i], corner[i]
        flat[160 + 16 * i : 176 + 16 * i, cols] = stack(
            jnp.where(low, d, turn(s)), jnp.where(low, turn(d), s)
        ).astype(BF)
        flat[224 + 16 * i : 240 + 16 * i, cols] = came[48 + 16 * i : 64 + 16 * i, cols]


def output_strips(flat, strips, cols):
    def rows_of(start):
        return [flat[start + 8 * i : start + 8 * i + 8, cols] for i in range(4)]

    for k in range(2):
        strips[16 * k : 16 * k + 16, cols] = four_pairs(pack_last, rows_of(64 + 32 * k))
    strips[32:48, cols] = four_pairs(pack_first, rows_of(128))
    strips[48:80, cols] = flat[224:256, cols].astype(BF)
    strips[80:96, cols] = four_pairs(pack_last, rows_of(160))
    strips[96:112, cols] = four_pairs(pack_first, rows_of(160))


def output_block(flat, came, block, cols, low):
    for k in range(2):
        pairs = halves(came, slice(16 * k, 16 * k + 16), cols)
        for i in range(4):
            r = 4 * k + i
            s = pairs[i // 2]
            s = s if i % 2 == 0 else turn(s)
            a = turn(flat[8 * r : 8 * r + 8, cols])
            b = turn(flat[64 + 8 * r : 72 + 8 * r, cols])
            block[r + 4, :, cols] = stack(jnp.where(low, s, a), jnp.where(low, a, b)).astype(BF)
    east = halves(came, slice(32, 48), cols)
    side = halves(came, slice(80, 96), cols)
    corner = halves(came, slice(96, 112), cols)
    for i in range(2):
        wides = halves(came, slice(48 + 16 * i, 64 + 16 * i), cols)
        for k in range(2):
            r = 2 * i + k
            a = turn(flat[128 + 8 * r : 136 + 8 * r, cols])
            b = turn(flat[192 + 8 * r : 200 + 8 * r, cols])
            s = turn(east[i]) if k == 0 else east[i]
            block[12 + r, :, cols] = stack(jnp.where(low, a, b), jnp.where(low, b, s)).astype(BF)
            wide = turn(wides[k])
            at_low = side[i] if k == 0 else turn(side[i])
            at_high = turn(corner[i]) if k == 0 else corner[i]
            block[r, :, cols] = stack(
                jnp.where(low, at_low, wide), jnp.where(low, wide, at_high)
            ).astype(BF)


def block_diagonal(value, lane_head):
    zero = jnp.zeros_like(value)
    return stack(*[jnp.where(lane_head == h, value, zero) for h in range(4)])


def diagonal(product, left):
    tiles = []
    for t in range(2):
        cols = slice(128 * t, 128 * t + 128)
        tiles.append(
            jnp.where(
                left,
                product[128 * t : 128 * t + 64, cols],
                product[128 * t + 64 : 128 * t + 128, cols],
            )
        )
    return jnp.concatenate(tiles, axis=1)


def sublayer(
    tok_h, wq_h, rel_h, pw_h, gain_h, shift_h, cot_h,
    out_h, dtok_h, dpw_ref, drel_ref, dgain_ref, dshift_ref,
    tok_v, cot_v, w_v, pw_v, x_v, c_v, qkv_v, pt_v, mix_v, mixt_v, proj_v, flat_v, dflat_v,
    dp_v, dps_v, dmix_v, dqkv_v, oblk_v, dblk_v,
    rel_ref, gain_ref, shift_ref, e_v, rel_v, gain_v, shift_v, wb_v, bt_v, mask_v, u_v, acc_v,
    send_x, came_x, send_c, came_c, send_o, came_o, send_d, came_d,
    p_v, r1a, r1c, s2a, s2b, s2c, r2a, r2b, r2c, s3a, s3b, s3c, r3, fin_v,
    sm_v, sq_v,
    load_sem, w_sem, store_sem, halo_send, halo_recv, mix_sem, dp_sem,
    rs_send, rs_recv, sm_send, sm_recv, sq_send, sq_recv, fin_sem,
):
    lon = lax.axis_index("lon")
    lat = lax.axis_index("lat")
    core = lax.rem(lat, 2)
    at = {
        "x": lax.rem(lon // 4, 4),
        "y": lax.rem(lon, 4),
        "z": (lon // 16) * 2 + lat // 2,
    }

    def device(chip, on_core):
        z = chip["z"]
        return {
            "lon": (z // 2) * 16 + chip["x"] * 4 + chip["y"],
            "lat": lax.rem(z, 2) * 2 + on_core,
        }

    def along(axis, steps, on_core=core):
        chip = dict(at)
        chip[axis] = lax.rem(at[axis] + steps, 4)
        return device(chip, on_core)

    sibling = device(at, 1 - core)

    def shifted(lat_steps, lon_steps):
        return {
            "lon": lax.rem(lon + lon_steps + 32, 32),
            "lat": lax.rem(lat + lat_steps + 4, 4),
        }

    def remote(src, dst, send, recv, target):
        return pltpu.make_async_remote_copy(
            src_ref=src, dst_ref=dst, send_sem=send, recv_sem=recv,
            device_id=target, device_id_type=MESH,
        )

    def arrive(whole, send, recv):
        group = remote(whole, whole, send, recv, sibling)
        group.wait_send()
        group.wait_recv()

    load_tok = pltpu.make_async_copy(tok_h, tok_v, load_sem.at[0])
    load_cot = pltpu.make_async_copy(cot_h, cot_v, load_sem.at[1])
    load_pw = pltpu.make_async_copy(pw_h, pw_v, load_sem.at[2])

    def load_w(g, part):
        source = wq_h.at[:, columns_of(part * GROUPS + g)]
        return pltpu.make_async_copy(source, w_v.at[:, columns_of(3 * g + part)], w_sem.at[g])

    load_tok.start()
    load_cot.start()
    loads = [
        pltpu.make_async_copy(rel_h, rel_ref, load_sem.at[3]),
        pltpu.make_async_copy(gain_h, gain_ref, load_sem.at[4]),
        pltpu.make_async_copy(shift_h, shift_ref, load_sem.at[5]),
    ]
    for load in loads:
        load.start()

    partners = [shifted(0, 1), shifted(0, -1), shifted(1, 0), shifted(-1, 0), shifted(1, -1), shifted(-1, 1)]
    circles = [[], []]
    for k in range(1, 16):
        chip = dict(at)
        chip["x"] = lax.rem(at["x"] + k // 4, 4)
        chip["y"] = lax.rem(at["y"] + k % 4, 4)
        circles[0].append(device(chip, core))
    circles[1] += [sibling] + [along("z", steps) for steps in (1, 2, 3)]
    circles[1] += [along("z", steps, 1 - core) for steps in (1, 2, 3)]
    partners += circles[0] + circles[1]
    barrier = pltpu.get_barrier_semaphore()
    for partner in partners:
        pl.semaphore_signal(barrier, inc=1, device_id=partner, device_id_type=MESH)

    for g in range(GROUPS):
        for part in range(3):
            load_w(g, part).start()
    load_pw.start()

    low = low_rows(LANES)

    def each_column(body):
        lax.fori_loop(0, GROUPS, lambda n, _: (body(columns_of(n)), 0)[1], 0)

    def halo(strips, came, which, sign, cols=slice(None)):
        return [
            remote(
                strips.at[rows, cols], came.at[rows, cols],
                halo_send.at[which], halo_recv.at[which],
                shifted(sign * STRIP_STEPS[i][0], sign * STRIP_STEPS[i][1]),
            )
            for i, rows in enumerate(STRIPS)
        ]

    load_tok.wait()
    each_column(lambda cols: input_strips(tok_v, send_x, cols, low))
    pl.semaphore_wait(barrier, len(partners))
    halo_x = halo(send_x, came_x, 0, -1)
    for copy in halo_x:
        copy.start()
    each_column(lambda cols: own_windows(tok_v, x_v, cols, low))
    load_cot.wait()
    each_column(lambda cols: input_strips(cot_v, send_c, cols, low))
    halo_c = halo(send_c, came_c, 1, -1)

    spot = lax.broadcasted_iota(jnp.int32, (128, LANES), 0)
    slot = lax.broadcasted_iota(jnp.int32, (128, LANES), 1)
    for cj in range(8):
        hit = ((spot >> 3) == (slot >> 4)) & ((spot & 7) - cj + 7 == (slot & 15))
        e_v[128 * cj : 128 * cj + 128, :] = jnp.where(hit, 1.0, 0.0).astype(BF)
    for load in loads:
        load.wait()
    rel_v[...] = jnp.zeros_like(rel_v)
    for a in range(15):
        rel_v[16 * a : 16 * a + 15, :] = rel_ref[a]
    rel = rel_v[...]
    for cj in range(8):
        wb_v[:, cj, :] = dot_exact(rel, e_v[128 * cj : 128 * cj + 128, :], 0, 1)
    left8 = lax.broadcasted_iota(jnp.int32, (8, 128), 1) < 64

    def bias_step(g, _):
        for t in range(2):
            first = wb_v[g * 4 + 2 * t]
            second = wb_v[g * 4 + 2 * t + 1]
            for rj in range(8):
                shift = (7 - rj) * 8
                bt_v[g, 8 * rj : 8 * rj + 8, 128 * t : 128 * t + 128] = jnp.where(
                    left8,
                    pltpu.roll(first, (128 - shift) % 128, 1),
                    pltpu.roll(second, (192 - shift) % 128, 1),
                )
        return 0

    lax.fori_loop(0, GROUPS, bias_step, 0)
    j_upper = lax.broadcasted_iota(jnp.int32, (CELLS, LANES), 0) < 32
    i_upper = (lax.broadcasted_iota(jnp.int32, (CELLS, LANES), 1) & 63) < 32
    crossing = (j_upper != i_upper) & (lat == 3)
    mask_v[...] = jnp.where(crossing, -jnp.inf, 0.0)

    arrive(came_x, halo_send.at[0], halo_recv.at[0])
    for copy in halo_c:
        copy.start()
    each_column(lambda cols: input_windows(tok_v, came_x, x_v, cols, low))

    lane_head = lax.broadcasted_iota(jnp.int32, (CELLS, LANES), 1) >> 6
    left = lax.broadcasted_iota(jnp.int32, (CELLS, 128), 1) < 64

    def mix_copy(g):
        rows = columns_of(g)
        return remote(
            mixt_v.at[0, rows], mixt_v.at[1, rows], mix_sem.at[0], mix_sem.at[1], sibling
        )

    def make_qkv(g):
        whole = dot(x_v[...], w_v[:, columns_of(g, HALF)], 1, 0).astype(BF)
        for part in range(3):
            value = whole[:, LANES * part : LANES * part + LANES]
            if part == 0:
                value = value * jnp.asarray(0.125, BF)
            qkv_v[part * GROUPS + g] = value

    def wait_weights(g):
        three = w_v.at[:, : 3 * LANES]
        pltpu.make_async_copy(three, three, w_sem.at[g]).wait()

    def attend(g):
        bias = bt_v[g]
        masked = bias + mask_v[...]
        mixed = []
        for w in range(WINDOWS):
            rows = slice(CELLS * w, CELLS * w + CELLS)
            q, k, v = [qkv_v[part * GROUPS + g, rows, :] for part in range(3)]
            scores = dot(k, block_diagonal(q, lane_head), 1, 1) + (bias if w < 2 else masked)
            peak = jnp.max(scores, axis=0, keepdims=True)
            raised = jnp.exp(scores - peak)
            shares = raised * (1.0 / jnp.sum(raised, axis=0, keepdims=True))
            pt_v[g, w] = shares
            mixed.append(diagonal(dot(shares.astype(BF), v, 0, 0), left).astype(BF))
        mixed = stack(*mixed)
        mix_v[:, columns_of(g)] = mixed
        mixt_v[0, columns_of(g), :] = mixed.T

    def forward_step(g, _):
        wait_weights(g + 1)
        attend(g)
        make_qkv(g + 1)
        mix_copy(g).start()
        return 0

    wait_weights(0)
    make_qkv(0)
    lax.fori_loop(0, GROUPS - 1, forward_step, 0)
    attend(GROUPS - 1)
    mix_copy(GROUPS - 1).start()

    def project_step(n, _):
        cols = columns_of(n, HALF)
        proj_v[:, cols] = dot(mix_v[...], pw_v[:, cols], 1, 0)
        return 0

    load_pw.wait()
    lax.fori_loop(0, 2, project_step, 0)

    each_column(lambda cols: own_windows(cot_v, c_v, cols, low))
    arrive(came_c, halo_send.at[1], halo_recv.at[1])
    each_column(lambda cols: input_windows(cot_v, came_c, c_v, cols, low))

    acc_v[...] = jnp.zeros_like(acc_v)
    gain = gain_ref[...].reshape(1, D)
    shift = shift_ref[...].reshape(1, D)
    gain_v[...] = gain
    shift_v[...] = shift

    other_half = pl.ds(pl.multiple_of((1 - core) * HALF, HALF), HALF)

    def dp_copy(m):
        rows = pl.ds(pl.multiple_of(m * CELLS, CELLS), CELLS)
        return remote(dp_v.at[rows, other_half], dps_v.at[rows], dp_sem.at[0], dp_sem.at[1], sibling)

    def norm_step(m, _):
        sums = [None, None]
        for part in range(4):
            rows = pl.ds(pl.multiple_of(m * CELLS + 16 * part, 16), 16)
            projected = proj_v[rows, :]
            centre = projected - jnp.mean(projected, axis=1, keepdims=True)
            inverse = lax.rsqrt(jnp.mean(centre * centre, axis=1, keepdims=True) + norm_epsilon)
            normed = centre * inverse
            flat_v[rows, :] = x_v[rows, :].astype(F32) + normed * gain_v[...] + shift_v[...]
            upstream = c_v[rows, :].astype(F32)
            product = upstream * normed
            terms = (product[:8] + product[8:], upstream[:8] + upstream[8:])
            sums = [b if a is None else a + b for a, b in zip(sums, terms)]
            d_normed = upstream * gain_v[...]
            inner = d_normed - jnp.mean(d_normed, axis=1, keepdims=True)
            inner = inner - normed * jnp.mean(d_normed * normed, axis=1, keepdims=True)
            dp_v[rows, :] = (inverse * inner).astype(BF)
        acc_v[0] += sums[0]
        acc_v[1] += sums[1]
        dp_copy(m).start()
        return 0

    lax.fori_loop(0, TOKENS // CELLS, norm_step, 0)

    each_column(lambda cols: output_strips(flat_v, send_o, cols))
    for copy in halo(send_o, came_o, 2, 1):
        copy.start()

    arrive(dps_v, dp_sem.at[0], dp_sem.at[1])
    arrive(mixt_v.at[1], mix_sem.at[0], mix_sem.at[1])

    def slot_of(buffer, lead, axes, axis, index):
        if axis == "z":
            places = {"h": index // 2, "l": lax.rem(index, 2)}
        else:
            places = {axis: index}
        return buffer.at[lead + tuple(places.get(name, slice(None)) for name in axes)]

    stages = (
        ((p_v, (0,), "hxyl"), (p_v, (1,), "hxyl"), (p_v, (2,), "hxyl")),
        ((s2a, (), "hyl"), (s2b, (), "hxl"), (s2c, (), "xy")),
        ((s3a, (), "hl"), (s3b, (), "x"), (s3c, (), "y")),
    )
    arrivals = (
        (r1a.at[0], r1a.at[1], r1c),
        (r2a, r2b, r2c),
        (r3.at[0], r3.at[1], r3.at[2]),
    )

    def scatter_copies(stage, part):
        buffer, lead, axes = stages[stage][part]
        axis = ORDERS[part][stage]
        copies = []
        for steps in (1, 2, 3):
            index = lax.rem(at[axis] + steps, 4)
            copies.append(
                remote(
                    slot_of(buffer, lead, axes, axis, index),
                    arrivals[stage][part].at[steps - 1],
                    rs_send.at[stage, part],
                    rs_recv.at[stage, part],
                    along(axis, steps),
                )
            )
        return copies

    def scatter_start(stage, part):
        for copy in scatter_copies(stage, part):
            copy.start()

    def scatter_sum(stage, part):
        buffer, lead, axes = stages[stage][part]
        axis = ORDERS[part][stage]
        came = arrivals[stage][part]
        arrive(came, rs_send.at[stage, part], rs_recv.at[stage, part])
        total = slot_of(buffer, lead, axes, axis, at[axis])[...].astype(F32)
        for steps in range(3):
            total = total + came[steps].astype(F32)
        if stage < 2:
            target = stages[stage + 1][part][0]
            target[...] = total.astype(target.dtype)
            scatter_start(stage + 1, part)
        else:
            fin_v[0, :, LANES * part : LANES * part + 128] = total[:24]
            fin_v[0, :, LANES * part + 128 : LANES * part + 256] = total[24:]

    def scatter_sums(stage):
        for part in range(3):
            scatter_sum(stage, part)

    for part in range(3):
        own = dp_v[:, pl.ds(pl.multiple_of(core * HALF + part * LANES, LANES), LANES)]
        other = dps_v[:, LANES * part : LANES * part + LANES]
        for mb in range(4):
            rows = slice(384 * mb, 384 * mb + 384)
            value = dot(mixt_v[0, rows, :], own, 1, 0) + dot(mixt_v[1, rows, :], other, 1, 0)
            value = jnp.concatenate(
                [value[:, :128].reshape(16, 24, 128), value[:, 128:].reshape(16, 24, 128)], axis=1
            )
            p_v[part, mb // 2, 2 * (mb % 2) : 2 * (mb % 2) + 2] = value.astype(BF).reshape(
                2, 4, 2, 48, 128
            )
        scatter_start(0, part)

    def make_d_mixed(g):
        dmix_v[g] = dot(dp_v[...], pw_v[columns_of(g), :], 1, 1).astype(BF)

    def backward(g):
        total = None
        for w in range(WINDOWS):
            rows = slice(CELLS * w, CELLS * w + CELLS)
            q, k, v = [qkv_v[part * GROUPS + g, rows, :] for part in range(3)]
            d_out = block_diagonal(dmix_v[g, rows, :], lane_head)
            shares = pt_v[g, w]
            d_shares = dot(v, d_out, 1, 1)
            d_scores = shares * (d_shares - jnp.sum(shares * d_shares, axis=0, keepdims=True))
            total = d_scores if total is None else total + d_scores
            low_scores = d_scores.astype(BF)
            dq = diagonal(dot(low_scores, k, 0, 0), left) * 0.125
            dk = dot(low_scores, block_diagonal(q, lane_head), 1, 0)
            dv = dot(shares.astype(BF), d_out, 1, 0)
            for part, value in enumerate((dq, dk, dv)):
                dqkv_v[rows, columns_of(3 * g + part)] = value.astype(BF)
        for t in range(2):
            sums = [None, None]
            for rj in range(8):
                shift = (7 - rj) * 8
                piece = total[8 * rj : 8 * rj + 8, 128 * t : 128 * t + 128]
                pair = (
                    pltpu.roll(jnp.where(left8, piece, 0.0), shift, 1),
                    pltpu.roll(jnp.where(left8, 0.0, piece), shift + 64, 1),
                )
                sums = [b if a is None else a + b for a, b in zip(sums, pair)]
            u_v[g * 4 + 2 * t] = sums[0]
            u_v[g * 4 + 2 * t + 1] = sums[1]

    def backward_step(g, _):
        backward(g)
        make_d_mixed(g + 1)
        return 0

    make_d_mixed(0)
    lax.fori_loop(0, GROUPS - 1, backward_step, 0)
    backward(GROUPS - 1)

    small = None
    for cj in range(8):
        term = dot_exact(u_v[:, cj, :], e_v[128 * cj : 128 * cj + 128, :], 1, 0)
        small = term if small is None else small + term
    gain_sum = jnp.sum(acc_v[0], axis=0, keepdims=True)
    shift_sum = jnp.sum(acc_v[1], axis=0, keepdims=True)
    zero2 = jnp.zeros((2, LANES), F32)
    small = stack(
        small,
        *[gain_sum[:, LANES * n : LANES * n + LANES] for n in range(GROUPS)], zero2,
        *[shift_sum[:, LANES * n : LANES * n + LANES] for n in range(GROUPS)], zero2,
    )

    def sum_copies(buffer, send, recv, stage):
        if stage == 0:
            return [remote(
                buffer.at[0, core], buffer.at[0, core], send.at[0], recv.at[0], sibling
            )]
        axis = "zxy"[stage - 1]
        return [
            remote(
                buffer.at[stage, at[axis]], buffer.at[stage, at[axis]],
                send.at[stage], recv.at[stage], along(axis, steps),
            )
            for steps in (1, 2, 3)
        ]

    def sum_start(buffer, send, recv, stage, value):
        place = core if stage == 0 else at["zxy"[stage - 1]]
        buffer[stage, place] = value
        for copy in sum_copies(buffer, send, recv, stage):
            copy.start()

    def sum_finish(buffer, send, recv, stage):
        arrive(buffer.at[stage, slice(0, 1 if stage == 0 else 3)], send.at[stage], recv.at[stage])
        total = buffer[stage, 0] + buffer[stage, 1]
        if stage > 0:
            total = total + buffer[stage, 2] + buffer[stage, 3]
        return total

    sum_start(sm_v, sm_send, sm_recv, 0, small)

    def squares_place(stage):
        return (at["x"] * 4 + at["y"], at["z"] * 2 + core)[stage]

    def squares_copies(stage):
        mine = sq_v.at[stage, squares_place(stage)]
        return [
            remote(mine, mine, sq_send.at[stage], sq_recv.at[stage], target)
            for target in circles[stage]
        ]

    def squares_start(stage, value):
        sq_v[stage, squares_place(stage)] = value
        for copy in squares_copies(stage):
            copy.start()

    def squares_finish(stage):
        count = (16, 8)[stage]
        arrive(sq_v.at[stage, slice(0, count - 1)], sq_send.at[stage], sq_recv.at[stage])
        total = sq_v[stage, 0]
        for k in range(1, count):
            total = total + sq_v[stage, k]
        return total

    def halo_d(n):
        return halo(send_d, came_d, 3 + n, 1, columns_of(n, 512))

    def store_d(n):
        cols = columns_of(n, 512)
        return pltpu.make_async_copy(dblk_v.at[:, :, cols], dtok_h.at[:, :, cols], store_sem.at[1])

    def last_step(n, _):
        arrive(came_d.at[:, columns_of(n, 512)], halo_send.at[3 + n], halo_recv.at[3 + n])
        output_block(dflat_v, came_d, dblk_v, columns_of(n, 512), low_rows(512))
        store_d(n).start()
        return 0

    def d_token_step(n, _):
        cols = columns_of(n, 512)
        dflat_v[:, cols] = c_v[:, cols].astype(F32) + dot(dqkv_v[...], w_v[cols, :], 1, 1)
        output_strips(dflat_v, send_d, cols)
        for copy in halo_d(n):
            copy.start()
        return 0

    scatter_sums(0)
    lax.fori_loop(0, 1, d_token_step, 0)
    scatter_sums(1)
    sum_start(sm_v, sm_send, sm_recv, 1, sum_finish(sm_v, sm_send, sm_recv, 0))
    lax.fori_loop(1, 3, d_token_step, 0)
    scatter_sums(2)
    fin_copy = remote(fin_v.at[0], fin_v.at[1], fin_sem.at[0], fin_sem.at[1], sibling)
    fin_copy.start()
    squares = fin_v[0] * fin_v[0]
    squares = squares[:8] + squares[8:16] + squares[16:]
    squares = sum(squares[:, 128 * n : 128 * n + 128] for n in range(6))
    squares = jnp.sum(squares, axis=0, keepdims=True)
    squares_start(0, squares)
    sum_start(sm_v, sm_send, sm_recv, 2, sum_finish(sm_v, sm_send, sm_recv, 1))
    arrive(came_o, halo_send.at[2], halo_recv.at[2])
    each_column(lambda cols: output_block(flat_v, came_o, oblk_v, cols, low))
    store_out = pltpu.make_async_copy(oblk_v, out_h, store_sem.at[0])
    store_out.start()
    squares_start(1, squares_finish(0))
    sum_start(sm_v, sm_send, sm_recv, 3, sum_finish(sm_v, sm_send, sm_recv, 2))
    lax.fori_loop(0, 3, last_step, 0)

    small = sum_finish(sm_v, sm_send, sm_recv, 3)
    small_total = jnp.sum(small * small, axis=(0, 1), keepdims=True)
    drel = small[:24].T
    fin_copy.wait()
    own = jnp.where(core == 0, fin_v[0, :12], fin_v[0, 12:])
    other = jnp.where(core == 0, fin_v[1, :12], fin_v[1, 12:])
    first, second = jnp.where(core == 0, own, other), jnp.where(core == 0, other, own)
    squares = squares_finish(1)
    total = jnp.sum(squares, axis=(0, 1), keepdims=True) + small_total
    factor = jnp.minimum(1.0, jnp.sqrt(PARAMS / (total + clip_epsilon)))
    dpw_ref[:, :HALF] = first * factor
    dpw_ref[:, HALF:] = second * factor
    drel = drel * factor
    for a in range(15):
        drel_ref[a] = drel[16 * a : 16 * a + 15]
    for n in range(GROUPS):
        dgain_ref[LANES * n : LANES * n + LANES] = (small[24 + n : 25 + n] * factor).reshape(LANES)
        dshift_ref[LANES * n : LANES * n + LANES] = (small[32 + n : 33 + n] * factor).reshape(LANES)
    store_out.wait()
    pltpu.make_async_copy(dblk_v, dtok_h, store_sem.at[1]).wait()


def hand_over(*refs):
    source, target, held, load_sem, store_sem = refs[:6], refs[6:12], refs[12:18], refs[18], refs[19]
    loads = [pltpu.make_async_copy(source[i], held[i], load_sem.at[i]) for i in range(6)]
    stores = [pltpu.make_async_copy(held[i], target[i], store_sem.at[i]) for i in range(6)]
    for load in loads:
        load.start()
    for load, store in zip(loads, stores):
        load.wait()
        store.start()
    for store in stores:
        store.wait()


def on_device(tokens, qkv_weight, rel_bias, proj_weight, norm_gain, norm_shift, cotangent):
    anywhere = pl.BlockSpec(memory_space=pl.ANY)
    vmem = pl.BlockSpec(memory_space=pltpu.VMEM)
    dma = pltpu.SemaphoreType.DMA
    strips = [pltpu.VMEM((112, D), BF)] * 8
    scratch = [
        pltpu.VMEM((16, 16, D), BF),
        pltpu.VMEM((16, 16, D), BF),
        pltpu.VMEM((D, 3 * D), BF),
        pltpu.VMEM((D, D), BF),
        pltpu.VMEM((TOKENS, D), BF),
        pltpu.VMEM((TOKENS, D), BF),
        pltpu.VMEM((18, TOKENS, LANES), BF),
        pltpu.VMEM((GROUPS, WINDOWS, CELLS, LANES), F32),
        pltpu.VMEM((TOKENS, D), BF),
        pltpu.VMEM((2, D, TOKENS), BF),
        pltpu.VMEM((TOKENS, D), F32),
        pltpu.VMEM((TOKENS, D), F32),
        pltpu.VMEM((TOKENS, D), F32),
        pltpu.VMEM((TOKENS, D), BF),
        pltpu.VMEM((TOKENS, HALF), BF),
        pltpu.VMEM((GROUPS, TOKENS, LANES), BF),
        pltpu.VMEM((TOKENS, 3 * D), BF),
        pltpu.VMEM((16, 16, D), BF),
        pltpu.VMEM((16, 16, D), BF),
        pltpu.VMEM((15, 15, HEADS), F32),
        pltpu.VMEM((D,), F32),
        pltpu.VMEM((D,), F32),
        pltpu.VMEM((1024, LANES), BF),
        pltpu.VMEM((LANES, HEADS), F32),
        pltpu.VMEM((1, D), F32),
        pltpu.VMEM((1, D), F32),
        pltpu.VMEM((HEADS, 8, 128), F32),
        pltpu.VMEM((GROUPS, CELLS, LANES), F32),
        pltpu.VMEM((CELLS, LANES), F32),
        pltpu.VMEM((HEADS, 8, 128), F32),
        pltpu.VMEM((2, 8, D), F32),
        *strips,
        pltpu.VMEM((3, 2, 4, 4, 2, 48, 128), BF),
        pltpu.VMEM((2, 3, 2, 4, 2, 48, 128), BF),
        pltpu.VMEM((3, 4, 4, 48, 128), BF),
        pltpu.VMEM((2, 4, 2, 48, 128), BF),
        pltpu.VMEM((2, 4, 2, 48, 128), BF),
        pltpu.VMEM((4, 4, 48, 128), BF),
        pltpu.VMEM((3, 2, 2, 48, 128), BF),
        pltpu.VMEM((3, 4, 48, 128), BF),
        pltpu.VMEM((3, 4, 48, 128), BF),
        pltpu.VMEM((2, 2, 48, 128), BF),
        pltpu.VMEM((4, 48, 128), BF),
        pltpu.VMEM((4, 48, 128), BF),
        pltpu.VMEM((3, 3, 48, 128), BF),
        pltpu.VMEM((2, 24, HALF), F32),
        pltpu.VMEM((4, 4, 40, LANES), F32),
        pltpu.VMEM((2, 16, 1, 128), F32),
        dma((6,)),
        dma((GROUPS,)),
        dma((2,)),
        dma((6,)),
        dma((6,)),
        dma((2,)),
        dma((2,)),
        dma((3, 3)),
        dma((3, 3)),
        dma((4,)),
        dma((4,)),
        dma((2,)),
        dma((2,)),
        dma((2,)),
    ]
    results = pl.pallas_call(
        sublayer,
        out_shape=(
            jax.ShapeDtypeStruct((16, 16, D), BF),
            jax.ShapeDtypeStruct((16, 16, D), BF),
            jax.ShapeDtypeStruct((12, D), F32),
            jax.ShapeDtypeStruct((15, 15, HEADS), F32),
            jax.ShapeDtypeStruct((D,), F32),
            jax.ShapeDtypeStruct((D,), F32),
        ),
        in_specs=[anywhere] * 7,
        out_specs=(anywhere, anywhere, vmem, vmem, vmem, vmem),
        scratch_shapes=scratch,
        compiler_params=pltpu.CompilerParams(
            collective_id=0, has_side_effects=True, vmem_limit_bytes=60 * 2**20
        ),
        name="sublayer",
    )(
        tokens, qkv_weight, rel_bias.transpose(1, 2, 0), proj_weight, norm_gain, norm_shift, cotangent,
    )
    out, d_tokens, d_proj, d_rel, d_gain, d_shift = pl.pallas_call(
        hand_over,
        out_shape=tuple(jax.ShapeDtypeStruct(r.shape, r.dtype) for r in results),
        in_specs=[anywhere] * 6,
        out_specs=(anywhere,) * 6,
        scratch_shapes=[pltpu.VMEM(r.shape, r.dtype) for r in results] + [dma((6,)), dma((6,))],
        compiler_params=pltpu.CompilerParams(vmem_limit_bytes=60 * 2**20),
        name="hand_over",
    )(*results)
    return out, d_tokens, d_proj, d_rel.transpose(2, 0, 1), d_gain, d_shift


def solution(mesh):
    in_specs = (P("lat", "lon", None), P(), P(), P(), P(), P(), P("lat", "lon", None))
    out_specs = (
        P("lat", "lon", None),
        P("lat", "lon", None),
        P(("lon", "lat"), None),
        P(),
        P(),
        P(),
    )
    return jax.shard_map(
        on_device, mesh=mesh, in_specs=in_specs, out_specs=out_specs, check_vma=False
    )
```
